128 devices in a mesh: ctx: 16 (over y_hi, z, core), wsh: 8 (over y_lo, x).
Axes of the slice: x: 4, y: 4 (y_hi: 2, y_lo: 2; y = y_hi * 2 + y_lo), z: 4, core: 2. Of those that a mesh axis runs over, the one named last changes fastest.
Arguments:
- tokens: bfloat16 [8, 2048, 768], P('wsh', 'ctx'), may hold values from -6 to 6
- gain_attn: float32 [768], replicated, may hold values from 0.1 to 1.9
- w_qkv: bfloat16 [768, 2304], replicated, may hold values from -0.21875 to 0.21875
- rel_bias: float32 [32, 12], replicated, may hold values from -4 to 4
- w_attn_out: bfloat16 [768, 768], replicated, may hold values from -2.5 to 2.5
- gain_ffn: float32 [768], replicated, may hold values from 0.1 to 1.9
- w_router: bfloat16 [768, 32], replicated, may hold values from -0.15625 to 0.15625
- w_in: bfloat16 [32, 768, 3072], P('ctx', None, 'wsh'), may hold values from -0.21875 to 0.21875
- w_out: bfloat16 [32, 3072, 768], P('ctx', 'wsh'), may hold values from -0.109375 to 0.109375
- routes: int32 [8, 2048, 2], P('wsh', 'ctx'), may hold values from 0 to 31, all different within a row; in each aligned block of 128 rows (0 to 127, 128 to 255, ..., all dimensions but the last counted through in order) at most 16 rows name the same one
- pair_order: int32 [16], replicated, may hold values from 0 to 15, each once
- bucket_table: int32 [2048], replicated, may hold values from 0 to 31, as said below
- cotangent: bfloat16 [8, 2048, 768], P('wsh', 'ctx'), may hold values from -6 to 6
Outputs:
- layer_out: bfloat16 [8, 2048, 768], P('wsh', 'ctx')
- grad_tokens: float32 [8, 2048, 768], P('wsh', 'ctx')
- grad_gain_attn: float32 [768], replicated
- grad_w_qkv: float32 [768, 2304], replicated
- grad_rel_bias: float32 [32, 12], replicated
- grad_w_attn_out: float32 [768, 768], replicated
- grad_gain_ffn: float32 [768], replicated
- grad_w_router: float32 [768, 32], replicated
- grad_w_in: float32 [32, 768, 3072], P('ctx', None, 'wsh')
- grad_w_out: float32 [32, 3072, 768], P('ctx', 'wsh')
The draws below stay inside these ranges and needn't reach their ends.
Inputs may be any that keep to these rules, and one draw needn't show every extreme that they name: `routes`: each row names two different experts; among the rows of one device no expert is named more than 16 times, a bound that some block reaches. `pair_order`: each index appears once. `bucket_table`: never falls as the distance grows; equals the distance below 16 and is 31 at the largest distance.
All inputs are finite; a program needn't handle non-finite values.
Results may differ from the reference program's by a relative error of at most 0.017.
Values may be sent and summed in bfloat16 or wider, within the bound.
No kernel may reach another device: no remote copies, remote signals or barrier semaphores. Data moves between devices by JAX's collectives and lax.ppermute only.
A program may use at most 192 MiB of HBM per device.

```python
import math
import jax
import jax.numpy as jnp
import numpy as np
from jax import lax

D = 768
HEADS = 12
FF = 3072
HEAD_DIM = 64
BUCKETS = 32
TOK_DEV = 128
EXPERTS = 32
CAP = 16
SEQ_LEN = 2048
SEQS = 8
N_CTX = 16


def draw_bucket_table(key, part):
    key = jax.random.fold_in(key, 7)
    half_count = BUCKETS // 2
    exact_cuts = jnp.arange(1, half_count, dtype=jnp.int32)
    spread_cuts = jax.random.permutation(key, SEQ_LEN - half_count)[:half_count].astype(jnp.int32) + half_count
    all_cuts = jnp.concatenate([exact_cuts, spread_cuts])
    distance = jnp.arange(SEQ_LEN, dtype=jnp.int32)
    return jnp.sum((distance[:, None] >= all_cuts[None, :]).astype(jnp.int32), axis=1, dtype=jnp.int32)


def block_scale(key, extent, split, low, largest):
    level, own = 1.0, jax.random.fold_in(key, 6)
    for axis_at, parts in split:
        steps = jnp.exp(jax.random.uniform(jax.random.fold_in(own, axis_at), (parts,), jnp.float32, low / len(split), largest / len(split)))
        level = level * jnp.repeat(steps, extent[axis_at] // parts).reshape([-1 if axis == axis_at else 1 for axis in range(len(extent))])
    return level


def routed_block(own_key, own, number, rows, count, top, most, skew):
    sequence = jax.random.permutation(own_key, count)
    crowded, ordinary = shares(count, rows * top, most, skew, True), shares(count, rows * top, most, skew, False)
    places = jnp.arange(count)

    def named(sizes, rotation):
        used = int((sizes > 0).sum())
        fixed = max(1, used // 4)
        passed = fixed + (places - fixed + rotation * (used - fixed)) % max(1, count - fixed)
        return jnp.zeros((count,), jnp.int32).at[sequence[jnp.where(places < fixed, places, passed)]].set(jnp.asarray(sizes, jnp.int32))

    sizes = jnp.where(number % 4 == 0, named(crowded, number // 4), named(ordinary, number - number // 4 - 1))
    mixed = jax.random.permutation(jax.random.fold_in(own, 3), count)
    source_of, sink = mixed[0:count // 2 * 2:2], mixed[1:count // 2 * 2:2]
    margin = jnp.minimum(sizes[source_of] - 1, most - sizes[sink]) // 2
    margin = jnp.where((source_of == sequence[0]) | (sink == sequence[0]) | (sizes[sink] == 0), 0, jnp.maximum(margin, 0))
    passed = jax.random.randint(jax.random.fold_in(own, 4), (count // 2,), 0, 1 << 20) % (margin + 1)
    sizes = sizes.at[source_of].add(-passed).at[sink].add(passed)
    items = jnp.searchsorted(jnp.cumsum(sizes), jnp.arange(rows * top), side="right").astype(jnp.int32)
    listing = items.reshape(top, rows).T
    listing = listing[jax.random.permutation(jax.random.fold_in(own, 1), rows)]
    rotation = jax.random.randint(jax.random.fold_in(own, 2), (rows, 1), 0, top)
    return jnp.take_along_axis(listing, (jnp.arange(top)[None, :] + rotation) % top, axis=1)


def shares(amount, total, bound, skew, full):
    loads = [(1 << 20) // math.isqrt(standing ** skew) + 1 for standing in range(1, amount + 1)]
    largest = bound if full else min(bound, max(-(-total // amount), total * loads[0] // sum(loads)))
    least = 1 if total - largest >= amount - 1 else 0
    counts, spare = [largest] + [least] * (amount - 1), total - largest - least * (amount - 1)
    while spare > 0:
        candidates = [i for i in range(1, amount) if counts[i] < largest] or [i for i in range(1, amount) if counts[i] < bound]
        whole, left = sum([loads[i] for i in candidates]), spare
        for i in candidates:
            addition = min(bound - counts[i], max(1, left * loads[i] // whole), spare)
            counts[i] = counts[i] + addition
            spare = spare - addition
    return np.array(counts)


def centred(own_key, dims, scale, limit, shards=(), kind=jnp.bfloat16):
    drawn = scale * jax.random.normal(own_key, dims, jnp.float32)
    if shards:
        drawn = drawn * block_scale(own_key, dims, shards, -0.22, 0.18)
    return jnp.clip(drawn, -limit, limit).astype(kind)


def setup_inputs(seed: int = 0) -> dict:
    key_list = jax.random.split(jax.random.key(seed), 14)
    tokens = centred(key_list[0], (SEQS, SEQ_LEN, D), 1.0, 6.0, ((0, 8), (1, 16)))
    gain_attn = jnp.clip(1.0 + 0.18 * jax.random.normal(key_list[1], (D,), jnp.float32), 0.1, 1.9)
    w_qkv = centred(key_list[2], (D, 3 * D), D ** -0.5, 0.21875)
    rel_bias = centred(key_list[3], (BUCKETS, HEADS), 1.0, 4.0, (), jnp.float32)
    w_attn_out = centred(key_list[4], (D, D), (max(D // 128, 1)) ** -0.5, 2.5)
    gain_ffn = jnp.clip(1.0 + 0.18 * jax.random.normal(key_list[5], (D,), jnp.float32), 0.1, 1.9)
    w_router = centred(key_list[6], (D, EXPERTS), (2 * D) ** -0.5, 0.15625)
    w_in = centred(key_list[7], (EXPERTS, D, FF), D ** -0.5, 0.21875, ((0, 16), (2, 8)))
    w_out = centred(key_list[8], (EXPERTS, FF, D), FF ** -0.5, 0.109375, ((0, 16), (1, 8)))
    routes_keys = jax.random.split(jax.random.fold_in(key_list[9], 1), SEQS * SEQ_LEN // TOK_DEV)
    routes_turns = jax.random.permutation(jax.random.fold_in(key_list[9], 3), SEQS * SEQ_LEN // TOK_DEV)
    routes = jax.vmap(lambda own, number: routed_block(jax.random.fold_in(key_list[9], 2), own, number, TOK_DEV, EXPERTS, 2, CAP, 1))(routes_keys, routes_turns).reshape((SEQS, SEQ_LEN, 2))
    pair_order = jax.random.permutation(key_list[10], N_CTX).astype(jnp.int32)
    bucket_table = draw_bucket_table(jax.random.fold_in(key_list[13], 71), 0)
    cotangent = centred(key_list[12], (SEQS, SEQ_LEN, D), 1.0, 6.0, ((0, 8), (1, 16)))
    return {"tokens": tokens, "gain_attn": gain_attn, "w_qkv": w_qkv, "rel_bias": rel_bias, "w_attn_out": w_attn_out, "gain_ffn": gain_ffn, "w_router": w_router, "w_in": w_in, "w_out": w_out, "routes": routes, "pair_order": pair_order, "bucket_table": bucket_table, "cotangent": cotangent}


@jax.custom_vjp
def low(v):
    return lax.optimization_barrier(v.astype(jnp.bfloat16)).astype(jnp.float32)

@jax.custom_vjp
def low_back(v):
    return v

def low_keep(v):
    return (low(v), None)

def low_pass(kept, grad):
    return (grad,)

def back_keep(v):
    return (v, None)

def back_low(kept, grad):
    return (low(grad),)
low.defvjp(low_keep, low_pass)
low_back.defvjp(back_keep, back_low)
EPSILON = 1e-06
HIGHEST = lax.Precision.HIGHEST
MASKED = -1e+30

def matmul_exact(left_matrix, right_matrix):
    return jnp.dot(left_matrix, right_matrix, precision=HIGHEST)

def rms_normed(values, gain_vector):
    inverse = lax.rsqrt(lax.optimization_barrier(jnp.mean(values * values, axis=-1, keepdims=True)) + EPSILON)
    return values * inverse * gain_vector

def softmax_rows(scores):
    row_maximum = lax.optimization_barrier(jnp.max(scores, axis=-1, keepdims=True))
    shifted = jnp.exp(scores - row_maximum)
    return shifted / lax.optimization_barrier(jnp.sum(shifted, axis=-1, keepdims=True))

def row_positions(pair_order):
    rows_all = jnp.arange(SEQ_LEN, dtype=jnp.int32)
    holder = rows_all // TOK_DEV
    within = rows_all % TOK_DEV
    half_rows = TOK_DEV // 2
    pair_index = pair_order[holder].astype(jnp.int32)
    later_place = (2 * N_CTX - 1 - pair_index) * half_rows + within - half_rows
    return jnp.where(within < half_rows, pair_index * half_rows + within, later_place).astype(jnp.int32)

def attention_block(query_block, query_pos, key_heads, value_heads, key_pos, bucket_table, rel_bias):
    raw_scores = jnp.einsum('qhd,khd->hqk', query_block, key_heads, precision=HIGHEST) * HEAD_DIM ** (-0.5)
    distance = (query_pos[:, None] - key_pos[None, :]).astype(jnp.int32)
    bucket_index = jnp.take(bucket_table, jnp.maximum(distance, 0), axis=0)
    score_bias = jnp.take(rel_bias.T, bucket_index, axis=1)
    scores = low_back(jnp.where(distance[None] >= 0, raw_scores + score_bias, MASKED))
    probabilities = low(softmax_rows(scores))
    return jnp.einsum('hqk,khd->qhd', probabilities, value_heads, precision=HIGHEST)

def attend_sequence(operands, positions, bucket_table, rel_bias):
    query_heads, key_heads, value_heads = operands
    block_rows = math.gcd(512, SEQ_LEN)
    block_count = SEQ_LEN // block_rows
    blocked = (query_heads.reshape(block_count, block_rows, HEADS, HEAD_DIM), positions.reshape(block_count, block_rows))

    def block_step(pieces):
        return attention_block(pieces[0], pieces[1], key_heads, value_heads, positions, bucket_table, rel_bias)
    return lax.map(jax.checkpoint(block_step), blocked).reshape(SEQ_LEN, HEADS * HEAD_DIM)

def expert_apply(operands):
    rows_in, weight_in, weight_out = operands
    pre_act = low_back(matmul_exact(rows_in, weight_in))
    activated = low(jax.nn.gelu(pre_act, approximate=False))
    return low_back(low(matmul_exact(activated, weight_out)))

def forward(tokens, gain_attn, w_qkv, rel_bias, w_attn_out, gain_ffn, w_router, w_in, w_out, routes, pair_order, bucket_table):
    positions = row_positions(pair_order)
    inputs = tokens.reshape(SEQS * SEQ_LEN, D)
    normed_one = low(rms_normed(inputs, gain_attn))
    projected = low_back(low(matmul_exact(normed_one, w_qkv)))
    split_heads = projected.reshape(SEQS, SEQ_LEN, 3, HEADS, HEAD_DIM)

    def attend(operands):
        return attend_sequence(operands, positions, bucket_table, rel_bias)
    attended = lax.map(attend, (split_heads[:, :, 0], split_heads[:, :, 1], split_heads[:, :, 2]))
    attended = low_back(low(attended.reshape(SEQS * SEQ_LEN, D)))
    residual_one = inputs + low_back(matmul_exact(attended, w_attn_out))
    normed_two = low(rms_normed(residual_one, gain_ffn))
    router_logits = matmul_exact(normed_two, w_router)
    chosen = routes.reshape(SEQS * SEQ_LEN, 2)
    gate_weights = softmax_rows(jnp.take_along_axis(router_logits, chosen, axis=1))
    block_total = SEQS * N_CTX
    expert_flat = routes.reshape(block_total, 2 * TOK_DEV)
    member = (expert_flat[:, :, None] == jnp.arange(EXPERTS, dtype=jnp.int32)[None, None, :]).astype(jnp.int32)
    running = jnp.cumsum(member, axis=1, dtype=jnp.int32) - 1
    slot_rank = lax.optimization_barrier(jnp.sum(member * running, axis=2, dtype=jnp.int32))
    slot_index = (jnp.arange(block_total, dtype=jnp.int32)[:, None] * CAP + slot_rank).reshape(-1).astype(jnp.int32)
    expert_index = expert_flat.reshape(-1).astype(jnp.int32)
    expert_rows = jnp.zeros((EXPERTS, block_total * CAP, D), jnp.float32)
    expert_rows = low_back(expert_rows.at[expert_index, slot_index].set(jnp.repeat(normed_two, 2, axis=0)))
    returned = lax.map(jax.checkpoint(expert_apply), (expert_rows, w_in, w_out))
    picked = returned[expert_index, slot_index].reshape(SEQS * SEQ_LEN, 2, D)
    mixture = lax.optimization_barrier(jnp.sum(gate_weights[:, :, None] * picked, axis=1))
    return (residual_one + mixture).reshape(SEQS, SEQ_LEN, D)

def reference(tokens, gain_attn, w_qkv, rel_bias, w_attn_out, gain_ffn, w_router, w_in, w_out, routes, pair_order, bucket_table, cotangent):
    params = tuple((operand.astype(jnp.float32) for operand in (tokens, gain_attn, w_qkv, rel_bias, w_attn_out, gain_ffn, w_router, w_in, w_out)))

    def whole_layer(weights_all):
        return forward(weights_all[0], weights_all[1], weights_all[2], weights_all[3], weights_all[4], weights_all[5], weights_all[6], weights_all[7], weights_all[8], routes, pair_order, bucket_table)
    layer_value, pullback = jax.vjp(whole_layer, params)
    gradients = pullback(cotangent.astype(jnp.float32))[0]
    return (layer_value.astype(jnp.bfloat16), gradients[0], gradients[1], gradients[2], gradients[3], gradients[4], gradients[5], gradients[6], gradients[7], gradients[8])
```

```python
import functools

import jax
import jax.numpy as jnp
from jax import lax
from jax.experimental import pallas as pl
from jax.experimental.pallas import tpu as pltpu
from jax.sharding import Mesh
from jax.sharding import PartitionSpec as P

BF = jnp.bfloat16
F32 = jnp.float32
EPSILON = 1e-06
HIGHEST = lax.Precision.HIGHEST
MASKED = -1e30
ROWS = (((0,), (0,)), ((), ()))
COLS = (((1,), (1,)), ((), ()))
LANES = 128
VMEM_LIMIT = 44 * 1024 * 1024
SPLIT = (2, 4, 2, 2, 4)
EVERY = ("ya", "z", "core", "yb", "x")
CTX = ("ya", "z", "core")
WSH = ("yb", "x")
SAME_CORE = ("ya", "z")
CHIPS = ("ya", "z", "yb", "x")
EXPERT_AXES = ("ya", "z", "core", "yb")
SWAP = ((0, 1), (1, 0))


def norm_scale(values):
    return lax.rsqrt(jnp.mean(values * values, axis=-1, keepdims=True) + EPSILON)


def norm_backward(values, scale_vector, gain_vector, upstream):
    weighted = upstream * gain_vector
    inner_mean = jnp.mean(weighted * values, axis=-1, keepdims=True)
    grad_input = (
        scale_vector * weighted - values * scale_vector * scale_vector * scale_vector * inner_mean
    )
    grad_gain = jnp.sum(upstream * values * scale_vector, axis=0)
    return (grad_input, grad_gain)


def contract_rows(left_matrix, right_matrix):
    return lax.dot_general(left_matrix, right_matrix, ROWS, preferred_element_type=F32)


def contract_cols(left_matrix, right_matrix):
    return lax.dot_general(left_matrix, right_matrix, COLS, preferred_element_type=F32)


def exchange(array, axes):
    return lax.all_to_all(array, axes, split_axis=0, concat_axis=0, tiled=True)


def spread(array, axes):
    return exchange(jnp.broadcast_to(array[None], (lax.axis_size(axes), *array.shape)), axes)


def sum_everywhere(part):
    rows, columns = part.shape
    chips = lax.axis_size(CHIPS)
    side = columns // 4
    tall = rows // (chips // 2)
    pieces = part.astype(BF).reshape(chips // 2, tall, 4, side).transpose(2, 0, 1, 3)
    first = lax.axis_index("core") == 0
    kept = jnp.where(first, pieces[:2], pieces[2:])
    given = jnp.where(first, pieces[2:], pieces[:2])
    got = lax.ppermute(given, "core", SWAP)
    half = (kept.astype(F32) + got.astype(F32)).astype(BF).reshape(chips, tall, side)
    share = jnp.sum(exchange(half, CHIPS).astype(F32), axis=0).astype(BF)
    mine = spread(share, CHIPS).reshape(2, chips // 2, tall, side)
    other = lax.ppermute(mine, "core", SWAP)
    whole = jnp.where(
        first, jnp.concatenate([mine, other], axis=0), jnp.concatenate([other, mine], axis=0)
    )
    return whole.transpose(1, 2, 0, 3).reshape(rows, columns).astype(F32)


def shear(tile, rows, width):
    while rows > 8:
        half = rows // 2
        tile = pltpu.roll(tile[:half], half, axis=1) + tile[half:]
        rows = half
    total = tile[rows - 1 : rows]
    for row in range(rows - 1):
        total = total + pltpu.roll(tile[row : row + 1], rows - 1 - row, axis=1)
    return total


def by_position(place_ref, source_ref, target_ref, half, blocks):
    for block in range(blocks):
        source = pl.ds(pl.multiple_of(place_ref[block] * half, half), half)
        target_ref[block * half : (block + 1) * half] = source_ref[source]


def head_lanes(array, head):
    lanes = lax.broadcasted_iota(jnp.int32, array.shape, 1) // (LANES // 2)
    return jnp.where(lanes == head, array.astype(F32), 0.0)


def attend_kernel(
    place_ref, q_ref, k_ref, v_ref, window_ref, out_ref, prob_ref, k_pos, v_pos, *, half, blocks
):
    by_position(place_ref, k_ref, k_pos, half, blocks)
    by_position(place_ref, v_ref, v_pos, half, blocks)
    seq = half * blocks
    window = seq + 2 * half
    total_out = None
    for head in range(2):
        q = (head_lanes(q_ref[...], head) * (LANES // 2) ** -0.5).astype(BF)
        raw = lax.dot_general(q, k_pos[...], COLS, preferred_element_type=F32)
        parts = []
        for part in range(2):
            row = 2 * head + part
            tile = jnp.broadcast_to(window_ref[row : row + 1, :], (half, window))
            tile = pltpu.roll(tile, window - half + 1, axis=1, stride=1, stride_axis=0)
            parts.append(raw[part * half : (part + 1) * half] + tile[:, :seq])
        scores = jnp.concatenate(parts, axis=0)
        exps = jnp.exp(scores - jnp.max(scores, axis=1, keepdims=True))
        prob = (exps * (1.0 / jnp.sum(exps, axis=1, keepdims=True))).astype(BF)
        prob_ref[head] = prob
        out = head_lanes(jnp.dot(prob, v_pos[...], preferred_element_type=F32), head)
        total_out = out if total_out is None else total_out + out
    out_ref[...] = total_out.astype(BF)


def attend(place, queries, key_value, windows, half):
    rows, width = queries.shape
    seq = key_value.shape[0]
    pairs = width // LANES
    window = seq + 2 * half
    work = rows * seq * width
    return pl.pallas_call(
        functools.partial(attend_kernel, half=half, blocks=seq // half),
        grid_spec=pltpu.PrefetchScalarGridSpec(
            num_scalar_prefetch=1,
            grid=(pairs,),
            in_specs=[
                pl.BlockSpec((rows, LANES), lambda h, p: (0, h)),
                pl.BlockSpec((seq, LANES), lambda h, p: (0, h)),
                pl.BlockSpec((seq, LANES), lambda h, p: (0, pairs + h)),
                pl.BlockSpec((None, 4, window), lambda h, p: (h, 0, 0)),
            ],
            out_specs=[
                pl.BlockSpec((rows, LANES), lambda h, p: (0, h)),
                pl.BlockSpec((2, rows, seq), lambda h, p: (h, 0, 0)),
            ],
            scratch_shapes=[pltpu.VMEM((seq, LANES), BF), pltpu.VMEM((seq, LANES), BF)],
        ),
        out_shape=[
            jax.ShapeDtypeStruct((rows, width), BF),
            jax.ShapeDtypeStruct((2 * pairs, rows, seq), BF),
        ],
        compiler_params=pltpu.CompilerParams(vmem_limit_bytes=VMEM_LIMIT),
        cost_estimate=pl.CostEstimate(
            flops=8 * work,
            bytes_accessed=4 * seq * width + 4 * pairs * rows * seq,
            transcendentals=2 * pairs * rows * seq,
        ),
        name="attend",
    )(place, queries, key_value, key_value, windows)


def attend_back_kernel(
    place_ref,
    prob_ref,
    q_ref,
    k_ref,
    v_ref,
    grad_ref,
    dq_ref,
    dkv_ref,
    diag_ref,
    k_pos,
    v_pos,
    *,
    half,
    blocks,
):
    seq = half * blocks

    def by_place(source_ref):
        for block in range(blocks):
            target = pl.ds(pl.multiple_of(place_ref[block] * half, half), half)
            dkv_ref[target] = source_ref[block * half : (block + 1) * half]

    @pl.when(pl.program_id(1) == 0)
    def _():
        by_position(place_ref, k_ref, k_pos, half, blocks)
        by_position(place_ref, v_ref, v_pos, half, blocks)
        factor = (LANES // 2) ** -0.5
        query_grad = None
        qs, score_grads, grads, probs = [], [], [], []
        for head in range(2):
            q = (head_lanes(q_ref[...], head) * factor).astype(BF)
            grad = head_lanes(grad_ref[...], head).astype(BF)
            prob = prob_ref[head]
            wide = prob.astype(F32)
            prob_grad = lax.dot_general(grad, v_pos[...], COLS, preferred_element_type=F32)
            inner = jnp.sum(wide * prob_grad, axis=1, keepdims=True)
            score_grad = wide * (prob_grad - inner)
            for part in range(2):
                row = 2 * head + part
                tile = score_grad[part * half : (part + 1) * half]
                tile = jnp.concatenate([tile, jnp.zeros((half, 2 * half), F32)], axis=1)
                diag_ref[row : row + 1, :] = shear(tile, half, seq + 2 * half)
            score_grad = score_grad.astype(BF)
            out = jnp.dot(score_grad, k_pos[...], preferred_element_type=F32) * factor
            out = head_lanes(out, head)
            query_grad = out if query_grad is None else query_grad + out
            qs.append(q)
            score_grads.append(score_grad)
            grads.append(grad)
            probs.append(prob)
        dq_ref[...] = query_grad.astype(BF)
        joined = functools.partial(jnp.concatenate, axis=0)
        dk = lax.dot_general(joined(score_grads), joined(qs), ROWS, preferred_element_type=F32)
        k_pos[...] = dk.astype(BF)
        by_place(k_pos)
        dv = lax.dot_general(joined(probs), joined(grads), ROWS, preferred_element_type=F32)
        v_pos[...] = dv.astype(BF)

    @pl.when(pl.program_id(1) == 1)
    def _():
        by_place(v_pos)


def attend_back(place, prob, queries, key_value, attended_grad, half):
    rows, width = queries.shape
    seq = key_value.shape[0]
    pairs = width // LANES
    window = seq + 2 * half
    return pl.pallas_call(
        functools.partial(attend_back_kernel, half=half, blocks=seq // half),
        grid_spec=pltpu.PrefetchScalarGridSpec(
            num_scalar_prefetch=1,
            grid=(pairs, 2),
            in_specs=[
                pl.BlockSpec((2, rows, seq), lambda h, j, p: (h, 0, 0)),
                pl.BlockSpec((rows, LANES), lambda h, j, p: (0, h)),
                pl.BlockSpec((seq, LANES), lambda h, j, p: (0, h)),
                pl.BlockSpec((seq, LANES), lambda h, j, p: (0, pairs + h)),
                pl.BlockSpec((rows, LANES), lambda h, j, p: (0, h)),
            ],
            out_specs=[
                pl.BlockSpec((rows, LANES), lambda h, j, p: (0, h)),
                pl.BlockSpec((seq, LANES), lambda h, j, p: (0, h + pairs * j)),
                pl.BlockSpec((None, 4, window), lambda h, j, p: (h, 0, 0)),
            ],
            scratch_shapes=[pltpu.VMEM((seq, LANES), BF), pltpu.VMEM((seq, LANES), BF)],
        ),
        out_shape=[
            jax.ShapeDtypeStruct((rows, width), BF),
            jax.ShapeDtypeStruct((seq, 2 * width), BF),
            jax.ShapeDtypeStruct((pairs, 4, window), F32),
        ],
        compiler_params=pltpu.CompilerParams(vmem_limit_bytes=VMEM_LIMIT),
        cost_estimate=pl.CostEstimate(
            flops=16 * rows * seq * width,
            bytes_accessed=8 * seq * width + 4 * pairs * rows * seq,
            transcendentals=0,
        ),
        name="attend_back",
    )(place, prob, queries, key_value, key_value, attended_grad)


def expert_kernel(
    x_ref, cot_ref, in_ref, out_ref, back_ref, grad_in_ref, grad_out_ref, ret_sum, dx_sum
):
    part = pl.program_id(1)
    width = cot_ref.shape[-1]
    rows = x_ref.shape[0] * x_ref.shape[1]
    rows_in = x_ref[...].reshape(rows, x_ref.shape[2])
    x = rows_in[:, :width]
    gate = jnp.sum(rows_in[:, width:].astype(F32), axis=1, keepdims=True)
    weight_in, weight_out = in_ref[...], out_ref[...]
    slot_grad = (cot_ref[...].reshape(rows, width).astype(F32) * gate).astype(BF)
    pre = jnp.dot(x, weight_in, preferred_element_type=F32)
    cumulative = 0.5 * (1.0 + lax.erf(pre * 0.7071067811865476))
    activated = (pre * cumulative).astype(BF)
    slope = cumulative + pre * (jnp.exp(-0.5 * pre * pre) * 0.3989422804014327)
    returned = jnp.dot(activated, weight_out, preferred_element_type=F32)
    act_grad = lax.dot_general(slot_grad, weight_out, COLS, preferred_element_type=F32)
    pre_grad = (act_grad * slope).astype(BF)
    input_grad = lax.dot_general(pre_grad, weight_in, COLS, preferred_element_type=F32)

    @pl.when(part == 0)
    def _():
        ret_sum[...] = returned
        dx_sum[...] = input_grad

    @pl.when(part > 0)
    def _():
        ret_sum[...] += returned
        dx_sum[...] += input_grad

    @pl.when(part == pl.num_programs(1) - 1)
    def _():
        shape = cot_ref.shape
        back_ref[:, :, :width] = ret_sum[...].astype(BF).reshape(shape)
        back_ref[:, :, width:] = dx_sum[...].astype(BF).reshape(shape)

    grad_in = lax.dot_general(x, pre_grad, ROWS, preferred_element_type=F32)
    grad_out = lax.dot_general(activated, slot_grad, ROWS, preferred_element_type=F32)
    grad_in_ref[...] = grad_in.astype(BF)
    grad_out_ref[...] = grad_out.astype(BF)


def run_experts(x_rows, cot_rows, weight_in, weight_out):
    devices, experts, slots, width = cot_rows.shape
    wide = x_rows.shape[3]
    parts, _, _, hidden = weight_in.shape
    rows = devices * slots

    def row_spec(columns):
        return pl.BlockSpec((devices, None, slots, columns), lambda e, w: (0, e, 0, 0))

    in_spec = pl.BlockSpec((None, None, width, hidden), lambda e, w: (w, e, 0, 0))
    out_spec = pl.BlockSpec((None, None, hidden, width), lambda e, w: (w, e, 0, 0))
    work = experts * rows * width * parts * hidden
    return pl.pallas_call(
        expert_kernel,
        grid=(experts, parts),
        in_specs=[row_spec(wide), row_spec(width), in_spec, out_spec],
        out_specs=[row_spec(2 * width), in_spec, out_spec],
        out_shape=[
            jax.ShapeDtypeStruct((devices, experts, slots, 2 * width), BF),
            jax.ShapeDtypeStruct(weight_in.shape, BF),
            jax.ShapeDtypeStruct(weight_out.shape, BF),
        ],
        scratch_shapes=[pltpu.VMEM((rows, width), F32), pltpu.VMEM((rows, width), F32)],
        compiler_params=pltpu.CompilerParams(vmem_limit_bytes=VMEM_LIMIT),
        cost_estimate=pl.CostEstimate(
            flops=12 * work,
            bytes_accessed=8 * experts * rows * width + 8 * parts * experts * width * hidden,
            transcendentals=2 * experts * rows * parts * hidden,
        ),
        name="experts",
    )(x_rows, cot_rows, weight_in, weight_out)


def on_device(
    tokens,
    gain_attn,
    w_qkv,
    rel_bias,
    w_attn_out,
    gain_ffn,
    w_router,
    w_in,
    w_out,
    routes,
    pair_order,
    bucket_table,
    cotangent,
):
    tok_rows = tokens.shape[1]
    model_width = tokens.shape[2]
    head_count = rel_bias.shape[1]
    bucket_count = rel_bias.shape[0]
    ctx_count = lax.axis_size(CTX)
    half = tok_rows // 2
    blocks = 2 * ctx_count
    seq = half * blocks
    window = seq + 2 * half
    head_pairs = head_count // 2
    local_experts = w_in.shape[0]
    experts = w_router.shape[1]
    capacity = 4 * tok_rows // experts
    device_slots = local_experts * capacity
    expert_devices = lax.axis_size(EXPERT_AXES)
    copies = expert_devices // ctx_count

    near_tokens = spread(tokens[0], SAME_CORE)
    far_tokens = lax.ppermute(near_tokens, "core", SWAP)
    all_tokens = jnp.concatenate([near_tokens, far_tokens], axis=0).reshape(seq, model_width)
    whole_in = lax.all_gather(w_in, "x", axis=0)
    whole_out = lax.all_gather(w_out, "x", axis=0)

    chosen = routes[0].T
    expert_ids = jnp.arange(experts, dtype=jnp.int32)
    flat_expert = chosen.reshape(2 * tok_rows)
    member = flat_expert[:, None] == expert_ids[None, :]
    picks = jnp.arange(2 * tok_rows, dtype=jnp.int32)
    before = (picks[:, None] > picks[None, :]).astype(BF)
    counts = jnp.dot(before, member.astype(BF), preferred_element_type=F32)
    slot_rank = jnp.sum(jnp.where(member, counts, 0.0), axis=1).astype(jnp.int32)
    owner_index = flat_expert // local_experts
    slot_of = (flat_expert % local_experts) * capacity + slot_rank
    slot_ids = jnp.arange(expert_devices * device_slots, dtype=jnp.int32)
    slot_hot = (owner_index[:, None] == (slot_ids // (copies * device_slots))[None, :]) & (
        slot_of[:, None] == (slot_ids % device_slots)[None, :]
    )
    slot_table = slot_hot.astype(BF)
    token_table = slot_table[:tok_rows] + slot_table[tok_rows:]

    def to_experts(table, rows):
        slots = contract_rows(table, rows).astype(BF)
        arrived = exchange(slots.reshape(expert_devices, device_slots, rows.shape[1]), EXPERT_AXES)
        return arrived.reshape(expert_devices, local_experts, capacity, rows.shape[1])

    cot_rows = to_experts(token_table, cotangent[0])

    ctx_ids = jnp.arange(ctx_count, dtype=jnp.int32)
    my_core = lax.axis_index("core")
    near = (ctx_ids % 2) == my_core
    lies = 2 * (jnp.where(near, 0, ctx_count // 2) + ctx_ids // 2)
    block_ids = jnp.arange(blocks, dtype=jnp.int32)[:, None]
    place = jnp.sum(
        jnp.where(pair_order[None, :] == block_ids, lies[None, :], 0)
        + jnp.where(blocks - 1 - pair_order[None, :] == block_ids, lies[None, :] + 1, 0),
        axis=1,
        dtype=jnp.int32,
    )
    my_pair = jnp.sum(jnp.where(ctx_ids == lax.axis_index(CTX), pair_order, 0))
    reversed_table = jnp.pad(bucket_table[::-1], (0, window - half), constant_values=-1)
    diagonal_bucket = jnp.stack(
        [
            lax.dynamic_slice(reversed_table, (seq - half - block * half,), (window,))
            for block in (my_pair, blocks - 1 - my_pair)
        ]
    ).reshape(1, 2 * window)
    bucket_ids = jnp.arange(bucket_count, dtype=jnp.int32)
    bucket_hot = (diagonal_bucket == bucket_ids[:, None]).astype(F32)
    windows = lax.dot_general(rel_bias, bucket_hot, ROWS, precision=HIGHEST)
    windows = jnp.where(diagonal_bucket >= 0, windows, MASKED)
    windows = windows.reshape(head_pairs, 4, window)

    w_q, w_kv = w_qkv[:, :model_width], w_qkv[:, model_width:]
    inputs = tokens[0].astype(F32)
    scale_one = norm_scale(inputs)
    normed_one = (inputs * scale_one * gain_attn).astype(BF)
    queries = jnp.dot(normed_one, w_q, preferred_element_type=F32).astype(BF)
    all_inputs = all_tokens.astype(F32)
    all_normed = (all_inputs * norm_scale(all_inputs) * gain_attn).astype(BF)
    key_value = jnp.dot(all_normed, w_kv, preferred_element_type=F32).astype(BF)
    attended, probabilities = attend(place, queries, key_value, windows, half)
    residual_one = inputs + jnp.dot(attended, w_attn_out, preferred_element_type=F32)
    scale_two = norm_scale(residual_one)
    normed_two = (residual_one * scale_two * gain_ffn).astype(BF)

    router_logits = jnp.dot(normed_two, w_router, preferred_element_type=F32)
    chosen_hot = (chosen[:, :, None] == expert_ids[None, None, :]).astype(F32)
    picked_logits = jnp.sum(chosen_hot * router_logits[None], axis=2)
    logit_peak = jnp.max(picked_logits, axis=0, keepdims=True)
    gate_exp = jnp.exp(picked_logits - logit_peak)
    gate_weights = (gate_exp / jnp.sum(gate_exp, axis=0, keepdims=True))[:, :, None]

    flat_gate = gate_weights.reshape(2 * tok_rows, 1)
    gate_high = flat_gate.astype(BF).astype(F32)
    lane_ids = jnp.arange(LANES, dtype=jnp.int32)[None, :]
    gate_lanes = jnp.where(lane_ids == 0, gate_high, 0.0)
    gate_lanes = jnp.where(lane_ids == 1, flat_gate - gate_high, gate_lanes).astype(BF)
    pick_rows = jnp.concatenate([normed_two, normed_two], axis=0)
    x_rows = to_experts(slot_table, jnp.concatenate([pick_rows, gate_lanes], axis=1))
    back, part_in, part_out = run_experts(x_rows, cot_rows, whole_in, whole_out)
    grad_w_in = lax.psum_scatter(part_in, "x", scatter_dimension=0).astype(F32)
    grad_w_out = lax.psum_scatter(part_out, "x", scatter_dimension=0).astype(F32)
    back = exchange(back.reshape(expert_devices, device_slots, 2 * model_width), EXPERT_AXES)
    back = back.reshape(expert_devices * device_slots, 2 * model_width)
    picked = jnp.dot(slot_table, back[:, :model_width], preferred_element_type=F32)
    picked = picked.reshape(2, tok_rows, model_width)
    expert_part = jnp.dot(token_table, back[:, model_width:], preferred_element_type=F32)
    mixture = jnp.sum(gate_weights * picked, axis=0)
    layer_out = (residual_one + mixture).astype(BF)[None]

    upstream = cotangent[0].astype(F32)
    gate_grad = jnp.sum(picked * upstream[None], axis=2, keepdims=True)
    inner_mean = jnp.sum(gate_weights * gate_grad, axis=0, keepdims=True)
    pick_grad = gate_weights * (gate_grad - inner_mean)
    logit_grad = jnp.sum(pick_grad * chosen_hot, axis=0)
    grad_w_router = lax.dot_general(normed_two.astype(F32), logit_grad, ROWS, precision=HIGHEST)
    router_back = lax.dot_general(logit_grad, w_router.astype(F32), COLS, precision=HIGHEST)
    normed_two_grad = expert_part + router_back
    norm_part, grad_gain_ffn = norm_backward(residual_one, scale_two, gain_ffn, normed_two_grad)
    mixed_grad = upstream + norm_part
    branch_grad = mixed_grad.astype(BF)
    grad_w_attn_out = contract_rows(attended, branch_grad)

    attended_grad = contract_cols(branch_grad, w_attn_out).astype(BF)
    query_grad, key_value_grad, diagonals = attend_back(
        place, probabilities, queries, key_value, attended_grad, half
    )
    all_normed_grad = contract_cols(key_value_grad, w_kv)
    all_normed_grad = all_normed_grad.reshape(2, ctx_count // 2, tok_rows, model_width)
    far_grad = lax.ppermute(all_normed_grad[1].astype(BF), "core", SWAP)
    near_grad = (all_normed_grad[0] + far_grad.astype(F32)).astype(BF)
    normed_one_grad = jnp.sum(exchange(near_grad, SAME_CORE).astype(F32), axis=0)
    normed_one_grad = normed_one_grad + contract_cols(query_grad, w_q)
    input_norm_grad, grad_gain_attn = norm_backward(inputs, scale_one, gain_attn, normed_one_grad)
    grad_tokens = (mixed_grad + input_norm_grad)[None]
    diagonals = diagonals.reshape(head_count, 2 * window)
    grad_rel_bias = lax.dot_general(bucket_hot, diagonals, COLS, precision=HIGHEST)
    grad_w_q = contract_rows(normed_one, query_grad)
    grad_w_kv = contract_rows(all_normed, key_value_grad)

    def column(array):
        array = array.reshape(-1)
        return jnp.pad(array, (0, model_width - array.shape[0]))[:, None]

    small = [grad_w_router, column(grad_rel_bias), column(grad_gain_ffn), column(grad_gain_attn)]
    wide = 5 * LANES * 4
    used = 3 * model_width + experts + 3
    small.append(jnp.zeros((model_width, wide - used), F32))
    sums = sum_everywhere(jnp.concatenate([grad_w_q, grad_w_kv, *small], axis=1))
    sum_w_attn_out = sum_everywhere(grad_w_attn_out)
    at = 3 * model_width
    sum_w_router = sums[:, at : at + experts]
    at = at + experts
    sum_rel_bias = sums[: bucket_count * head_count, at].reshape(bucket_count, head_count)
    return (
        layer_out,
        grad_tokens,
        sums[:, at + 2],
        sums[:, : 3 * model_width],
        sum_rel_bias,
        sum_w_attn_out,
        sums[:, at + 1],
        sum_w_router,
        grad_w_in,
        grad_w_out,
    )


def solution(mesh):
    split_mesh = Mesh(mesh.devices.reshape(SPLIT), EVERY)
    in_specs = (
        P(WSH, CTX, None),
        P(),
        P(),
        P(),
        P(),
        P(),
        P(),
        P(CTX, None, WSH),
        P(CTX, WSH, None),
        P(WSH, CTX, None),
        P(),
        P(),
        P(WSH, CTX, None),
    )
    out_specs = (
        P(WSH, CTX, None),
        P(WSH, CTX, None),
        P(),
        P(),
        P(),
        P(),
        P(),
        P(),
        P(CTX, None, WSH),
        P(CTX, WSH, None),
    )
    return jax.shard_map(
        on_device, mesh=split_mesh, in_specs=in_specs, out_specs=out_specs, check_vma=False
    )
```

```python
import functools

import jax
import jax.numpy as jnp
from jax import lax
from jax.experimental import pallas as pl
from jax.experimental.pallas import tpu as pltpu
from jax.sharding import Mesh
from jax.sharding import PartitionSpec as P

BF = jnp.bfloat16
F32 = jnp.float32
EPSILON = 1e-06
HIGHEST = lax.Precision.HIGHEST
MASKED = -1e30
ROWS = (((0,), (0,)), ((), ()))
COLS = (((1,), (1,)), ((), ()))
LANES = 128
VMEM_LIMIT = 44 * 1024 * 1024
SPLIT = (2, 4, 2, 2, 4)
EVERY = ("ya", "z", "core", "yb", "x")
CTX = ("ya", "z", "core")
WSH = ("yb", "x")
SAME_CORE = ("ya", "z")
CHIPS = ("ya", "z", "yb", "x")
EXPERT_AXES = ("ya", "z", "core", "yb")
SWAP = ((0, 1), (1, 0))


def norm_scale(values):
    return lax.rsqrt(jnp.mean(values * values, axis=-1, keepdims=True) + EPSILON)


def norm_backward(values, scale_vector, gain_vector, upstream):
    weighted = upstream * gain_vector
    inner_mean = jnp.mean(weighted * values, axis=-1, keepdims=True)
    grad_input = (
        scale_vector * weighted - values * scale_vector * scale_vector * scale_vector * inner_mean
    )
    grad_gain = jnp.sum(upstream * values * scale_vector, axis=0)
    return (grad_input, grad_gain)


def contract_rows(left_matrix, right_matrix):
    return lax.dot_general(left_matrix, right_matrix, ROWS, preferred_element_type=F32)


def contract_cols(left_matrix, right_matrix):
    return lax.dot_general(left_matrix, right_matrix, COLS, preferred_element_type=F32)


def exchange(array, axes):
    return lax.all_to_all(array, axes, split_axis=0, concat_axis=0, tiled=True)


def spread(array, axes):
    return exchange(jnp.broadcast_to(array[None], (lax.axis_size(axes), *array.shape)), axes)


def sum_halves(kept, given):
    rows, columns = kept.shape
    chips = lax.axis_size(CHIPS)
    got = lax.ppermute(given, "core", SWAP)
    half = (kept.astype(F32) + got.astype(F32)).astype(BF).reshape(chips, rows // chips, columns)
    share = jnp.sum(exchange(half, CHIPS).astype(F32), axis=0).astype(BF)
    mine = spread(share, CHIPS).reshape(rows, columns)
    return mine, lax.ppermute(mine, "core", SWAP)


def shear(tile, rows):
    while rows > 8:
        half = rows // 2
        tile = pltpu.roll(tile[:half], half, axis=1) + tile[half:]
        rows = half
    total = tile[rows - 1 : rows]
    for row in range(rows - 1):
        total = total + pltpu.roll(tile[row : row + 1], rows - 1 - row, axis=1)
    return total


def head_lanes(array, head):
    lanes = lax.broadcasted_iota(jnp.int32, array.shape, 1) // (LANES // 2)
    return jnp.where(lanes == head, array.astype(F32), 0.0)


def attend_kernel(q_ref, k_ref, v_ref, window_ref, out_ref, prob_ref):
    half, seq = q_ref.shape[0] // 2, k_ref.shape[0]
    window = seq + 2 * half
    total_out = None
    for head in range(2):
        q = (head_lanes(q_ref[...], head) * (LANES // 2) ** -0.5).astype(BF)
        raw = lax.dot_general(q, k_ref[...], COLS, preferred_element_type=F32)
        parts = []
        for part in range(2):
            row = 2 * head + part
            tile = jnp.broadcast_to(window_ref[row : row + 1, :], (half, window))
            tile = pltpu.roll(tile, window - half + 1, axis=1, stride=1, stride_axis=0)
            parts.append(raw[part * half : (part + 1) * half] + tile[:, :seq])
        scores = jnp.concatenate(parts, axis=0)
        exps = jnp.exp(scores - jnp.max(scores, axis=1, keepdims=True))
        prob = (exps * (1.0 / jnp.sum(exps, axis=1, keepdims=True))).astype(BF)
        prob_ref[head] = prob
        out = head_lanes(jnp.dot(prob, v_ref[...], preferred_element_type=F32), head)
        total_out = out if total_out is None else total_out + out
    out_ref[...] = total_out.astype(BF)


def attend(queries, key_value, windows):
    rows, width = queries.shape
    seq = key_value.shape[0]
    pairs = width // LANES
    work = rows * seq * width
    return pl.pallas_call(
        attend_kernel,
        grid=(pairs,),
        in_specs=[
            pl.BlockSpec((rows, LANES), lambda h: (0, h)),
            pl.BlockSpec((seq, LANES), lambda h: (0, h)),
            pl.BlockSpec((seq, LANES), lambda h: (0, pairs + h)),
            pl.BlockSpec((None, 4, windows.shape[2]), lambda h: (h, 0, 0)),
        ],
        out_specs=[
            pl.BlockSpec((rows, LANES), lambda h: (0, h)),
            pl.BlockSpec((2, rows, seq), lambda h: (h, 0, 0)),
        ],
        out_shape=[
            jax.ShapeDtypeStruct((rows, width), BF),
            jax.ShapeDtypeStruct((2 * pairs, rows, seq), BF),
        ],
        compiler_params=pltpu.CompilerParams(vmem_limit_bytes=VMEM_LIMIT),
        cost_estimate=pl.CostEstimate(
            flops=8 * work,
            bytes_accessed=4 * seq * width + 4 * pairs * rows * seq,
            transcendentals=2 * pairs * rows * seq,
        ),
        name="attend",
    )(queries, key_value, key_value, windows)


def attend_back_kernel(
    prob_ref, q_ref, k_ref, v_ref, grad_ref, dq_ref, dkv_ref, diag_ref, dv_kept
):
    half, seq = q_ref.shape[0] // 2, k_ref.shape[0]

    @pl.when(pl.program_id(1) == 0)
    def _():
        factor = (LANES // 2) ** -0.5
        query_grad = None
        qs, score_grads, grads, probs = [], [], [], []
        for head in range(2):
            q = (head_lanes(q_ref[...], head) * factor).astype(BF)
            grad = head_lanes(grad_ref[...], head).astype(BF)
            prob = prob_ref[head]
            wide = prob.astype(F32)
            prob_grad = lax.dot_general(grad, v_ref[...], COLS, preferred_element_type=F32)
            inner = jnp.sum(wide * prob_grad, axis=1, keepdims=True)
            score_grad = wide * (prob_grad - inner)
            for part in range(2):
                row = 2 * head + part
                tile = score_grad[part * half : (part + 1) * half]
                tile = jnp.concatenate([tile, jnp.zeros((half, 2 * half), F32)], axis=1)
                diag_ref[row : row + 1, :] = shear(tile, half)
            score_grad = score_grad.astype(BF)
            out = jnp.dot(score_grad, k_ref[...], preferred_element_type=F32) * factor
            out = head_lanes(out, head)
            query_grad = out if query_grad is None else query_grad + out
            qs.append(q)
            score_grads.append(score_grad)
            grads.append(grad)
            probs.append(prob)
        dq_ref[...] = query_grad.astype(BF)
        joined = functools.partial(jnp.concatenate, axis=0)
        dk = lax.dot_general(joined(score_grads), joined(qs), ROWS, preferred_element_type=F32)
        dkv_ref[...] = dk.astype(BF)
        dv = lax.dot_general(joined(probs), joined(grads), ROWS, preferred_element_type=F32)
        dv_kept[...] = dv.astype(BF)

    @pl.when(pl.program_id(1) == 1)
    def _():
        dkv_ref[...] = dv_kept[...]


def attend_back(prob, queries, key_value, attended_grad):
    rows, width = queries.shape
    seq = key_value.shape[0]
    pairs = width // LANES
    window = seq + rows
    return pl.pallas_call(
        attend_back_kernel,
        grid=(pairs, 2),
        in_specs=[
            pl.BlockSpec((2, rows, seq), lambda h, j: (h, 0, 0)),
            pl.BlockSpec((rows, LANES), lambda h, j: (0, h)),
            pl.BlockSpec((seq, LANES), lambda h, j: (0, h)),
            pl.BlockSpec((seq, LANES), lambda h, j: (0, pairs + h)),
            pl.BlockSpec((rows, LANES), lambda h, j: (0, h)),
        ],
        out_specs=[
            pl.BlockSpec((rows, LANES), lambda h, j: (0, h)),
            pl.BlockSpec((seq, LANES), lambda h, j: (0, h + pairs * j)),
            pl.BlockSpec((None, 4, window), lambda h, j: (h, 0, 0)),
        ],
        scratch_shapes=[pltpu.VMEM((seq, LANES), BF)],
        out_shape=[
            jax.ShapeDtypeStruct((rows, width), BF),
            jax.ShapeDtypeStruct((seq, 2 * width), BF),
            jax.ShapeDtypeStruct((pairs, 4, window), F32),
        ],
        compiler_params=pltpu.CompilerParams(vmem_limit_bytes=VMEM_LIMIT),
        cost_estimate=pl.CostEstimate(
            flops=16 * rows * seq * width,
            bytes_accessed=8 * seq * width + 4 * pairs * rows * seq,
            transcendentals=0,
        ),
        name="attend_back",
    )(prob, queries, key_value, key_value, attended_grad)


def key_value_kernel(place_ref, near_ref, far_ref, gain_ref, wk_ref, wv_ref, normed_ref, kv_ref, *, half):
    tile = normed_ref.shape[0] // half
    near_blocks = near_ref.shape[0] // half
    rows = []
    for block in range(tile):
        source = place_ref[pl.program_id(0) * tile + block]
        at = pl.ds(pl.multiple_of(lax.rem(source, near_blocks) * half, half), half)
        rows.append(jnp.where(source < near_blocks, near_ref[at].astype(F32), far_ref[at].astype(F32)))
    inputs = jnp.concatenate(rows, axis=0)
    normed = (inputs * norm_scale(inputs) * gain_ref[...]).astype(BF)
    normed_ref[...] = normed
    width = normed.shape[1]
    kv_ref[:, :width] = jnp.dot(normed, wk_ref[...], preferred_element_type=F32).astype(BF)
    kv_ref[:, width:] = jnp.dot(normed, wv_ref[...], preferred_element_type=F32).astype(BF)


def keys_and_values(place, near, far, gain, w_qkv, half):
    near_rows, width = near.shape
    seq = 2 * near_rows
    tile = 4 * half
    return pl.pallas_call(
        functools.partial(key_value_kernel, half=half),
        grid_spec=pltpu.PrefetchScalarGridSpec(
            num_scalar_prefetch=1,
            grid=(seq // tile,),
            in_specs=[
                pl.BlockSpec((near_rows, width), lambda r, p: (0, 0)),
                pl.BlockSpec((near_rows, width), lambda r, p: (0, 0)),
                pl.BlockSpec((1, width), lambda r, p: (0, 0)),
                pl.BlockSpec((width, width), lambda r, p: (0, 1)),
                pl.BlockSpec((width, width), lambda r, p: (0, 2)),
            ],
            out_specs=[
                pl.BlockSpec((tile, width), lambda r, p: (r, 0)),
                pl.BlockSpec((tile, 2 * width), lambda r, p: (r, 0)),
            ],
        ),
        out_shape=[
            jax.ShapeDtypeStruct((seq, width), BF),
            jax.ShapeDtypeStruct((seq, 2 * width), BF),
        ],
        compiler_params=pltpu.CompilerParams(vmem_limit_bytes=VMEM_LIMIT),
        cost_estimate=pl.CostEstimate(
            flops=4 * seq * width * width, bytes_accessed=8 * seq * width, transcendentals=seq
        ),
        name="keys_and_values",
    )(place, near, far, gain[None], w_qkv, w_qkv)


def normed_grad_kernel(position_ref, dkv_ref, wk_ref, wv_ref, out_ref, *, half):
    tile = out_ref.shape[0] // half
    rows = []
    for block in range(tile):
        source = position_ref[pl.program_id(0) * tile + block]
        rows.append(dkv_ref[pl.ds(pl.multiple_of(source * half, half), half)])
    grads = jnp.concatenate(rows, axis=0)
    width = out_ref.shape[1]
    out = lax.dot_general(grads[:, :width], wk_ref[...], COLS, preferred_element_type=F32)
    out += lax.dot_general(grads[:, width:], wv_ref[...], COLS, preferred_element_type=F32)
    out_ref[...] = out.astype(BF)


def normed_grads(position, key_value_grad, w_qkv, half):
    seq, width = key_value_grad.shape[0], w_qkv.shape[0]
    rows = position.shape[0] * half
    tile = 4 * half
    return pl.pallas_call(
        functools.partial(normed_grad_kernel, half=half),
        grid_spec=pltpu.PrefetchScalarGridSpec(
            num_scalar_prefetch=1,
            grid=(rows // tile,),
            in_specs=[
                pl.BlockSpec((seq, 2 * width), lambda r, p: (0, 0)),
                pl.BlockSpec((width, width), lambda r, p: (0, 1)),
                pl.BlockSpec((width, width), lambda r, p: (0, 2)),
            ],
            out_specs=pl.BlockSpec((tile, width), lambda r, p: (r, 0)),
        ),
        out_shape=jax.ShapeDtypeStruct((rows, width), BF),
        compiler_params=pltpu.CompilerParams(vmem_limit_bytes=VMEM_LIMIT),
        cost_estimate=pl.CostEstimate(
            flops=4 * rows * width * width, bytes_accessed=8 * rows * width, transcendentals=0
        ),
        name="normed_grads",
    )(position, key_value_grad, w_qkv, w_qkv)


def weight_grad_kernel(
    core_ref, dq_ref, normed_ref, dkv_ref, all_normed_ref, extra_ref, kept_ref, given_ref, total
):
    step = pl.program_id(0)
    tiles = normed_ref.shape[1] // dq_ref.shape[1]

    @pl.when(step < tiles)
    def _():
        total[...] = lax.dot_general(
            dq_ref[...], normed_ref[...], ROWS, preferred_element_type=F32
        )

    @pl.when((step >= tiles) & (step < 3 * tiles))
    def _():
        total[...] = lax.dot_general(
            dkv_ref[...], all_normed_ref[...], ROWS, preferred_element_type=F32
        )

    @pl.when(step == 3 * tiles)
    def _():
        total[...] = extra_ref[...]

    side = kept_ref.shape[1]
    left, right = total[:, :side].astype(BF), total[:, side:].astype(BF)

    @pl.when(core_ref[0] == 0)
    def _():
        kept_ref[...] = left
        given_ref[...] = right

    @pl.when(core_ref[0] != 0)
    def _():
        kept_ref[...] = right
        given_ref[...] = left


def weight_grads(core, query_grad, normed_one, key_value_grad, all_normed, extra):
    rows, width = normed_one.shape
    seq = all_normed.shape[0]
    tile = extra.shape[0]
    tiles = width // tile
    out_spec = pl.BlockSpec((tile, width // 2), lambda t, p: (t, 0))
    out_shape = jax.ShapeDtypeStruct((3 * width + tile, width // 2), BF)
    return pl.pallas_call(
        weight_grad_kernel,
        grid_spec=pltpu.PrefetchScalarGridSpec(
            num_scalar_prefetch=1,
            grid=(3 * tiles + 1,),
            in_specs=[
                pl.BlockSpec((rows, tile), lambda t, p: (0, jnp.minimum(t, tiles - 1))),
                pl.BlockSpec((rows, width), lambda t, p: (0, 0)),
                pl.BlockSpec((seq, tile), lambda t, p: (0, jnp.clip(t - tiles, 0, 2 * tiles - 1))),
                pl.BlockSpec((seq, width), lambda t, p: (0, 0)),
                pl.BlockSpec((tile, width), lambda t, p: (0, 0)),
            ],
            out_specs=[out_spec, out_spec],
            scratch_shapes=[pltpu.VMEM((tile, width), F32)],
        ),
        out_shape=[out_shape, out_shape],
        compiler_params=pltpu.CompilerParams(vmem_limit_bytes=VMEM_LIMIT),
        cost_estimate=pl.CostEstimate(
            flops=4 * seq * width * width, bytes_accessed=10 * seq * width, transcendentals=0
        ),
        name="weight_grads",
    )(core, query_grad, normed_one, key_value_grad, all_normed, extra)


def whole_grad_kernel(core_ref, mine_ref, other_ref, weight_ref, grad_ref, product_ref):
    side, tile = mine_ref.shape[1], mine_ref.shape[0]
    width = 2 * side
    first = pl.multiple_of(core_ref[0] * side, side)
    grad_ref[pl.ds(first, side), :] = mine_ref[...].astype(F32).T
    grad_ref[pl.ds(pl.multiple_of(side - first, side), side), :] = other_ref[...].astype(F32).T
    product = jnp.sum(grad_ref[...] * weight_ref[...].astype(F32), axis=1, keepdims=True)
    product = jnp.broadcast_to(product, (width, LANES))

    @pl.when(pl.program_id(0) == 0)
    def _():
        product_ref[...] = product

    @pl.when(pl.program_id(0) > 0)
    def _():
        product_ref[...] += product


def whole_grad(core, mine, other, weight):
    width, columns = weight.shape
    side = mine.shape[1]
    tile = 2 * LANES
    half_spec = pl.BlockSpec((tile, side), lambda t, p: (t, 0))
    whole_spec = pl.BlockSpec((width, tile), lambda t, p: (0, t))
    return pl.pallas_call(
        whole_grad_kernel,
        grid_spec=pltpu.PrefetchScalarGridSpec(
            num_scalar_prefetch=1,
            grid=(columns // tile,),
            in_specs=[half_spec, half_spec, whole_spec],
            out_specs=[whole_spec, pl.BlockSpec((width, LANES), lambda t, p: (0, 0))],
        ),
        out_shape=[
            jax.ShapeDtypeStruct((width, columns), F32),
            jax.ShapeDtypeStruct((width, LANES), F32),
        ],
        compiler_params=pltpu.CompilerParams(vmem_limit_bytes=VMEM_LIMIT),
        cost_estimate=pl.CostEstimate(
            flops=2 * width * columns, bytes_accessed=8 * width * columns, transcendentals=0
        ),
        name="whole_grad",
    )(core, mine, other, weight)


def expert_kernel(
    x_ref, cot_ref, in_ref, out_ref, back_ref, act_ref, pre_grad_ref, ret_sum, dx_sum
):
    part = pl.program_id(1)
    width = cot_ref.shape[-1]
    rows = x_ref.shape[0] * x_ref.shape[1]
    x, slot_grad = expert_rows(x_ref, cot_ref)
    weight_in, weight_out = in_ref[...], out_ref[...]
    pre = jnp.dot(x, weight_in, preferred_element_type=F32)
    act_grad = lax.dot_general(slot_grad, weight_out, COLS, preferred_element_type=F32)
    cumulative = 0.5 * (1.0 + lax.erf(pre * 0.7071067811865476))
    activated = (pre * cumulative).astype(BF)
    slope = cumulative + pre * (jnp.exp(-0.5 * pre * pre) * 0.3989422804014327)
    pre_grad = (act_grad * slope).astype(BF)
    act_ref[...] = activated
    pre_grad_ref[...] = pre_grad
    returned = jnp.dot(activated, weight_out, preferred_element_type=F32)
    input_grad = lax.dot_general(pre_grad, weight_in, COLS, preferred_element_type=F32)

    @pl.when(part == 0)
    def _():
        ret_sum[...] = returned
        dx_sum[...] = input_grad

    @pl.when(part > 0)
    def _():
        ret_sum[...] += returned
        dx_sum[...] += input_grad

    @pl.when(part == pl.num_programs(1) - 1)
    def _():
        shape = cot_ref.shape
        back_ref[:, :, :width] = ret_sum[...].astype(BF).reshape(shape)
        back_ref[:, :, width:] = dx_sum[...].astype(BF).reshape(shape)


def expert_rows(x_ref, cot_ref):
    width = cot_ref.shape[-1]
    rows = x_ref.shape[0] * x_ref.shape[1]
    rows_in = x_ref[...].reshape(rows, x_ref.shape[2])
    gate = jnp.sum(rows_in[:, width:].astype(F32), axis=1, keepdims=True)
    slot_grad = (cot_ref[...].reshape(rows, width).astype(F32) * gate).astype(BF)
    return rows_in[:, :width], slot_grad


def expert_grad_kernel(x_ref, cot_ref, act_ref, pre_grad_ref, grad_in_ref, grad_out_ref):
    x, slot_grad = expert_rows(x_ref, cot_ref)
    grad_in = lax.dot_general(x, pre_grad_ref[...], ROWS, preferred_element_type=F32)
    grad_out = lax.dot_general(act_ref[...], slot_grad, ROWS, preferred_element_type=F32)
    grad_in_ref[...] = grad_in.astype(BF)
    grad_out_ref[...] = grad_out.astype(BF)


def run_experts(x_rows, cot_rows, weight_in, weight_out):
    devices, experts, slots, width = cot_rows.shape
    wide = x_rows.shape[3]
    parts, _, _, hidden = weight_in.shape
    rows = devices * slots

    def row_spec(columns):
        return pl.BlockSpec((devices, None, slots, columns), lambda e, w: (0, e, 0, 0))

    def part_spec(tall, columns):
        return pl.BlockSpec((None, None, tall, columns), lambda e, w: (w, e, 0, 0))

    in_spec, out_spec = part_spec(width, hidden), part_spec(hidden, width)
    hidden_spec = part_spec(rows, hidden)
    hidden_shape = jax.ShapeDtypeStruct((parts, experts, rows, hidden), BF)
    work = experts * rows * width * parts * hidden
    params = pltpu.CompilerParams(vmem_limit_bytes=VMEM_LIMIT)
    back, activated, pre_grad = pl.pallas_call(
        expert_kernel,
        grid=(experts, parts),
        in_specs=[row_spec(wide), row_spec(width), in_spec, out_spec],
        out_specs=[row_spec(2 * width), hidden_spec, hidden_spec],
        out_shape=[
            jax.ShapeDtypeStruct((devices, experts, slots, 2 * width), BF),
            hidden_shape,
            hidden_shape,
        ],
        scratch_shapes=[pltpu.VMEM((rows, width), F32), pltpu.VMEM((rows, width), F32)],
        compiler_params=params,
        cost_estimate=pl.CostEstimate(
            flops=8 * work,
            bytes_accessed=8 * experts * rows * width + 8 * parts * experts * width * hidden,
            transcendentals=2 * experts * rows * parts * hidden,
        ),
        name="experts",
    )(x_rows, cot_rows, weight_in, weight_out)
    grads = pl.pallas_call(
        expert_grad_kernel,
        grid=(experts, parts),
        in_specs=[row_spec(wide), row_spec(width), hidden_spec, hidden_spec],
        out_specs=[in_spec, out_spec],
        out_shape=[
            jax.ShapeDtypeStruct(weight_in.shape, BF),
            jax.ShapeDtypeStruct(weight_out.shape, BF),
        ],
        compiler_params=params,
        cost_estimate=pl.CostEstimate(
            flops=4 * work,
            bytes_accessed=8 * experts * rows * width + 4 * parts * experts * width * hidden,
            transcendentals=0,
        ),
        name="expert_grads",
    )(x_rows, cot_rows, activated, pre_grad)
    return back, *grads


def on_device(
    tokens,
    gain_attn,
    w_qkv,
    rel_bias,
    w_attn_out,
    gain_ffn,
    w_router,
    w_in,
    w_out,
    routes,
    pair_order,
    bucket_table,
    cotangent,
):
    tok_rows = tokens.shape[1]
    model_width = tokens.shape[2]
    head_count = rel_bias.shape[1]
    bucket_count = rel_bias.shape[0]
    ctx_count = lax.axis_size(CTX)
    half = tok_rows // 2
    blocks = 2 * ctx_count
    seq = half * blocks
    window = seq + 2 * half
    head_pairs = head_count // 2
    local_experts = w_in.shape[0]
    experts = w_router.shape[1]
    capacity = 4 * tok_rows // experts
    device_slots = local_experts * capacity
    expert_devices = lax.axis_size(EXPERT_AXES)
    copies = expert_devices // ctx_count

    near_tokens = spread(tokens[0], SAME_CORE)
    far_tokens = lax.ppermute(near_tokens, "core", SWAP)
    near_tokens = near_tokens.reshape(seq // 2, model_width)
    far_tokens = far_tokens.reshape(seq // 2, model_width)
    whole_in = lax.all_gather(w_in, "x", axis=0)
    whole_out = lax.all_gather(w_out, "x", axis=0)

    chosen = routes[0].T
    expert_ids = jnp.arange(experts, dtype=jnp.int32)
    flat_expert = chosen.reshape(2 * tok_rows)
    member = flat_expert[:, None] == expert_ids[None, :]
    picks = jnp.arange(2 * tok_rows, dtype=jnp.int32)
    before = (picks[:, None] > picks[None, :]).astype(BF)
    counts = jnp.dot(before, member.astype(BF), preferred_element_type=F32)
    slot_rank = jnp.sum(jnp.where(member, counts, 0.0), axis=1).astype(jnp.int32)
    owner_index = flat_expert // local_experts
    slot_of = (flat_expert % local_experts) * capacity + slot_rank
    slot_ids = jnp.arange(expert_devices * device_slots, dtype=jnp.int32)
    slot_hot = (owner_index[:, None] == (slot_ids // (copies * device_slots))[None, :]) & (
        slot_of[:, None] == (slot_ids % device_slots)[None, :]
    )
    slot_table = slot_hot.astype(BF)
    token_table = slot_table[:tok_rows] + slot_table[tok_rows:]

    def to_experts(table, rows):
        slots = contract_rows(table, rows).astype(BF)
        arrived = exchange(slots.reshape(expert_devices, device_slots, rows.shape[1]), EXPERT_AXES)
        return arrived.reshape(expert_devices, local_experts, capacity, rows.shape[1])

    cot_rows = to_experts(token_table, cotangent[0])

    ctx_ids = jnp.arange(ctx_count, dtype=jnp.int32)
    my_core = lax.axis_index("core")
    near = (ctx_ids % 2) == my_core
    lies = 2 * (jnp.where(near, 0, ctx_count // 2) + ctx_ids // 2)
    block_ids = jnp.arange(blocks, dtype=jnp.int32)[:, None]
    place = jnp.sum(
        jnp.where(pair_order[None, :] == block_ids, lies[None, :], 0)
        + jnp.where(blocks - 1 - pair_order[None, :] == block_ids, lies[None, :] + 1, 0),
        axis=1,
        dtype=jnp.int32,
    )
    positions = jnp.sum(
        jnp.where(
            2 * (block_ids // 2) == lies[None, :],
            jnp.where(block_ids % 2 == 0, pair_order[None, :], blocks - 1 - pair_order[None, :]),
            0,
        ),
        axis=1,
        dtype=jnp.int32,
    )
    my_pair = jnp.sum(jnp.where(ctx_ids == lax.axis_index(CTX), pair_order, 0))
    reversed_table = jnp.pad(bucket_table[::-1], (0, window - half), constant_values=-1)
    diagonal_bucket = jnp.stack(
        [
            lax.dynamic_slice(reversed_table, (seq - half - block * half,), (window,))
            for block in (my_pair, blocks - 1 - my_pair)
        ]
    ).reshape(1, 2 * window)
    bucket_ids = jnp.arange(bucket_count, dtype=jnp.int32)
    bucket_hot = (diagonal_bucket == bucket_ids[:, None]).astype(F32)
    windows = lax.dot_general(rel_bias, bucket_hot, ROWS, precision=HIGHEST)
    windows = jnp.where(diagonal_bucket >= 0, windows, MASKED)
    windows = windows.reshape(head_pairs, 4, window)

    inputs = tokens[0].astype(F32)
    scale_one = norm_scale(inputs)
    normed_one = (inputs * scale_one * gain_attn).astype(BF)
    w_q = w_qkv[:, :model_width]
    queries = jnp.dot(normed_one, w_q, preferred_element_type=F32).astype(BF)
    all_normed, key_value = keys_and_values(
        place, near_tokens, far_tokens, gain_attn, w_qkv, half
    )
    attended, probabilities = attend(queries, key_value, windows)
    residual_one = inputs + jnp.dot(attended, w_attn_out, preferred_element_type=F32)
    scale_two = norm_scale(residual_one)
    normed_two = (residual_one * scale_two * gain_ffn).astype(BF)

    router_logits = jnp.dot(normed_two, w_router, preferred_element_type=F32)
    chosen_hot = (chosen[:, :, None] == expert_ids[None, None, :]).astype(F32)
    picked_logits = jnp.sum(chosen_hot * router_logits[None], axis=2)
    logit_peak = jnp.max(picked_logits, axis=0, keepdims=True)
    gate_exp = jnp.exp(picked_logits - logit_peak)
    gate_weights = (gate_exp / jnp.sum(gate_exp, axis=0, keepdims=True))[:, :, None]

    flat_gate = gate_weights.reshape(2 * tok_rows, 1)
    gate_high = flat_gate.astype(BF).astype(F32)
    lane_ids = jnp.arange(LANES, dtype=jnp.int32)[None, :]
    gate_lanes = jnp.where(lane_ids == 0, gate_high, 0.0)
    gate_lanes = jnp.where(lane_ids == 1, flat_gate - gate_high, gate_lanes).astype(BF)
    pick_rows = jnp.concatenate([normed_two, normed_two], axis=0)
    x_rows = to_experts(slot_table, jnp.concatenate([pick_rows, gate_lanes], axis=1))
    back, part_in, part_out = run_experts(x_rows, cot_rows, whole_in, whole_out)
    grad_w_in = lax.psum_scatter(part_in, "x", scatter_dimension=0).astype(F32)
    grad_w_out = lax.psum_scatter(part_out, "x", scatter_dimension=0).astype(F32)
    back = exchange(back.reshape(expert_devices, device_slots, 2 * model_width), EXPERT_AXES)
    back = back.reshape(expert_devices * device_slots, 2 * model_width)
    picked = jnp.dot(slot_table, back[:, :model_width], preferred_element_type=F32)
    picked = picked.reshape(2, tok_rows, model_width)
    expert_part = jnp.dot(token_table, back[:, model_width:], preferred_element_type=F32)
    mixture = jnp.sum(gate_weights * picked, axis=0)
    layer_out = (residual_one + mixture).astype(BF)[None]

    upstream = cotangent[0].astype(F32)
    gate_grad = jnp.sum(picked * upstream[None], axis=2, keepdims=True)
    inner_mean = jnp.sum(gate_weights * gate_grad, axis=0, keepdims=True)
    pick_grad = gate_weights * (gate_grad - inner_mean)
    logit_grad = jnp.sum(pick_grad * chosen_hot, axis=0)
    grad_w_router = lax.dot_general(normed_two.astype(F32), logit_grad, ROWS, precision=HIGHEST)
    router_back = lax.dot_general(logit_grad, w_router.astype(F32), COLS, precision=HIGHEST)
    normed_two_grad = expert_part + router_back
    norm_part, grad_gain_ffn = norm_backward(residual_one, scale_two, gain_ffn, normed_two_grad)
    mixed_grad = upstream + norm_part
    branch_grad = mixed_grad.astype(BF)
    grad_w_attn_out = contract_rows(attended, branch_grad)

    core = jnp.reshape(my_core, (1,)).astype(jnp.int32)
    side = model_width // 2
    chips = lax.axis_size(CHIPS)
    small = jnp.concatenate([grad_w_attn_out, grad_w_router.T, grad_gain_ffn[None]], axis=0)
    spare = -small.shape[0] % (16 * chips)
    small = jnp.pad(small, ((0, spare), (0, 0))).astype(BF)
    left, right = small[:, :side], small[:, side:]
    first = my_core == 0
    mine, other = sum_halves(jnp.where(first, left, right), jnp.where(first, right, left))
    left, right = jnp.where(first, mine, other), jnp.where(first, other, mine)
    small = jnp.concatenate([left, right], axis=1).astype(F32)
    sum_w_attn_out = small[:model_width]
    sum_w_router = small[model_width : model_width + experts].T
    sum_gain_ffn = small[model_width + experts]

    attended_grad = contract_cols(branch_grad, w_attn_out).astype(BF)
    query_grad, key_value_grad, diagonals = attend_back(
        probabilities, queries, key_value, attended_grad
    )
    diagonals = diagonals.reshape(head_count, 2 * window)
    grad_rel_bias = lax.dot_general(bucket_hot, diagonals, COLS, precision=HIGHEST)
    biases = bucket_count * head_count
    bias_row = jnp.pad(grad_rel_bias.reshape(1, biases), ((0, 0), (0, side - biases)))
    bias_row = jnp.concatenate([bias_row, bias_row], axis=1)
    extra = jnp.pad(bias_row, ((0, 2 * LANES - 1), (0, 0)))
    kept, given = weight_grads(core, query_grad, normed_one, key_value_grad, all_normed, extra)
    key_value_grad, kept, given = lax.optimization_barrier((key_value_grad, kept, given))
    mine, other = sum_halves(kept, given)
    sum_w_qkv, products = whole_grad(core, mine, other, w_qkv)
    sum_gain_attn = products[:, 0] / gain_attn
    sum_rel_bias = mine[3 * model_width, :biases].astype(F32).reshape(bucket_count, head_count)
    far_grad = normed_grads(positions[blocks // 2 :], key_value_grad, w_qkv, half)
    near_grad = normed_grads(positions[: blocks // 2], key_value_grad, w_qkv, half)
    near_grad = near_grad.astype(F32) + lax.ppermute(far_grad, "core", SWAP).astype(F32)
    near_grad = near_grad.astype(BF).reshape(ctx_count // 2, tok_rows, model_width)
    normed_one_grad = jnp.sum(exchange(near_grad, SAME_CORE).astype(F32), axis=0)
    normed_one_grad = normed_one_grad + contract_cols(query_grad, w_q)
    input_norm_grad, _ = norm_backward(inputs, scale_one, gain_attn, normed_one_grad)
    grad_tokens = (mixed_grad + input_norm_grad)[None]
    return (
        layer_out,
        grad_tokens,
        sum_gain_attn,
        sum_w_qkv,
        sum_rel_bias,
        sum_w_attn_out,
        sum_gain_ffn,
        sum_w_router,
        grad_w_in,
        grad_w_out,
    )


def solution(mesh):
    split_mesh = Mesh(mesh.devices.reshape(SPLIT), EVERY)
    in_specs = (
        P(WSH, CTX, None),
        P(),
        P(),
        P(),
        P(),
        P(),
        P(),
        P(CTX, None, WSH),
        P(CTX, WSH, None),
        P(WSH, CTX, None),
        P(),
        P(),
        P(WSH, CTX, None),
    )
    out_specs = (
        P(WSH, CTX, None),
        P(WSH, CTX, None),
        P(),
        P(),
        P(),
        P(),
        P(),
        P(),
        P(CTX, None, WSH),
        P(CTX, WSH, None),
    )
    return jax.shard_map(
        on_device, mesh=split_mesh, in_specs=in_specs, out_specs=out_specs, check_vma=False
    )
```

```python
import functools

import jax
import jax.numpy as jnp
from jax import lax
from jax.experimental import pallas as pl
from jax.experimental.pallas import tpu as pltpu
from jax.sharding import Mesh
from jax.sharding import PartitionSpec as P

BF = jnp.bfloat16
F32 = jnp.float32
EPSILON = 1e-06
HIGHEST = lax.Precision.HIGHEST
MASKED = -1e30
ROWS = (((0,), (0,)), ((), ()))
COLS = (((1,), (1,)), ((), ()))
LANES = 128
VMEM_LIMIT = 58 * 1024 * 1024
SPLIT = (2, 4, 2, 2, 4)
EVERY = ("ya", "z", "core", "yb", "x")
CTX = ("ya", "z", "core")
WSH = ("yb", "x")
SAME_CORE = ("ya", "z")
CHIPS = ("ya", "z", "yb", "x")
EXPERT_AXES = ("ya", "z", "core", "yb")
SWAP = ((0, 1), (1, 0))


def norm_scale(values):
    return lax.rsqrt(jnp.mean(values * values, axis=-1, keepdims=True) + EPSILON)


def norm_backward(values, scale_vector, gain_vector, upstream):
    weighted = upstream * gain_vector
    inner_mean = jnp.mean(weighted * values, axis=-1, keepdims=True)
    grad_input = (
        scale_vector * weighted - values * scale_vector * scale_vector * scale_vector * inner_mean
    )
    grad_gain = jnp.sum(upstream * values * scale_vector, axis=0)
    return (grad_input, grad_gain)


def contract_rows(left_matrix, right_matrix):
    return lax.dot_general(left_matrix, right_matrix, ROWS, preferred_element_type=F32)


def contract_cols(left_matrix, right_matrix):
    return lax.dot_general(left_matrix, right_matrix, COLS, preferred_element_type=F32)


def exchange(array, axes):
    return lax.all_to_all(array, axes, split_axis=0, concat_axis=0, tiled=True)


def spread(array, axes):
    return exchange(jnp.broadcast_to(array[None], (lax.axis_size(axes), *array.shape)), axes)


def half_share(kept, given):
    rows, columns = kept.shape
    chips = lax.axis_size(CHIPS)
    got = lax.ppermute(given, "core", SWAP)
    half = (kept.astype(F32) + got.astype(F32)).astype(BF).reshape(chips, rows // chips, columns)
    return jnp.sum(exchange(half, CHIPS).astype(F32), axis=0).astype(BF)


def shear(tiles):
    count, rows, columns = tiles.shape
    while rows > 8:
        half = rows // 2
        moved = pltpu.roll(tiles[:, :half].reshape(count * half, columns), half, axis=1)
        tiles = moved.reshape(count, half, columns) + tiles[:, half:]
        rows = half
    flat = tiles.reshape(count * rows, columns)
    row_ids = lax.broadcasted_iota(jnp.int32, flat.shape, 0)
    step = rows // 2
    while step:
        flat = jnp.where(row_ids // step % 2 == 0, pltpu.roll(flat, step, axis=1), flat)
        step //= 2
    return jnp.sum(flat.reshape(count, rows, columns), axis=1)


def split_heads(array, factor):
    lanes = lax.broadcasted_iota(jnp.int32, array.shape, 1) // (LANES // 2)
    wide = array.astype(F32) * factor
    parts = [jnp.where(lanes == head, wide, 0.0).astype(BF) for head in range(2)]
    return jnp.concatenate(parts, axis=0)


def join_heads(array):
    rows = array.shape[0] // 2
    lanes = lax.broadcasted_iota(jnp.int32, (rows, LANES), 1) // (LANES // 2)
    return jnp.where(lanes == 0, array[:rows], array[rows:]).astype(BF)


def attend_kernel(q_ref, kv_ref, window_ref, out_ref, prob_ref):
    half, seq = q_ref.shape[0] // 2, kv_ref.shape[1]
    window = seq + 2 * half
    q = split_heads(q_ref[...], (LANES // 2) ** -0.5)
    raw = contract_cols(q, kv_ref[0])
    tiles = jnp.broadcast_to(window_ref[...][:, None], (4, half, window))
    tiles = [
        pltpu.roll(tiles[part], window - half + 1, axis=1, stride=1, stride_axis=0)[:, :seq]
        for part in range(4)
    ]
    scores = raw + jnp.concatenate(tiles, axis=0)
    exps = jnp.exp(scores - jnp.max(scores, axis=1, keepdims=True))
    prob = (exps * (1.0 / jnp.sum(exps, axis=1, keepdims=True))).astype(BF)
    prob_ref[...] = prob.reshape(prob_ref.shape)
    out_ref[...] = join_heads(jnp.dot(prob, kv_ref[1], preferred_element_type=F32))


def attend(queries, key_value, windows):
    rows, width = queries.shape
    pairs, seq = key_value.shape[1:3]
    work = rows * seq * width
    return pl.pallas_call(
        attend_kernel,
        grid=(pairs,),
        in_specs=[
            pl.BlockSpec((rows, LANES), lambda h: (0, h)),
            pl.BlockSpec((2, None, seq, LANES), lambda h: (0, h, 0, 0)),
            pl.BlockSpec((None, 4, windows.shape[2]), lambda h: (h, 0, 0)),
        ],
        out_specs=[
            pl.BlockSpec((rows, LANES), lambda h: (0, h)),
            pl.BlockSpec((2, rows, seq), lambda h: (h, 0, 0)),
        ],
        out_shape=[
            jax.ShapeDtypeStruct((rows, width), BF),
            jax.ShapeDtypeStruct((2 * pairs, rows, seq), BF),
        ],
        compiler_params=pltpu.CompilerParams(vmem_limit_bytes=VMEM_LIMIT),
        cost_estimate=pl.CostEstimate(
            flops=8 * work,
            bytes_accessed=4 * seq * width + 4 * pairs * rows * seq,
            transcendentals=2 * pairs * rows * seq,
        ),
        name="attend",
    )(queries, key_value, windows)


def attend_back_kernel(prob_ref, q_ref, kv_ref, grad_ref, dq_ref, dkv_ref, diag_ref):
    half, seq = q_ref.shape[0] // 2, kv_ref.shape[1]
    factor = (LANES // 2) ** -0.5
    rows = 4 * half
    q = split_heads(q_ref[...], factor)
    grad = split_heads(grad_ref[...], 1.0)
    prob = prob_ref[...].reshape(rows, seq)
    wide = prob.astype(F32)
    prob_grad = contract_cols(grad, kv_ref[1])
    inner = jnp.sum(wide * prob_grad, axis=1, keepdims=True)
    score_grad = wide * (prob_grad - inner)
    tiles = jnp.concatenate([score_grad, jnp.zeros((rows, 2 * half), F32)], axis=1)
    diag_ref[...] = shear(tiles.reshape(4, half, seq + 2 * half))
    score_grad = score_grad.astype(BF)
    query_grad = jnp.dot(score_grad, kv_ref[0], preferred_element_type=F32) * factor
    dq_ref[...] = join_heads(query_grad)
    dkv_ref[0] = contract_rows(q, score_grad).T.astype(BF)
    dkv_ref[1] = contract_rows(grad, prob).T.astype(BF)


def attend_back(prob, queries, key_value, attended_grad):
    rows, width = queries.shape
    pairs, seq = key_value.shape[1:3]
    window = seq + rows
    row_spec = pl.BlockSpec((rows, LANES), lambda h: (0, h))
    kv_spec = pl.BlockSpec((2, None, seq, LANES), lambda h: (0, h, 0, 0))
    return pl.pallas_call(
        attend_back_kernel,
        grid=(pairs,),
        in_specs=[
            pl.BlockSpec((2, rows, seq), lambda h: (h, 0, 0)),
            row_spec,
            kv_spec,
            row_spec,
        ],
        out_specs=[
            row_spec,
            kv_spec,
            pl.BlockSpec((None, 4, window), lambda h: (h, 0, 0)),
        ],
        out_shape=[
            jax.ShapeDtypeStruct((rows, width), BF),
            jax.ShapeDtypeStruct(key_value.shape, BF),
            jax.ShapeDtypeStruct((pairs, 4, window), F32),
        ],
        compiler_params=pltpu.CompilerParams(vmem_limit_bytes=VMEM_LIMIT),
        cost_estimate=pl.CostEstimate(
            flops=16 * rows * seq * width,
            bytes_accessed=8 * seq * width + 4 * pairs * rows * seq,
            transcendentals=0,
        ),
        name="attend_back",
    )(prob, queries, key_value, attended_grad)


def key_value_kernel(place_ref, near_ref, far_ref, gain_ref, wk_ref, wv_ref, normed_ref, kv_ref, *, half):
    tile = normed_ref.shape[0] // half
    near_blocks = near_ref.shape[0] // half
    rows = []
    for block in range(tile):
        source = place_ref[pl.program_id(0) * tile + block]
        at = pl.ds(pl.multiple_of(lax.rem(source, near_blocks) * half, half), half)
        rows.append(jnp.where(source < near_blocks, near_ref[at].astype(F32), far_ref[at].astype(F32)))
    inputs = jnp.concatenate(rows, axis=0)
    normed = (inputs * norm_scale(inputs) * gain_ref[...]).astype(BF)
    normed_ref[...] = normed
    for part, weight_ref in enumerate((wk_ref, wv_ref)):
        out = jnp.dot(normed, weight_ref[...], preferred_element_type=F32).astype(BF)
        for pair in range(kv_ref.shape[1]):
            kv_ref[part, pair] = out[:, pair * LANES : (pair + 1) * LANES]


def keys_and_values(place, near, far, gain, w_qkv, half):
    near_rows, width = near.shape
    seq = 2 * near_rows
    tile = 8 * half
    return pl.pallas_call(
        functools.partial(key_value_kernel, half=half),
        grid_spec=pltpu.PrefetchScalarGridSpec(
            num_scalar_prefetch=1,
            grid=(seq // tile,),
            in_specs=[
                pl.BlockSpec((near_rows, width), lambda r, p: (0, 0)),
                pl.BlockSpec((near_rows, width), lambda r, p: (0, 0)),
                pl.BlockSpec((1, width), lambda r, p: (0, 0)),
                pl.BlockSpec((width, width), lambda r, p: (0, 1)),
                pl.BlockSpec((width, width), lambda r, p: (0, 2)),
            ],
            out_specs=[
                pl.BlockSpec((tile, width), lambda r, p: (r, 0)),
                pl.BlockSpec((2, width // LANES, tile, LANES), lambda r, p: (0, 0, r, 0)),
            ],
        ),
        out_shape=[
            jax.ShapeDtypeStruct((seq, width), BF),
            jax.ShapeDtypeStruct((2, width // LANES, seq, LANES), BF),
        ],
        compiler_params=pltpu.CompilerParams(vmem_limit_bytes=VMEM_LIMIT),
        cost_estimate=pl.CostEstimate(
            flops=4 * seq * width * width, bytes_accessed=8 * seq * width, transcendentals=seq
        ),
        name="keys_and_values",
    )(place, near, far, gain[None], w_qkv, w_qkv)


def normed_grad_kernel(position_ref, dkv_ref, wk_ref, wv_ref, out_ref, *, half):
    tile = out_ref.shape[0] // half
    out = 0.0
    for part, weight_ref in enumerate((wk_ref, wv_ref)):
        rows = []
        for block in range(tile):
            source = position_ref[pl.program_id(0) * tile + block]
            at = pl.ds(pl.multiple_of(source * half, half), half)
            pairs = [dkv_ref[part, pair, at] for pair in range(dkv_ref.shape[1])]
            rows.append(jnp.concatenate(pairs, axis=1))
        out += contract_cols(jnp.concatenate(rows, axis=0), weight_ref[...])
    out_ref[...] = out.astype(BF)


def normed_grads(position, key_value_grad, w_qkv, half):
    width = w_qkv.shape[0]
    rows = position.shape[0] * half
    tile = 8 * half
    return pl.pallas_call(
        functools.partial(normed_grad_kernel, half=half),
        grid_spec=pltpu.PrefetchScalarGridSpec(
            num_scalar_prefetch=1,
            grid=(rows // tile,),
            in_specs=[
                pl.BlockSpec(key_value_grad.shape, lambda r, p: (0, 0, 0, 0)),
                pl.BlockSpec((width, width), lambda r, p: (0, 1)),
                pl.BlockSpec((width, width), lambda r, p: (0, 2)),
            ],
            out_specs=pl.BlockSpec((tile, width), lambda r, p: (r, 0)),
        ),
        out_shape=jax.ShapeDtypeStruct((rows, width), BF),
        compiler_params=pltpu.CompilerParams(vmem_limit_bytes=VMEM_LIMIT),
        cost_estimate=pl.CostEstimate(
            flops=4 * rows * width * width, bytes_accessed=8 * rows * width, transcendentals=0
        ),
        name="normed_grads",
    )(position, key_value_grad, w_qkv, w_qkv)


def weight_grad_kernel(
    core_ref,
    dq_ref,
    normed_ref,
    dkv_ref,
    all_normed_ref,
    attended_ref,
    branch_ref,
    extra_ref,
    kept_ref,
    given_ref,
):
    step = pl.program_id(0)
    side = kept_ref.shape[1]

    def give(total):
        left, right = total[:, :side].astype(BF), total[:, side:].astype(BF)
        rows = total.shape[0]

        @pl.when(core_ref[0] == 0)
        def _():
            kept_ref[:rows] = left
            given_ref[:rows] = right

        @pl.when(core_ref[0] != 0)
        def _():
            kept_ref[:rows] = right
            given_ref[:rows] = left

    @pl.when(step == 0)
    def _():
        give(contract_rows(dq_ref[...], normed_ref[...]))

    @pl.when((step == 1) | (step == 2))
    def _():
        pairs = [dkv_ref[pair] for pair in range(dkv_ref.shape[0])]
        give(contract_rows(jnp.concatenate(pairs, axis=1), all_normed_ref[...]))

    @pl.when(step == 3)
    def _():
        give(contract_rows(attended_ref[...], branch_ref[...]))

    @pl.when(step == 4)
    def _():
        give(extra_ref[...])


def weight_grads(
    core, query_grad, normed_one, key_value_grad, all_normed, attended, branch_grad, extra
):
    rows, width = normed_one.shape
    seq = all_normed.shape[0]
    total = 4 * width + extra.shape[0]
    row_spec = pl.BlockSpec((rows, width), lambda t, p: (0, 0))
    out_spec = pl.BlockSpec((width, width // 2), lambda t, p: (t, 0))
    out_shape = jax.ShapeDtypeStruct((total, width // 2), BF)
    return pl.pallas_call(
        weight_grad_kernel,
        grid_spec=pltpu.PrefetchScalarGridSpec(
            num_scalar_prefetch=1,
            grid=(5,),
            in_specs=[
                row_spec,
                row_spec,
                pl.BlockSpec(
                    (None, width // LANES, seq, LANES), lambda t, p: (jnp.clip(t - 1, 0, 1), 0, 0, 0)
                ),
                pl.BlockSpec((seq, width), lambda t, p: (0, 0)),
                row_spec,
                row_spec,
                pl.BlockSpec(extra.shape, lambda t, p: (0, 0)),
            ],
            out_specs=[out_spec, out_spec],
        ),
        out_shape=[out_shape, out_shape],
        compiler_params=pltpu.CompilerParams(vmem_limit_bytes=VMEM_LIMIT),
        cost_estimate=pl.CostEstimate(
            flops=4 * seq * width * width, bytes_accessed=10 * seq * width, transcendentals=0
        ),
        name="weight_grads",
    )(core, query_grad, normed_one, key_value_grad, all_normed, attended, branch_grad, extra)


def whole_grad_kernel(core_ref, mine_ref, other_ref, weight_ref, grad_ref, product_ref, out_ref):
    step = pl.program_id(0)
    last = pl.num_programs(0) - out_ref.shape[0] // mine_ref.shape[0]
    side, tile = mine_ref.shape[1], mine_ref.shape[0]
    width = 2 * side
    mine_at = pl.ds(pl.multiple_of(core_ref[0] * side, side), side)
    other_at = pl.ds(pl.multiple_of(side - core_ref[0] * side, side), side)

    @pl.when(step < last)
    def _():
        grad_ref[mine_at, :] = mine_ref[...].astype(F32).T
        grad_ref[other_at, :] = other_ref[...].astype(F32).T
        product = jnp.sum(grad_ref[...] * weight_ref[...].astype(F32), axis=1, keepdims=True)
        product = jnp.broadcast_to(product, (width, LANES))

        @pl.when(step == 0)
        def _():
            product_ref[...] = product

        @pl.when(step > 0)
        def _():
            product_ref[...] += product

    @pl.when(step >= last)
    def _():
        at = pl.ds(pl.multiple_of((step - last) * tile, tile), tile)

        @pl.when(core_ref[0] == 0)
        def _():
            out_ref[at, :side] = mine_ref[...].astype(F32)
            out_ref[at, side:] = other_ref[...].astype(F32)

        @pl.when(core_ref[0] != 0)
        def _():
            out_ref[at, :side] = other_ref[...].astype(F32)
            out_ref[at, side:] = mine_ref[...].astype(F32)


def whole_grad(core, mine, other, weight):
    width, columns = weight.shape
    side = mine.shape[1]
    tile = width
    count = columns // tile
    half_spec = pl.BlockSpec((tile, side), lambda t, p: (t, 0))
    whole_spec = pl.BlockSpec((width, tile), lambda t, p: (0, jnp.minimum(t, count - 1)))
    return pl.pallas_call(
        whole_grad_kernel,
        grid_spec=pltpu.PrefetchScalarGridSpec(
            num_scalar_prefetch=1,
            grid=(count + width // tile,),
            in_specs=[half_spec, half_spec, whole_spec],
            out_specs=[
                whole_spec,
                pl.BlockSpec((width, LANES), lambda t, p: (0, 0)),
                pl.BlockSpec((width, width), lambda t, p: (0, 0)),
            ],
        ),
        out_shape=[
            jax.ShapeDtypeStruct((width, columns), F32),
            jax.ShapeDtypeStruct((width, LANES), F32),
            jax.ShapeDtypeStruct((width, width), F32),
        ],
        compiler_params=pltpu.CompilerParams(vmem_limit_bytes=VMEM_LIMIT),
        cost_estimate=pl.CostEstimate(
            flops=2 * width * columns, bytes_accessed=8 * width * columns, transcendentals=0
        ),
        name="whole_grad",
    )(core, mine, other, weight)


def expert_rows(x_ref, cot_ref):
    width = cot_ref.shape[-1]
    rows = x_ref.shape[0] * x_ref.shape[1]
    rows_in = x_ref[...].reshape(rows, x_ref.shape[2])
    gate = jnp.sum(rows_in[:, width:].astype(F32), axis=1, keepdims=True)
    slot_grad = (cot_ref[...].reshape(rows, width).astype(F32) * gate).astype(BF)
    return rows_in[:, :width], slot_grad


def high_and_low(column):
    high = column.astype(BF).astype(F32)
    lanes = lax.broadcasted_iota(jnp.int32, (column.shape[0], LANES), 1)
    wide = jnp.where(lanes == 0, high, jnp.where(lanes == 1, column - high, 0.0))
    return wide.astype(BF)


def write_weight_grads(x, slot_grad, activated, pre_grad, grad_ref):
    grad_in = contract_rows(pre_grad, x).astype(BF)
    grad_out = contract_rows(activated, slot_grad).astype(BF)
    slices, hidden = grad_ref.shape[0], grad_ref.shape[1] // 2
    for index in range(slices):
        grad_ref[index, :hidden] = grad_in[index * hidden : (index + 1) * hidden]
        grad_ref[index, hidden:] = grad_out[index * hidden : (index + 1) * hidden]


def expert_kernel(
    x_ref,
    cot_ref,
    weight_ref,
    dx_ref,
    ret_ref,
    first_grad_ref,
    act_ref,
    pre_grad_ref,
    ret_sum,
    dx_sum,
):
    part = pl.program_id(1)
    width = cot_ref.shape[-1]
    x, slot_grad = expert_rows(x_ref, cot_ref)
    slices, hidden = weight_ref.shape[0], weight_ref.shape[1] // 2
    weights = [weight_ref[index] for index in range(slices)]
    weight_in = jnp.concatenate([weight[:hidden] for weight in weights], axis=0)
    weight_out = jnp.concatenate([weight[hidden:] for weight in weights], axis=0)
    pre = contract_cols(x, weight_in)
    act_grad = contract_cols(slot_grad, weight_out)
    cumulative = 0.5 * (1.0 + lax.erf(pre * 0.7071067811865476))
    activated = (pre * cumulative).astype(BF)
    slope = cumulative + pre * (jnp.exp(-0.5 * pre * pre) * 0.3989422804014327)
    pre_grad = (act_grad * slope).astype(BF)
    returned = jnp.dot(activated, weight_out, preferred_element_type=F32)
    input_grad = jnp.dot(pre_grad, weight_in, preferred_element_type=F32)

    @pl.when(pl.program_id(0) == 0)
    def _():
        write_weight_grads(x, slot_grad, activated, pre_grad, first_grad_ref)

    @pl.when(pl.program_id(0) > 0)
    def _():
        act_ref[...] = activated
        pre_grad_ref[...] = pre_grad

    @pl.when(part == 0)
    def _():
        ret_sum[...] = returned
        dx_sum[...] = input_grad

    @pl.when(part > 0)
    def _():
        ret_sum[...] += returned
        dx_sum[...] += input_grad

    @pl.when(part == pl.num_programs(1) - 1)
    def _():
        shape = cot_ref.shape
        rows = shape[0] * shape[1]
        ret = ret_sum[...]
        ret_ref[...] = ret.astype(BF).reshape(shape)
        upstream = cot_ref[...].reshape(rows, width).astype(F32)
        gate_grad = high_and_low(jnp.sum(ret * upstream, axis=1, keepdims=True))
        dx_ref[:, :, :width] = dx_sum[...].astype(BF).reshape(shape)
        dx_ref[:, :, width:] = gate_grad.reshape(shape[0], shape[1], LANES)


def expert_grad_kernel(x_ref, cot_ref, act_ref, pre_grad_ref, grad_ref):
    x, slot_grad = expert_rows(x_ref, cot_ref)
    write_weight_grads(x, slot_grad, act_ref[...], pre_grad_ref[...], grad_ref)


def run_experts(x_rows, cot_rows, weights):
    devices, experts, slots, width = cot_rows.shape
    wide = x_rows.shape[3]
    parts, _, both, _ = weights.shape
    hidden = both // 2
    rows = devices * slots
    slices = 2
    steps = parts // slices

    def row_spec(columns):
        return pl.BlockSpec((devices, None, slots, columns), lambda e, w: (0, e, 0, 0))

    later = experts - 1
    hidden_spec = pl.BlockSpec(
        (None, rows, slices * hidden),
        lambda e, w: (jnp.maximum(e - 1, 0), 0, jnp.where(e == 0, 0, w)),
    )
    hidden_shape = jax.ShapeDtypeStruct((later, rows, parts * hidden), BF)
    grad_shape = jax.ShapeDtypeStruct((parts, both, width), BF)
    work = experts * rows * width * parts * hidden
    params = pltpu.CompilerParams(vmem_limit_bytes=VMEM_LIMIT)
    input_grad, returned, first_grad, activated, pre_grad = pl.pallas_call(
        expert_kernel,
        grid=(experts, steps),
        in_specs=[
            row_spec(wide),
            row_spec(width),
            pl.BlockSpec((slices, None, both, width), lambda e, w: (w, e, 0, 0)),
        ],
        out_specs=[
            row_spec(width + LANES),
            row_spec(width),
            pl.BlockSpec(
                (slices, both, width), lambda e, w: (jnp.where(e == 0, w, steps - 1), 0, 0)
            ),
            hidden_spec,
            hidden_spec,
        ],
        out_shape=[
            jax.ShapeDtypeStruct((devices, experts, slots, width + LANES), BF),
            jax.ShapeDtypeStruct((devices, experts, slots, width), BF),
            grad_shape,
            hidden_shape,
            hidden_shape,
        ],
        scratch_shapes=[pltpu.VMEM((rows, width), F32), pltpu.VMEM((rows, width), F32)],
        compiler_params=params,
        cost_estimate=pl.CostEstimate(
            flops=10 * work,
            bytes_accessed=8 * experts * rows * width + 4 * parts * experts * width * hidden,
            transcendentals=2 * experts * rows * parts * hidden,
        ),
        name="experts",
    )(x_rows, cot_rows, weights)
    weight_grads_of = [first_grad]
    for expert in range(1, experts):

        def own_rows(columns, expert=expert):
            return pl.BlockSpec((devices, None, slots, columns), lambda w: (0, expert, 0, 0))

        own_hidden = pl.BlockSpec(
            (None, rows, slices * hidden), lambda w, expert=expert: (expert - 1, 0, w)
        )
        weight_grads_of.append(
            pl.pallas_call(
                expert_grad_kernel,
                grid=(steps,),
                in_specs=[own_rows(wide), own_rows(width), own_hidden, own_hidden],
                out_specs=pl.BlockSpec((slices, both, width), lambda w: (w, 0, 0)),
                out_shape=grad_shape,
                compiler_params=params,
                cost_estimate=pl.CostEstimate(
                    flops=4 * work // experts,
                    bytes_accessed=8 * rows * width + 4 * parts * width * hidden,
                    transcendentals=0,
                ),
                name="expert_grads",
            )(x_rows, cot_rows, activated, pre_grad)
        )
    return input_grad, returned, weight_grads_of


def on_device(
    tokens,
    gain_attn,
    w_qkv,
    rel_bias,
    w_attn_out,
    gain_ffn,
    w_router,
    w_in,
    w_out,
    routes,
    pair_order,
    bucket_table,
    cotangent,
):
    tok_rows = tokens.shape[1]
    model_width = tokens.shape[2]
    head_count = rel_bias.shape[1]
    bucket_count = rel_bias.shape[0]
    ctx_count = lax.axis_size(CTX)
    half = tok_rows // 2
    blocks = 2 * ctx_count
    seq = half * blocks
    window = seq + 2 * half
    head_pairs = head_count // 2
    local_experts = w_in.shape[0]
    experts = w_router.shape[1]
    capacity = 4 * tok_rows // experts
    device_slots = local_experts * capacity
    expert_devices = lax.axis_size(EXPERT_AXES)
    copies = expert_devices // ctx_count

    near_tokens = spread(tokens[0], SAME_CORE)
    far_tokens = lax.ppermute(near_tokens, "core", SWAP)
    near_tokens = near_tokens.reshape(seq // 2, model_width)
    far_tokens = far_tokens.reshape(seq // 2, model_width)
    weights = jnp.concatenate([w_in.transpose(0, 2, 1), w_out], axis=1)
    weights = lax.all_gather(weights, "x", axis=0)

    chosen = routes[0].T
    expert_ids = jnp.arange(experts, dtype=jnp.int32)
    flat_expert = chosen.reshape(2 * tok_rows)
    member = flat_expert[:, None] == expert_ids[None, :]
    picks = jnp.arange(2 * tok_rows, dtype=jnp.int32)
    before = (picks[:, None] > picks[None, :]).astype(BF)
    counts = jnp.dot(before, member.astype(BF), preferred_element_type=F32)
    slot_rank = jnp.sum(jnp.where(member, counts, 0.0), axis=1).astype(jnp.int32)
    owner_index = flat_expert // local_experts
    slot_of = (flat_expert % local_experts) * capacity + slot_rank
    slot_ids = jnp.arange(expert_devices * device_slots, dtype=jnp.int32)
    slot_hot = (owner_index[:, None] == (slot_ids // (copies * device_slots))[None, :]) & (
        slot_of[:, None] == (slot_ids % device_slots)[None, :]
    )
    slot_table = slot_hot.astype(BF)
    token_table = slot_table[:tok_rows] + slot_table[tok_rows:]

    def to_experts(table, rows):
        slots = contract_rows(table, rows).astype(BF)
        arrived = exchange(slots.reshape(expert_devices, device_slots, rows.shape[1]), EXPERT_AXES)
        return arrived.reshape(expert_devices, local_experts, capacity, rows.shape[1])

    cot_rows = to_experts(token_table, cotangent[0])

    ctx_ids = jnp.arange(ctx_count, dtype=jnp.int32)
    my_core = lax.axis_index("core")
    near = (ctx_ids % 2) == my_core
    lies = 2 * (jnp.where(near, 0, ctx_count // 2) + ctx_ids // 2)
    block_ids = jnp.arange(blocks, dtype=jnp.int32)[:, None]
    place = jnp.sum(
        jnp.where(pair_order[None, :] == block_ids, lies[None, :], 0)
        + jnp.where(blocks - 1 - pair_order[None, :] == block_ids, lies[None, :] + 1, 0),
        axis=1,
        dtype=jnp.int32,
    )
    positions = jnp.sum(
        jnp.where(
            2 * (block_ids // 2) == lies[None, :],
            jnp.where(block_ids % 2 == 0, pair_order[None, :], blocks - 1 - pair_order[None, :]),
            0,
        ),
        axis=1,
        dtype=jnp.int32,
    )
    my_pair = jnp.sum(jnp.where(ctx_ids == lax.axis_index(CTX), pair_order, 0))
    reversed_table = jnp.pad(bucket_table[::-1], (0, window - half), constant_values=-1)
    diagonal_bucket = jnp.stack(
        [
            lax.dynamic_slice(reversed_table, (seq - half - block * half,), (window,))
            for block in (my_pair, blocks - 1 - my_pair)
        ]
    ).reshape(1, 2 * window)
    bucket_ids = jnp.arange(bucket_count, dtype=jnp.int32)
    bucket_hot = (diagonal_bucket == bucket_ids[:, None]).astype(F32)
    windows = lax.dot_general(rel_bias, bucket_hot, ROWS, precision=HIGHEST)
    windows = jnp.where(diagonal_bucket >= 0, windows, MASKED)
    windows = windows.reshape(head_pairs, 4, window)

    inputs = tokens[0].astype(F32)
    scale_one = norm_scale(inputs)
    normed_one = (inputs * scale_one * gain_attn).astype(BF)
    w_q = w_qkv[:, :model_width]
    queries = jnp.dot(normed_one, w_q, preferred_element_type=F32).astype(BF)
    all_normed, key_value = keys_and_values(
        place, near_tokens, far_tokens, gain_attn, w_qkv, half
    )
    attended, probabilities = attend(queries, key_value, windows)
    residual_one = inputs + jnp.dot(attended, w_attn_out, preferred_element_type=F32)
    scale_two = norm_scale(residual_one)
    normed_two = (residual_one * scale_two * gain_ffn).astype(BF)

    router_logits = jnp.dot(normed_two, w_router, preferred_element_type=F32)
    chosen_hot = (chosen[:, :, None] == expert_ids[None, None, :]).astype(F32)
    picked_logits = jnp.sum(chosen_hot * router_logits[None], axis=2)
    logit_peak = jnp.max(picked_logits, axis=0, keepdims=True)
    gate_exp = jnp.exp(picked_logits - logit_peak)
    gate_weights = (gate_exp / jnp.sum(gate_exp, axis=0, keepdims=True))[:, :, None]

    flat_gate = gate_weights.reshape(2 * tok_rows, 1)
    gate_lanes = high_and_low(flat_gate)
    pick_rows = jnp.concatenate([normed_two, normed_two], axis=0)
    x_rows = to_experts(slot_table, jnp.concatenate([pick_rows, gate_lanes], axis=1))
    input_grad, returned, parts = run_experts(x_rows, cot_rows, weights)

    def from_experts(rows):
        rows = exchange(rows.reshape(expert_devices, device_slots, rows.shape[3]), EXPERT_AXES)
        return rows.reshape(expert_devices * device_slots, rows.shape[2])

    input_grad = from_experts(input_grad)
    later_parts, input_grad, returned = lax.optimization_barrier(
        (parts[1:], input_grad, returned)
    )
    shares = [
        lax.psum_scatter(part, "x", scatter_dimension=0) for part in (parts[0], *later_parts)
    ]
    expert_part = jnp.dot(
        token_table, input_grad[:, :model_width], preferred_element_type=F32
    )
    gate_grad = jnp.dot(slot_table, input_grad[:, model_width:], preferred_element_type=F32)
    gate_grad = jnp.sum(gate_grad.reshape(2, tok_rows, LANES), axis=2, keepdims=True)
    returned = from_experts(returned)

    upstream = cotangent[0].astype(F32)
    inner_mean = jnp.sum(gate_weights * gate_grad, axis=0, keepdims=True)
    pick_grad = gate_weights * (gate_grad - inner_mean)
    logit_grad = jnp.sum(pick_grad * chosen_hot, axis=0)
    grad_w_router = lax.dot_general(normed_two.astype(F32), logit_grad, ROWS, precision=HIGHEST)
    router_back = lax.dot_general(logit_grad, w_router.astype(F32), COLS, precision=HIGHEST)
    normed_two_grad = expert_part + router_back
    norm_part, grad_gain_ffn = norm_backward(residual_one, scale_two, gain_ffn, normed_two_grad)
    mixed_grad = upstream + norm_part
    branch_grad = mixed_grad.astype(BF)

    attended_grad = contract_cols(branch_grad, w_attn_out).astype(BF)
    query_grad, key_value_grad, diagonals = attend_back(
        probabilities, queries, key_value, attended_grad
    )
    query_grad, returned = lax.optimization_barrier((query_grad, returned))
    diagonals = diagonals.reshape(head_count, 2 * window)
    grad_rel_bias = lax.dot_general(bucket_hot, diagonals, COLS, precision=HIGHEST)

    core = jnp.reshape(my_core, (1,)).astype(jnp.int32)
    side = model_width // 2
    biases = bucket_count * head_count
    bias_row = jnp.pad(grad_rel_bias.reshape(1, biases), ((0, 0), (0, model_width - biases)))
    extra = jnp.concatenate([grad_w_router.T, grad_gain_ffn[None], bias_row], axis=0)
    spare = -(4 * model_width + extra.shape[0]) % (8 * lax.axis_size(CHIPS))
    extra = jnp.pad(extra, ((0, spare), (0, 0)))
    kept, given = weight_grads(
        core,
        query_grad,
        normed_one,
        key_value_grad,
        all_normed,
        attended,
        branch_grad,
        extra,
    )
    key_value_grad, kept, given, returned = lax.optimization_barrier(
        (key_value_grad, kept, given, returned)
    )
    picked = jnp.dot(slot_table, returned, preferred_element_type=F32)
    mixture = jnp.sum(gate_weights * picked.reshape(2, tok_rows, model_width), axis=0)
    layer_out = (residual_one + mixture).astype(BF)[None]
    share = half_share(kept, given)

    far_grad = normed_grads(positions[blocks // 2 :], key_value_grad, w_qkv, half)
    near_grad = normed_grads(positions[: blocks // 2], key_value_grad, w_qkv, half)
    near_grad = near_grad.astype(F32) + lax.ppermute(far_grad, "core", SWAP).astype(F32)
    near_grad = near_grad.astype(BF).reshape(2, ctx_count // 4, tok_rows, model_width)
    share, near_grad, layer_out, shares = lax.optimization_barrier(
        (share, near_grad, layer_out, shares)
    )
    my_ya, my_z = lax.axis_index("ya"), lax.axis_index("z")
    ring = lax.axis_size("z")
    along_z = 0.0
    for hop in range(ring):
        rows = lax.dynamic_index_in_dim(near_grad, (my_z + hop) % ring, axis=1, keepdims=False)
        if hop:
            rows = lax.ppermute(rows, "z", [(at, (at + hop) % ring) for at in range(ring)])
        along_z = along_z + rows.astype(F32)
    given = jnp.where(my_ya == 0, along_z[1], along_z[0]).astype(BF)
    kept = jnp.where(my_ya == 0, along_z[0], along_z[1])
    mine = spread(share, CHIPS).reshape(-1, side)
    hidden = w_in.shape[2]
    shares = jnp.stack(shares)
    grad_w_in = shares[:, :hidden].transpose(0, 2, 1).astype(F32)
    grad_w_out = shares[:, hidden:].astype(F32)
    mine, given, grad_w_in, grad_w_out = lax.optimization_barrier(
        (mine, given, grad_w_in, grad_w_out)
    )
    other = lax.ppermute(mine, "core", SWAP)
    normed_one_grad = kept + lax.ppermute(given, "ya", SWAP).astype(F32)
    normed_one_grad = normed_one_grad + contract_cols(query_grad, w_q)
    input_norm_grad, _ = norm_backward(inputs, scale_one, gain_attn, normed_one_grad)
    grad_tokens = (mixed_grad + input_norm_grad)[None]
    sum_w_qkv, products, sum_w_attn_out = whole_grad(core, mine, other, w_qkv)
    sum_gain_attn = products[:, 0] / gain_attn
    small = slice(4 * model_width, 4 * model_width + experts + 2)
    left = jnp.where(my_core == 0, mine[small], other[small])
    right = jnp.where(my_core == 0, other[small], mine[small])
    sums = jnp.concatenate([left, right], axis=1).astype(F32)
    sum_w_router, sum_gain_ffn = sums[:experts].T, sums[experts]
    sum_rel_bias = sums[experts + 1, :biases].reshape(bucket_count, head_count)
    return (
        layer_out,
        grad_tokens,
        sum_gain_attn,
        sum_w_qkv,
        sum_rel_bias,
        sum_w_attn_out,
        sum_gain_ffn,
        sum_w_router,
        grad_w_in,
        grad_w_out,
    )


def solution(mesh):
    split_mesh = Mesh(mesh.devices.reshape(SPLIT), EVERY)
    in_specs = (
        P(WSH, CTX, None),
        P(),
        P(),
        P(),
        P(),
        P(),
        P(),
        P(CTX, None, WSH),
        P(CTX, WSH, None),
        P(WSH, CTX, None),
        P(),
        P(),
        P(WSH, CTX, None),
    )
    out_specs = (
        P(WSH, CTX, None),
        P(WSH, CTX, None),
        P(),
        P(),
        P(),
        P(),
        P(),
        P(),
        P(CTX, None, WSH),
        P(CTX, WSH, None),
    )
    return jax.shard_map(
        on_device, mesh=split_mesh, in_specs=in_specs, out_specs=out_specs, check_vma=False
    )
```

```python
import functools

import jax
import jax.numpy as jnp
from jax import lax
from jax.experimental import pallas as pl
from jax.experimental.pallas import tpu as pltpu
from jax.sharding import Mesh
from jax.sharding import PartitionSpec as P

BF = jnp.bfloat16
F32 = jnp.float32
EPSILON = 1e-06
HIGHEST = lax.Precision.HIGHEST
MASKED = -1e30
ROWS = (((0,), (0,)), ((), ()))
COLS = (((1,), (1,)), ((), ()))
LANES = 128
VMEM_LIMIT = 58 * 1024 * 1024
SPLIT = (2, 4, 2, 2, 4)
EVERY = ("ya", "z", "core", "yb", "x")
CTX = ("ya", "z", "core")
WSH = ("yb", "x")
SAME_CORE = ("ya", "z")
CHIPS = ("ya", "z", "yb", "x")
EXPERT_AXES = ("ya", "z", "core", "yb")
SWAP = ((0, 1), (1, 0))


def norm_scale(values):
    return lax.rsqrt(jnp.mean(values * values, axis=-1, keepdims=True) + EPSILON)


def norm_backward(values, scale_vector, gain_vector, upstream):
    weighted = upstream * gain_vector
    inner_mean = jnp.mean(weighted * values, axis=-1, keepdims=True)
    grad_input = (
        scale_vector * weighted - values * scale_vector * scale_vector * scale_vector * inner_mean
    )
    grad_gain = jnp.sum(upstream * values * scale_vector, axis=0)
    return (grad_input, grad_gain)


def contract_rows(left_matrix, right_matrix):
    return lax.dot_general(left_matrix, right_matrix, ROWS, preferred_element_type=F32)


def contract_cols(left_matrix, right_matrix):
    return lax.dot_general(left_matrix, right_matrix, COLS, preferred_element_type=F32)


def exchange(array, axes):
    return lax.all_to_all(array, axes, split_axis=0, concat_axis=0, tiled=True)


def spread(array, axes):
    return exchange(jnp.broadcast_to(array[None], (lax.axis_size(axes), *array.shape)), axes)


def half_share(kept, given):
    rows, columns = kept.shape
    chips = lax.axis_size(CHIPS)
    got = lax.ppermute(given, "core", SWAP)
    half = (kept.astype(F32) + got.astype(F32)).astype(BF).reshape(chips, rows // chips, columns)
    return jnp.sum(exchange(half, CHIPS).astype(F32), axis=0).astype(BF)


def shear(tiles):
    count, rows, columns = tiles.shape
    while rows > 8:
        half = rows // 2
        moved = pltpu.roll(tiles[:, :half].reshape(count * half, columns), half, axis=1)
        tiles = moved.reshape(count, half, columns) + tiles[:, half:]
        rows = half
    flat = tiles.reshape(count * rows, columns)
    row_ids = lax.broadcasted_iota(jnp.int32, flat.shape, 0)
    step = rows // 2
    while step:
        flat = jnp.where(row_ids // step % 2 == 0, pltpu.roll(flat, step, axis=1), flat)
        step //= 2
    return jnp.sum(flat.reshape(count, rows, columns), axis=1)


def split_heads(array, factor):
    lanes = lax.broadcasted_iota(jnp.int32, array.shape, 1) // (LANES // 2)
    wide = array.astype(F32) * factor
    parts = [jnp.where(lanes == head, wide, 0.0).astype(BF) for head in range(2)]
    return jnp.concatenate(parts, axis=0)


def join_heads(array):
    rows = array.shape[0] // 2
    lanes = lax.broadcasted_iota(jnp.int32, (rows, LANES), 1) // (LANES // 2)
    return jnp.where(lanes == 0, array[:rows], array[rows:]).astype(BF)


def attend_kernel(q_ref, kv_ref, window_ref, out_ref, exps_ref, total_ref):
    half, seq = q_ref.shape[0] // 2, kv_ref.shape[1]
    window = seq + 2 * half
    q = split_heads(q_ref[...], (LANES // 2) ** -0.5)
    raw = contract_cols(q, kv_ref[0])
    tiles = jnp.broadcast_to(window_ref[...][:, None], (4, half, window))
    tiles = [
        pltpu.roll(tiles[part], window - half + 1, axis=1, stride=1, stride_axis=0)[:, :seq]
        for part in range(4)
    ]
    scores = raw + jnp.concatenate(tiles, axis=0)
    exps = jnp.exp(scores - jnp.max(scores, axis=1, keepdims=True))
    inverse = 1.0 / jnp.sum(exps, axis=1, keepdims=True)
    exps = exps.astype(BF)
    exps_ref[...] = exps.reshape(exps_ref.shape)
    total_ref[...] = jnp.broadcast_to(inverse, total_ref.shape)
    out_ref[...] = join_heads(jnp.dot(exps, kv_ref[1], preferred_element_type=F32) * inverse)


def attend(queries, key_value, windows):
    rows, width = queries.shape
    pairs, seq = key_value.shape[1:3]
    work = rows * seq * width
    return pl.pallas_call(
        attend_kernel,
        grid=(pairs,),
        in_specs=[
            pl.BlockSpec((rows, LANES), lambda h: (0, h)),
            pl.BlockSpec((2, None, seq, LANES), lambda h: (0, h, 0, 0)),
            pl.BlockSpec((None, 4, windows.shape[2]), lambda h: (h, 0, 0)),
        ],
        out_specs=[
            pl.BlockSpec((rows, LANES), lambda h: (0, h)),
            pl.BlockSpec((2, rows, seq), lambda h: (h, 0, 0)),
            pl.BlockSpec((None, 2 * rows, LANES), lambda h: (h, 0, 0)),
        ],
        out_shape=[
            jax.ShapeDtypeStruct((rows, width), BF),
            jax.ShapeDtypeStruct((2 * pairs, rows, seq), BF),
            jax.ShapeDtypeStruct((pairs, 2 * rows, LANES), F32),
        ],
        compiler_params=pltpu.CompilerParams(vmem_limit_bytes=VMEM_LIMIT),
        cost_estimate=pl.CostEstimate(
            flops=8 * work,
            bytes_accessed=4 * seq * width + 4 * pairs * rows * seq,
            transcendentals=2 * pairs * rows * seq,
        ),
        name="attend",
    )(queries, key_value, windows)


def attend_back_kernel(
    exps_ref, inverse_ref, q_ref, kv_ref, grad_ref, dq_ref, dkv_ref, diag_ref
):
    half, seq = q_ref.shape[0] // 2, kv_ref.shape[1]
    factor = (LANES // 2) ** -0.5
    rows = 4 * half
    q = split_heads(q_ref[...], factor)
    inverse = inverse_ref[:, :1]
    grad = (split_heads(grad_ref[...], 1.0).astype(F32) * inverse).astype(BF)
    exps = exps_ref[...].reshape(rows, seq)
    wide = exps.astype(F32)
    prob_grad = contract_cols(grad, kv_ref[1])
    inner = jnp.sum(wide * prob_grad, axis=1, keepdims=True)
    score_grad = wide * (prob_grad - inner * inverse)
    tiles = jnp.concatenate([score_grad, jnp.zeros((rows, 2 * half), F32)], axis=1)
    sums = shear(tiles.reshape(4, half, seq + 2 * half))
    for part in range(2):
        for head in range(2):
            diag_ref[part, head : head + 1] = sums[2 * head + part : 2 * head + part + 1]
    score_grad = score_grad.astype(BF)
    query_grad = jnp.dot(score_grad, kv_ref[0], preferred_element_type=F32) * factor
    dq_ref[...] = join_heads(query_grad)
    dkv_ref[0] = contract_rows(q, score_grad).T.astype(BF)
    dkv_ref[1] = contract_rows(grad, exps).T.astype(BF)


def attend_back(exps, inverse, queries, key_value, attended_grad):
    rows, width = queries.shape
    pairs, seq = key_value.shape[1:3]
    window = seq + rows
    row_spec = pl.BlockSpec((rows, LANES), lambda h: (0, h))
    kv_spec = pl.BlockSpec((2, None, seq, LANES), lambda h: (0, h, 0, 0))
    return pl.pallas_call(
        attend_back_kernel,
        grid=(pairs,),
        in_specs=[
            pl.BlockSpec((2, rows, seq), lambda h: (h, 0, 0)),
            pl.BlockSpec((None, 2 * rows, LANES), lambda h: (h, 0, 0)),
            row_spec,
            kv_spec,
            row_spec,
        ],
        out_specs=[
            row_spec,
            kv_spec,
            pl.BlockSpec((2, None, 2, window), lambda h: (0, h, 0, 0)),
        ],
        out_shape=[
            jax.ShapeDtypeStruct((rows, width), BF),
            jax.ShapeDtypeStruct(key_value.shape, BF),
            jax.ShapeDtypeStruct((2, pairs, 2, window), F32),
        ],
        compiler_params=pltpu.CompilerParams(vmem_limit_bytes=VMEM_LIMIT),
        cost_estimate=pl.CostEstimate(
            flops=16 * rows * seq * width,
            bytes_accessed=8 * seq * width + 4 * pairs * rows * seq,
            transcendentals=0,
        ),
        name="attend_back",
    )(exps, inverse, queries, key_value, attended_grad)


def key_value_kernel(place_ref, near_ref, far_ref, gain_ref, wk_ref, wv_ref, normed_ref, kv_ref, *, half):
    tile = normed_ref.shape[0] // half
    near_blocks = near_ref.shape[0] // half
    rows = []
    for block in range(tile):
        source = place_ref[pl.program_id(0) * tile + block]
        at = pl.ds(pl.multiple_of(lax.rem(source, near_blocks) * half, half), half)
        rows.append(jnp.where(source < near_blocks, near_ref[at].astype(F32), far_ref[at].astype(F32)))
    inputs = jnp.concatenate(rows, axis=0)
    normed = (inputs * norm_scale(inputs) * gain_ref[...]).astype(BF)
    normed_ref[...] = normed
    for part, weight_ref in enumerate((wk_ref, wv_ref)):
        out = jnp.dot(normed, weight_ref[...], preferred_element_type=F32).astype(BF)
        for pair in range(kv_ref.shape[1]):
            kv_ref[part, pair] = out[:, pair * LANES : (pair + 1) * LANES]


def keys_and_values(place, near, far, gain, w_qkv, half):
    near_rows, width = near.shape
    seq = 2 * near_rows
    tile = 8 * half
    return pl.pallas_call(
        functools.partial(key_value_kernel, half=half),
        grid_spec=pltpu.PrefetchScalarGridSpec(
            num_scalar_prefetch=1,
            grid=(seq // tile,),
            in_specs=[
                pl.BlockSpec((near_rows, width), lambda r, p: (0, 0)),
                pl.BlockSpec((near_rows, width), lambda r, p: (0, 0)),
                pl.BlockSpec((1, width), lambda r, p: (0, 0)),
                pl.BlockSpec((width, width), lambda r, p: (0, 1)),
                pl.BlockSpec((width, width), lambda r, p: (0, 2)),
            ],
            out_specs=[
                pl.BlockSpec((tile, width), lambda r, p: (r, 0)),
                pl.BlockSpec((2, width // LANES, tile, LANES), lambda r, p: (0, 0, r, 0)),
            ],
        ),
        out_shape=[
            jax.ShapeDtypeStruct((seq, width), BF),
            jax.ShapeDtypeStruct((2, width // LANES, seq, LANES), BF),
        ],
        compiler_params=pltpu.CompilerParams(vmem_limit_bytes=VMEM_LIMIT),
        cost_estimate=pl.CostEstimate(
            flops=4 * seq * width * width, bytes_accessed=8 * seq * width, transcendentals=seq
        ),
        name="keys_and_values",
    )(place, near, far, gain[None], w_qkv, w_qkv)


def normed_grad_kernel(position_ref, *refs):
    *block_refs, wk_ref, wv_ref, out_ref = refs
    out = 0.0
    for part, weight_ref in enumerate((wk_ref, wv_ref)):
        rows = []
        for block_ref in block_refs:
            pairs = [block_ref[part, pair] for pair in range(block_ref.shape[1])]
            rows.append(jnp.concatenate(pairs, axis=1))
        out += contract_cols(jnp.concatenate(rows, axis=0), weight_ref[...])
    out_ref[...] = out.astype(BF)


def normed_grads(position, key_value_grad, w_qkv, half):
    width = w_qkv.shape[0]
    pairs = key_value_grad.shape[1]
    count = position.shape[0]
    rows = count * half
    step = 8

    def block_spec(at):
        return pl.BlockSpec((2, pairs, half, LANES), lambda r, p: (0, 0, p[step * r + at], 0))

    return pl.pallas_call(
        normed_grad_kernel,
        grid_spec=pltpu.PrefetchScalarGridSpec(
            num_scalar_prefetch=1,
            grid=(count // step,),
            in_specs=[
                *[block_spec(at) for at in range(step)],
                pl.BlockSpec((width, width), lambda r, p: (0, 1)),
                pl.BlockSpec((width, width), lambda r, p: (0, 2)),
            ],
            out_specs=pl.BlockSpec((step * half, width), lambda r, p: (r, 0)),
        ),
        out_shape=jax.ShapeDtypeStruct((rows, width), BF),
        compiler_params=pltpu.CompilerParams(vmem_limit_bytes=VMEM_LIMIT),
        cost_estimate=pl.CostEstimate(
            flops=4 * rows * width * width, bytes_accessed=8 * rows * width, transcendentals=0
        ),
        name="normed_grads",
    )(position, *([key_value_grad] * step), w_qkv, w_qkv)


def weight_grad_kernel(
    core_ref,
    dq_ref,
    normed_ref,
    dkv_ref,
    all_normed_ref,
    attended_ref,
    branch_ref,
    small_ref,
    hot_ref,
    diag_ref,
    kept_ref,
    given_ref,
):
    step = pl.program_id(0)
    side = kept_ref.shape[1]

    def give(total):
        left, right = total[:, :side].astype(BF), total[:, side:].astype(BF)
        rows = total.shape[0]

        @pl.when(core_ref[0] == 0)
        def _():
            kept_ref[:rows] = left
            given_ref[:rows] = right

        @pl.when(core_ref[0] != 0)
        def _():
            kept_ref[:rows] = right
            given_ref[:rows] = left

    @pl.when(step == 0)
    def _():
        give(contract_rows(dq_ref[...], normed_ref[...]))

    @pl.when((step == 1) | (step == 2))
    def _():
        pairs = [dkv_ref[pair] for pair in range(dkv_ref.shape[0])]
        give(contract_rows(jnp.concatenate(pairs, axis=1), all_normed_ref[...]))

    @pl.when(step == 3)
    def _():
        give(contract_rows(attended_ref[...], branch_ref[...]))

    @pl.when(step == 4)
    def _():
        window = diag_ref.shape[3]
        bias_grad = 0.0
        for part in range(2):
            sums = jnp.concatenate([diag_ref[part, pair] for pair in range(diag_ref.shape[1])], axis=0)
            bias_grad += lax.dot_general(
                hot_ref[:, part * window : (part + 1) * window],
                sums,
                COLS,
                precision=HIGHEST,
                preferred_element_type=F32,
            )
        buckets, heads = bias_grad.shape
        spare = jnp.zeros((buckets, small_ref.shape[1] - heads), F32)
        bias_rows = jnp.concatenate([bias_grad, spare], axis=1)
        give(jnp.concatenate([small_ref[...], bias_rows], axis=0))


def weight_grads(
    core,
    query_grad,
    normed_one,
    key_value_grad,
    all_normed,
    attended,
    branch_grad,
    small,
    bucket_hot,
    diagonals,
    spare,
):
    rows, width = normed_one.shape
    seq = all_normed.shape[0]
    total = 4 * width + small.shape[0] + bucket_hot.shape[0] + spare
    row_spec = pl.BlockSpec((rows, width), lambda t, p: (0, 0))
    out_spec = pl.BlockSpec((width, width // 2), lambda t, p: (t, 0))
    out_shape = jax.ShapeDtypeStruct((total, width // 2), BF)
    return pl.pallas_call(
        weight_grad_kernel,
        grid_spec=pltpu.PrefetchScalarGridSpec(
            num_scalar_prefetch=1,
            grid=(5,),
            in_specs=[
                row_spec,
                row_spec,
                pl.BlockSpec(
                    (None, width // LANES, seq, LANES), lambda t, p: (jnp.clip(t - 1, 0, 1), 0, 0, 0)
                ),
                pl.BlockSpec((seq, width), lambda t, p: (0, 0)),
                row_spec,
                row_spec,
                pl.BlockSpec(small.shape, lambda t, p: (0, 0)),
                pl.BlockSpec(bucket_hot.shape, lambda t, p: (0, 0)),
                pl.BlockSpec(diagonals.shape, lambda t, p: (0, 0, 0, 0)),
            ],
            out_specs=[out_spec, out_spec],
        ),
        out_shape=[out_shape, out_shape],
        compiler_params=pltpu.CompilerParams(vmem_limit_bytes=VMEM_LIMIT),
        cost_estimate=pl.CostEstimate(
            flops=4 * seq * width * width, bytes_accessed=10 * seq * width, transcendentals=0
        ),
        name="weight_grads",
    )(
        core,
        query_grad,
        normed_one,
        key_value_grad,
        all_normed,
        attended,
        branch_grad,
        small,
        bucket_hot,
        diagonals,
    )


def whole_grad_kernel(side_ref, half_ref, weight_ref, *refs):
    grad_ref, product_ref, out_ref = refs[-3:]
    step = pl.program_id(0)
    last = pl.num_programs(0) - 1
    half = half_ref[...].astype(F32)

    @pl.when(step < last)
    def _():
        grad = half.T
        grad_ref[...] = grad
        product = jnp.sum(grad * weight_ref[...].astype(F32), axis=1, keepdims=True)
        product = jnp.broadcast_to(product, product_ref.shape)

        @pl.when(step == 0)
        def _():
            product_ref[...] = product

        @pl.when(step > 0)
        def _():
            product_ref[...] += product

    @pl.when(step == last)
    def _():
        out_ref[...] = half


def whole_grad(side, half_sums, weight, held):
    width, columns = weight.shape
    half = half_sums.shape[1]
    steps = columns // width + 1

    def tile_map(t, p):
        return (p[0], jnp.minimum(t, steps - 2))

    return pl.pallas_call(
        whole_grad_kernel,
        grid_spec=pltpu.PrefetchScalarGridSpec(
            num_scalar_prefetch=1,
            grid=(steps,),
            in_specs=[
                pl.BlockSpec((width, half), lambda t, p: (t, 0)),
                pl.BlockSpec((half, width), tile_map),
                *[pl.BlockSpec(memory_space=pl.ANY) for _ in held],
            ],
            out_specs=[
                pl.BlockSpec((half, width), tile_map),
                pl.BlockSpec((half, LANES), lambda t, p: (p[0], 0)),
                pl.BlockSpec((width, half), lambda t, p: (0, p[0])),
            ],
        ),
        out_shape=[
            jax.ShapeDtypeStruct((width, columns), F32),
            jax.ShapeDtypeStruct((width, LANES), F32),
            jax.ShapeDtypeStruct((width, width), F32),
        ],
        input_output_aliases={3 + at: at for at in range(len(held))},
        compiler_params=pltpu.CompilerParams(vmem_limit_bytes=VMEM_LIMIT),
        cost_estimate=pl.CostEstimate(
            flops=width * columns, bytes_accessed=4 * width * columns, transcendentals=0
        ),
        name="whole_grad",
    )(side, half_sums, weight, *held)


def expert_rows(x_ref, cot_ref):
    width = cot_ref.shape[-1]
    rows = x_ref.shape[0] * x_ref.shape[1]
    rows_in = x_ref[...].reshape(rows, x_ref.shape[2])
    gate = jnp.sum(rows_in[:, width:].astype(F32), axis=1, keepdims=True)
    slot_grad = (cot_ref[...].reshape(rows, width).astype(F32) * gate).astype(BF)
    return rows_in[:, :width], slot_grad, gate


def high_and_low(column):
    high = column.astype(BF).astype(F32)
    lanes = lax.broadcasted_iota(jnp.int32, (column.shape[0], LANES), 1)
    wide = jnp.where(lanes == 0, high, jnp.where(lanes == 1, column - high, 0.0))
    return wide.astype(BF)


def write_weight_grads(x, slot_grad, activated, pre_grad, grad_ref):
    grad_in = contract_rows(x, pre_grad).astype(BF)
    grad_out = contract_rows(activated, slot_grad).astype(BF)
    slices, hidden = grad_ref.shape[0], grad_ref.shape[1] // 2
    for index in range(slices):
        columns = grad_in[:, index * hidden : (index + 1) * hidden]
        grad_ref[index, :hidden, :hidden] = columns[:hidden]
        grad_ref[index, :hidden, hidden:] = columns[hidden:]
        grad_ref[index, hidden:] = grad_out[index * hidden : (index + 1) * hidden]


def slice_weights(weight_ref):
    slices, hidden = weight_ref.shape[0], weight_ref.shape[1] // 2
    weights = [weight_ref[index] for index in range(slices)]
    tops = [weight[:hidden] for weight in weights]
    tops = [jnp.concatenate([top[:, :hidden], top[:, hidden:]], axis=0) for top in tops]
    weight_out = jnp.concatenate([weight[hidden:] for weight in weights], axis=0)
    return jnp.concatenate(tops, axis=1), weight_out


def cotangent_kernel(cot_ref, weight_ref, units_ref):
    rows = cot_ref.shape[0] * cot_ref.shape[1]
    cot = cot_ref[...].reshape(rows, cot_ref.shape[2])
    slices, hidden = weight_ref.shape[0], weight_ref.shape[1]
    weight_out = weight_ref[...].reshape(slices * hidden, weight_ref.shape[2])
    units_ref[...] = contract_cols(cot, weight_out).astype(BF)


def cotangent_units(cot_rows, weights):
    devices, experts, slots, width = cot_rows.shape
    parts, _, both, _ = weights.shape
    hidden = both // 2
    rows = devices * slots
    slices = 2
    return pl.pallas_call(
        cotangent_kernel,
        grid=(experts, parts // slices),
        in_specs=[
            pl.BlockSpec((devices, None, slots, width), lambda e, w: (0, e, 0, 0)),
            pl.BlockSpec((slices, None, hidden, width), lambda e, w: (w, e, 1, 0)),
        ],
        out_specs=pl.BlockSpec((None, rows, slices * hidden), lambda e, w: (e, 0, w)),
        out_shape=jax.ShapeDtypeStruct((experts, rows, parts * hidden), BF),
        compiler_params=pltpu.CompilerParams(vmem_limit_bytes=VMEM_LIMIT),
        cost_estimate=pl.CostEstimate(
            flops=2 * experts * rows * width * parts * hidden,
            bytes_accessed=4 * experts * rows * width + 2 * parts * experts * width * hidden,
            transcendentals=0,
        ),
        name="cotangent_units",
    )(cot_rows, weights)


def expert_kernel(
    x_ref,
    cot_ref,
    units_ref,
    weight_ref,
    dx_ref,
    ret_ref,
    first_grad_ref,
    act_ref,
    pre_grad_ref,
    ret_sum,
    dx_sum,
):
    part = pl.program_id(1)
    width = cot_ref.shape[-1]
    x, slot_grad, gate = expert_rows(x_ref, cot_ref)
    weight_in, weight_out = slice_weights(weight_ref)
    pre = jnp.dot(x, weight_in, preferred_element_type=F32)
    act_grad = units_ref[...].astype(F32) * gate
    cumulative = 0.5 * (1.0 + lax.erf(pre * 0.7071067811865476))
    activated = (pre * cumulative).astype(BF)
    slope = cumulative + pre * (jnp.exp(-0.5 * pre * pre) * 0.3989422804014327)
    pre_grad = (act_grad * slope).astype(BF)
    returned = jnp.dot(activated, weight_out, preferred_element_type=F32)
    input_grad = contract_cols(pre_grad, weight_in)

    @pl.when(pl.program_id(0) == 0)
    def _():
        write_weight_grads(x, slot_grad, activated, pre_grad, first_grad_ref)

    @pl.when(pl.program_id(0) > 0)
    def _():
        act_ref[...] = activated
        pre_grad_ref[...] = pre_grad

    @pl.when(part == 0)
    def _():
        ret_sum[...] = returned
        dx_sum[...] = input_grad

    @pl.when(part > 0)
    def _():
        ret_sum[...] += returned
        dx_sum[...] += input_grad

    @pl.when(part == pl.num_programs(1) - 1)
    def _():
        shape = cot_ref.shape
        rows = shape[0] * shape[1]
        ret = ret_sum[...]
        ret_ref[...] = ret.astype(BF).reshape(shape)
        upstream = cot_ref[...].reshape(rows, width).astype(F32)
        gate_grad = high_and_low(jnp.sum(ret * upstream, axis=1, keepdims=True))
        dx_ref[:, :, :width] = dx_sum[...].astype(BF).reshape(shape)
        dx_ref[:, :, width:] = gate_grad.reshape(shape[0], shape[1], LANES)


def expert_grad_kernel(x_ref, cot_ref, act_ref, pre_grad_ref, grad_ref):
    x, slot_grad, _ = expert_rows(x_ref, cot_ref)
    write_weight_grads(x, slot_grad, act_ref[...], pre_grad_ref[...], grad_ref)


def run_experts(x_rows, cot_rows, units, weights):
    devices, experts, slots, width = cot_rows.shape
    wide = x_rows.shape[3]
    parts, _, both, _ = weights.shape
    hidden = both // 2
    rows = devices * slots
    slices = 2
    steps = parts // slices

    def row_spec(columns):
        return pl.BlockSpec((devices, None, slots, columns), lambda e, w: (0, e, 0, 0))

    later = experts - 1
    hidden_spec = pl.BlockSpec(
        (None, rows, slices * hidden),
        lambda e, w: (jnp.maximum(e - 1, 0), 0, jnp.where(e == 0, 0, w)),
    )
    hidden_shape = jax.ShapeDtypeStruct((later, rows, parts * hidden), BF)
    grad_shape = jax.ShapeDtypeStruct((parts, both, width), BF)
    work = experts * rows * width * parts * hidden
    params = pltpu.CompilerParams(vmem_limit_bytes=VMEM_LIMIT)
    input_grad, returned, first_grad, activated, pre_grad = pl.pallas_call(
        expert_kernel,
        grid=(experts, steps),
        in_specs=[
            row_spec(wide),
            row_spec(width),
            pl.BlockSpec((None, rows, slices * hidden), lambda e, w: (e, 0, w)),
            pl.BlockSpec((slices, None, both, width), lambda e, w: (w, e, 0, 0)),
        ],
        out_specs=[
            row_spec(width + LANES),
            row_spec(width),
            pl.BlockSpec(
                (slices, both, width), lambda e, w: (jnp.where(e == 0, w, steps - 1), 0, 0)
            ),
            hidden_spec,
            hidden_spec,
        ],
        out_shape=[
            jax.ShapeDtypeStruct((devices, experts, slots, width + LANES), BF),
            jax.ShapeDtypeStruct((devices, experts, slots, width), BF),
            grad_shape,
            hidden_shape,
            hidden_shape,
        ],
        scratch_shapes=[pltpu.VMEM((rows, width), F32), pltpu.VMEM((rows, width), F32)],
        compiler_params=params,
        cost_estimate=pl.CostEstimate(
            flops=10 * work,
            bytes_accessed=8 * experts * rows * width + 4 * parts * experts * width * hidden,
            transcendentals=2 * experts * rows * parts * hidden,
        ),
        name="experts",
    )(x_rows, cot_rows, units, weights)
    weight_grads_of = [first_grad]
    for expert in range(1, experts):

        def own_rows(columns, expert=expert):
            return pl.BlockSpec((devices, None, slots, columns), lambda w: (0, expert, 0, 0))

        own_hidden = pl.BlockSpec(
            (None, rows, slices * hidden), lambda w, expert=expert: (expert - 1, 0, w)
        )
        weight_grads_of.append(
            pl.pallas_call(
                expert_grad_kernel,
                grid=(steps,),
                in_specs=[own_rows(wide), own_rows(width), own_hidden, own_hidden],
                out_specs=pl.BlockSpec((slices, both, width), lambda w: (w, 0, 0)),
                out_shape=grad_shape,
                compiler_params=params,
                cost_estimate=pl.CostEstimate(
                    flops=4 * work // experts,
                    bytes_accessed=8 * rows * width + 4 * parts * width * hidden,
                    transcendentals=0,
                ),
                name="expert_grads",
            )(x_rows, cot_rows, activated, pre_grad)
        )
    return input_grad, returned, weight_grads_of


def into_experts_kernel(
    attended_ref,
    tokens_ref,
    w_out_ref,
    gain_ref,
    w_router_ref,
    chosen_ref,
    table_ref,
    residual_ref,
    normed_ref,
    gate_ref,
    slots_ref,
):
    inputs = tokens_ref[...].astype(F32)
    residual = inputs + jnp.dot(attended_ref[...], w_out_ref[...], preferred_element_type=F32)
    residual_ref[...] = residual
    normed = (residual * norm_scale(residual) * gain_ref[...]).astype(BF)
    normed_ref[...] = normed
    logits = jnp.dot(normed, w_router_ref[...], preferred_element_type=F32)
    hots = picked_hots(chosen_ref, logits.shape)
    first, second = [jnp.sum(hot * logits, axis=1, keepdims=True) for hot in hots]
    peak = jnp.maximum(first, second)
    first, second = jnp.exp(first - peak), jnp.exp(second - peak)
    gates = [first / (first + second), second / (first + second)]
    lanes = lax.broadcasted_iota(jnp.int32, gate_ref.shape, 1)
    gate_ref[...] = jnp.where(lanes == 0, gates[0], jnp.where(lanes == 1, gates[1], 0.0))
    picks = [jnp.concatenate([normed, high_and_low(gate)], axis=1) for gate in gates]
    slots_ref[...] = contract_rows(table_ref[...], jnp.concatenate(picks, axis=0)).astype(BF)


def picked_hots(chosen_ref, shape):
    ids = lax.broadcasted_iota(jnp.int32, shape, 1)
    return [jnp.where(chosen_ref[:, pick : pick + 1] == ids, 1.0, 0.0) for pick in range(2)]


def into_experts(attended, tokens, w_attn_out, gain, w_router, chosen, table):
    rows, width = attended.shape
    return pl.pallas_call(
        into_experts_kernel,
        out_shape=[
            jax.ShapeDtypeStruct((rows, width), F32),
            jax.ShapeDtypeStruct((rows, width), BF),
            jax.ShapeDtypeStruct((rows, LANES), F32),
            jax.ShapeDtypeStruct((table.shape[1], width + LANES), BF),
        ],
        compiler_params=pltpu.CompilerParams(vmem_limit_bytes=VMEM_LIMIT),
        name="into_experts",
    )(attended, tokens, w_attn_out, gain[None], w_router, chosen, table)


def out_of_experts_kernel(
    grads_ref,
    table_ref,
    gate_ref,
    chosen_ref,
    normed_ref,
    residual_ref,
    cot_ref,
    gain_ref,
    w_router_ref,
    w_out_ref,
    mixed_ref,
    branch_ref,
    attended_grad_ref,
    small_ref,
):
    rows, width = residual_ref.shape
    table = table_ref[...]
    grads = jnp.dot(table, grads_ref[...], preferred_element_type=F32)
    gate_grads = jnp.sum(grads[:, width:], axis=1, keepdims=True)
    gate_grads = [gate_grads[:rows], gate_grads[rows:]]
    gates = [gate_ref[:, :1], gate_ref[:, 1:2]]
    inner = gates[0] * gate_grads[0] + gates[1] * gate_grads[1]
    hots = picked_hots(chosen_ref, (rows, w_router_ref.shape[1]))
    logit_grad = sum(
        hot * (gate * (gate_grad - inner)) for hot, gate, gate_grad in zip(hots, gates, gate_grads)
    )
    normed = normed_ref[...].astype(F32)
    w_router = w_router_ref[...].astype(F32)
    w_router_grad = lax.dot_general(
        logit_grad, normed, ROWS, precision=HIGHEST, preferred_element_type=F32
    )
    router_back = lax.dot_general(
        logit_grad, w_router, COLS, precision=HIGHEST, preferred_element_type=F32
    )
    normed_grad = grads[:rows, :width] + grads[rows:, :width] + router_back
    residual = residual_ref[...]
    norm_part, gain_grad = norm_backward(
        residual, norm_scale(residual), gain_ref[...], normed_grad
    )
    mixed = cot_ref[...].astype(F32) + norm_part
    mixed_ref[...] = mixed
    branch = mixed.astype(BF)
    branch_ref[...] = branch
    attended_grad_ref[...] = contract_cols(branch, w_out_ref[...]).astype(BF)
    experts = w_router_grad.shape[0]
    small_ref[:experts] = w_router_grad
    tail = small_ref.shape[0] - experts
    first = lax.broadcasted_iota(jnp.int32, (tail, width), 0) == 0
    small_ref[experts:] = jnp.where(first, gain_grad[None], 0.0)


def out_of_experts(
    grads, table, gates, chosen, normed, residual, cotangent, gain, w_router, w_attn_out
):
    rows, width = residual.shape
    return pl.pallas_call(
        out_of_experts_kernel,
        out_shape=[
            jax.ShapeDtypeStruct((rows, width), F32),
            jax.ShapeDtypeStruct((rows, width), BF),
            jax.ShapeDtypeStruct((rows, width), BF),
            jax.ShapeDtypeStruct((w_router.shape[1] + 8, width), F32),
        ],
        compiler_params=pltpu.CompilerParams(vmem_limit_bytes=VMEM_LIMIT),
        name="out_of_experts",
    )(grads, table, gates, chosen, normed, residual, cotangent, gain[None], w_router, w_attn_out)


def on_device(
    tokens,
    gain_attn,
    w_qkv,
    rel_bias,
    w_attn_out,
    gain_ffn,
    w_router,
    w_in,
    w_out,
    routes,
    pair_order,
    bucket_table,
    cotangent,
):
    tok_rows = tokens.shape[1]
    model_width = tokens.shape[2]
    head_count = rel_bias.shape[1]
    bucket_count = rel_bias.shape[0]
    ctx_count = lax.axis_size(CTX)
    half = tok_rows // 2
    blocks = 2 * ctx_count
    seq = half * blocks
    window = seq + 2 * half
    head_pairs = head_count // 2
    local_experts = w_in.shape[0]
    experts = w_router.shape[1]
    capacity = 4 * tok_rows // experts
    device_slots = local_experts * capacity
    expert_devices = lax.axis_size(EXPERT_AXES)
    copies = expert_devices // ctx_count

    near_tokens = spread(tokens[0], SAME_CORE)
    far_tokens = lax.ppermute(near_tokens, "core", SWAP)
    near_tokens = near_tokens.reshape(seq // 2, model_width)
    far_tokens = far_tokens.reshape(seq // 2, model_width)
    hidden = w_in.shape[2]
    weights = jnp.concatenate([w_in[:, :hidden], w_in[:, hidden:]], axis=2)
    weights = jnp.concatenate([weights, w_out], axis=1)
    weights = lax.all_gather(weights, "x", axis=0)

    chosen = routes[0].T
    expert_ids = jnp.arange(experts, dtype=jnp.int32)
    flat_expert = chosen.reshape(2 * tok_rows)
    member = flat_expert[:, None] == expert_ids[None, :]
    picks = jnp.arange(2 * tok_rows, dtype=jnp.int32)
    before = (picks[:, None] > picks[None, :]).astype(BF)
    counts = jnp.dot(before, member.astype(BF), preferred_element_type=F32)
    slot_rank = jnp.sum(jnp.where(member, counts, 0.0), axis=1).astype(jnp.int32)
    owner_index = flat_expert // local_experts
    slot_of = (flat_expert % local_experts) * capacity + slot_rank
    slot_ids = jnp.arange(expert_devices * device_slots, dtype=jnp.int32)
    slot_hot = (owner_index[:, None] == (slot_ids // (copies * device_slots))[None, :]) & (
        slot_of[:, None] == (slot_ids % device_slots)[None, :]
    )
    slot_table = slot_hot.astype(BF)
    token_table = slot_table[:tok_rows] + slot_table[tok_rows:]

    def to_slots(slots):
        arrived = exchange(slots.reshape(expert_devices, device_slots, -1), EXPERT_AXES)
        return arrived.reshape(expert_devices, local_experts, capacity, -1)

    cot_rows = to_slots(contract_rows(token_table, cotangent[0]).astype(BF))

    ctx_ids = jnp.arange(ctx_count, dtype=jnp.int32)
    my_core = lax.axis_index("core")
    near = (ctx_ids % 2) == my_core
    lies = 2 * (jnp.where(near, 0, ctx_count // 2) + ctx_ids // 2)
    block_ids = jnp.arange(blocks, dtype=jnp.int32)[:, None]
    place = jnp.sum(
        jnp.where(pair_order[None, :] == block_ids, lies[None, :], 0)
        + jnp.where(blocks - 1 - pair_order[None, :] == block_ids, lies[None, :] + 1, 0),
        axis=1,
        dtype=jnp.int32,
    )
    positions = jnp.sum(
        jnp.where(
            2 * (block_ids // 2) == lies[None, :],
            jnp.where(block_ids % 2 == 0, pair_order[None, :], blocks - 1 - pair_order[None, :]),
            0,
        ),
        axis=1,
        dtype=jnp.int32,
    )
    my_pair = jnp.sum(jnp.where(ctx_ids == lax.axis_index(CTX), pair_order, 0))
    reversed_table = jnp.pad(bucket_table[::-1], (0, window - half), constant_values=-1)
    diagonal_bucket = jnp.stack(
        [
            lax.dynamic_slice(reversed_table, (seq - half - block * half,), (window,))
            for block in (my_pair, blocks - 1 - my_pair)
        ]
    ).reshape(1, 2 * window)
    bucket_ids = jnp.arange(bucket_count, dtype=jnp.int32)
    bucket_hot = (diagonal_bucket == bucket_ids[:, None]).astype(F32)
    windows = lax.dot_general(rel_bias, bucket_hot, ROWS, precision=HIGHEST)
    windows = jnp.where(diagonal_bucket >= 0, windows, MASKED)
    windows = windows.reshape(head_pairs, 4, window)

    inputs = tokens[0].astype(F32)
    scale_one = norm_scale(inputs)
    normed_one = (inputs * scale_one * gain_attn).astype(BF)
    w_q = w_qkv[:, :model_width]
    queries = jnp.dot(normed_one, w_q, preferred_element_type=F32).astype(BF)
    all_normed, key_value = keys_and_values(
        place, near_tokens, far_tokens, gain_attn, w_qkv, half
    )
    attended, exps, inverse = attend(queries, key_value, windows)

    residual_one, normed_two, gates, slots = into_experts(
        attended, tokens[0], w_attn_out, gain_ffn, w_router, routes[0], slot_table
    )
    x_rows = to_slots(slots)
    units = cotangent_units(cot_rows, weights)
    input_grad, returned, parts = run_experts(x_rows, cot_rows, units, weights)

    def from_experts(rows):
        rows = exchange(rows.reshape(expert_devices, device_slots, rows.shape[3]), EXPERT_AXES)
        return rows.reshape(expert_devices * device_slots, rows.shape[2])

    input_grad = from_experts(input_grad)
    later_parts, input_grad, returned = lax.optimization_barrier(
        (parts[1:], input_grad, returned)
    )
    shares = [
        lax.psum_scatter(part, "x", scatter_dimension=0) for part in (parts[0], *later_parts)
    ]
    returned = from_experts(returned)

    mixed_grad, branch_grad, attended_grad, small = out_of_experts(
        input_grad,
        slot_table,
        gates,
        routes[0],
        normed_two,
        residual_one,
        cotangent[0],
        gain_ffn,
        w_router,
        w_attn_out,
    )

    query_grad, key_value_grad, diagonals = attend_back(
        exps, inverse, queries, key_value, attended_grad
    )
    query_grad, returned = lax.optimization_barrier((query_grad, returned))

    core = jnp.reshape(my_core, (1,)).astype(jnp.int32)
    side = model_width // 2
    spare = -(4 * model_width + small.shape[0] + bucket_count) % (8 * lax.axis_size(CHIPS))
    kept, given = weight_grads(
        core,
        query_grad,
        normed_one,
        key_value_grad,
        all_normed,
        attended,
        branch_grad,
        small,
        bucket_hot,
        diagonals,
        spare,
    )
    key_value_grad, kept, given, returned = lax.optimization_barrier(
        (key_value_grad, kept, given, returned)
    )
    share = half_share(kept, given)
    picked = jnp.dot(slot_table, returned, preferred_element_type=F32)
    mixture = gates[:, :1] * picked[:tok_rows] + gates[:, 1:2] * picked[tok_rows:]
    layer_out = (residual_one + mixture).astype(BF)[None]

    far_grad = normed_grads(positions[blocks // 2 :], key_value_grad, w_qkv, half)
    near_grad = normed_grads(positions[: blocks // 2], key_value_grad, w_qkv, half)
    near_grad = near_grad.astype(F32) + lax.ppermute(far_grad, "core", SWAP).astype(F32)
    near_grad = near_grad.astype(BF).reshape(ctx_count // 2, tok_rows, model_width)
    query_part = contract_cols(query_grad, w_q)
    share, near_grad, query_part, layer_out, shares = lax.optimization_barrier(
        (share, near_grad, query_part, layer_out, shares)
    )

    mine = spread(share, CHIPS).reshape(-1, side)
    shares = jnp.stack(shares).astype(F32)
    grad_w_in = jnp.concatenate([shares[:, :hidden, :hidden], shares[:, :hidden, hidden:]], axis=1)
    grad_w_out = shares[:, hidden:]
    mine, near_grad, grad_w_in, grad_w_out = lax.optimization_barrier(
        (mine, near_grad, grad_w_in, grad_w_out)
    )
    other = lax.ppermute(mine, "core", SWAP)
    row_grads = exchange(near_grad, SAME_CORE)
    held = whole_grad(core, mine, w_qkv, ())
    whole = whole_grad(1 - core, other, w_qkv, held)
    row_grads, sum_w_qkv, products, sum_w_attn_out = lax.optimization_barrier((row_grads, *whole))
    normed_one_grad = jnp.sum(row_grads.astype(F32), axis=0) + query_part
    input_norm_grad, _ = norm_backward(inputs, scale_one, gain_attn, normed_one_grad)
    grad_tokens = (mixed_grad + input_norm_grad)[None]
    sum_gain_attn = products[:, 0] / gain_attn
    rows = slice(4 * model_width, 4 * model_width + small.shape[0] + bucket_count)
    left = jnp.where(my_core == 0, mine[rows], other[rows])
    right = jnp.where(my_core == 0, other[rows], mine[rows])
    sums = jnp.concatenate([left, right], axis=1).astype(F32)
    sum_w_router, sum_gain_ffn = sums[:experts].T, sums[experts]
    sum_rel_bias = sums[small.shape[0] :, :head_count]
    return (
        layer_out,
        grad_tokens,
        sum_gain_attn,
        sum_w_qkv,
        sum_rel_bias,
        sum_w_attn_out,
        sum_gain_ffn,
        sum_w_router,
        grad_w_in,
        grad_w_out,
    )


def solution(mesh):
    split_mesh = Mesh(mesh.devices.reshape(SPLIT), EVERY)
    in_specs = (
        P(WSH, CTX, None),
        P(),
        P(),
        P(),
        P(),
        P(),
        P(),
        P(CTX, None, WSH),
        P(CTX, WSH, None),
        P(WSH, CTX, None),
        P(),
        P(),
        P(WSH, CTX, None),
    )
    out_specs = (
        P(WSH, CTX, None),
        P(WSH, CTX, None),
        P(),
        P(),
        P(),
        P(),
        P(),
        P(),
        P(CTX, None, WSH),
        P(CTX, WSH, None),
    )
    return jax.shard_map(
        on_device, mesh=split_mesh, in_specs=in_specs, out_specs=out_specs, check_vma=False
    )
```

```python
import functools

import jax
import jax.numpy as jnp
from jax import lax
from jax.experimental import pallas as pl
from jax.experimental.pallas import tpu as pltpu
from jax.sharding import Mesh
from jax.sharding import PartitionSpec as P

BF = jnp.bfloat16
F32 = jnp.float32
EPSILON = 1e-06
HIGHEST = lax.Precision.HIGHEST
MASKED = -1e30
ROWS = (((0,), (0,)), ((), ()))
COLS = (((1,), (1,)), ((), ()))
LANES = 128
VMEM_LIMIT = 58 * 1024 * 1024
SPLIT = (2, 4, 2, 2, 4)
EVERY = ("ya", "z", "core", "yb", "x")
CTX = ("ya", "z", "core")
WSH = ("yb", "x")
SAME_CORE = ("ya", "z")
CHIPS = ("ya", "z", "yb", "x")
EXPERT_AXES = ("ya", "z", "core", "yb")
SWAP = ((0, 1), (1, 0))


def norm_scale(values):
    return lax.rsqrt(jnp.mean(values * values, axis=-1, keepdims=True) + EPSILON)


def norm_backward(values, scale_vector, gain_vector, upstream):
    weighted = upstream * gain_vector
    inner_mean = jnp.mean(weighted * values, axis=-1, keepdims=True)
    grad_input = (
        scale_vector * weighted - values * scale_vector * scale_vector * scale_vector * inner_mean
    )
    grad_gain = jnp.sum(upstream * values * scale_vector, axis=0)
    return (grad_input, grad_gain)


def contract_rows(left_matrix, right_matrix):
    return lax.dot_general(left_matrix, right_matrix, ROWS, preferred_element_type=F32)


def contract_cols(left_matrix, right_matrix):
    return lax.dot_general(left_matrix, right_matrix, COLS, preferred_element_type=F32)


def exchange(array, axes):
    return lax.all_to_all(array, axes, split_axis=0, concat_axis=0, tiled=True)


def spread(array, axes):
    return exchange(jnp.broadcast_to(array[None], (lax.axis_size(axes), *array.shape)), axes)


def half_share(kept, given):
    rows, columns = kept.shape
    chips = lax.axis_size(CHIPS)
    got = lax.ppermute(given, "core", SWAP)
    half = (kept.astype(F32) + got.astype(F32)).astype(BF).reshape(chips, rows // chips, columns)
    return jnp.sum(exchange(half, CHIPS).astype(F32), axis=0).astype(BF)


def shear(tiles):
    count, rows, columns = tiles.shape
    while rows > 8:
        half = rows // 2
        moved = pltpu.roll(tiles[:, :half].reshape(count * half, columns), half, axis=1)
        tiles = moved.reshape(count, half, columns) + tiles[:, half:]
        rows = half
    flat = tiles.reshape(count * rows, columns)
    row_ids = lax.broadcasted_iota(jnp.int32, flat.shape, 0)
    step = rows // 2
    while step:
        flat = jnp.where(row_ids // step % 2 == 0, pltpu.roll(flat, step, axis=1), flat)
        step //= 2
    return jnp.sum(flat.reshape(count, rows, columns), axis=1)


def split_heads(array, factor):
    lanes = lax.broadcasted_iota(jnp.int32, array.shape, 1) // (LANES // 2)
    wide = array.astype(F32) * factor
    parts = [jnp.where(lanes == head, wide, 0.0).astype(BF) for head in range(2)]
    return jnp.concatenate(parts, axis=0)


def join_heads(array):
    rows = array.shape[0] // 2
    lanes = lax.broadcasted_iota(jnp.int32, (rows, LANES), 1) // (LANES // 2)
    return jnp.where(lanes == 0, array[:rows], array[rows:]).astype(BF)


def attend_kernel(q_ref, kv_ref, window_ref, out_ref, exps_ref, total_ref):
    half, seq = q_ref.shape[0] // 2, kv_ref.shape[1]
    window = seq + 2 * half
    q = split_heads(q_ref[...], (LANES // 2) ** -0.5)
    raw = contract_cols(q, kv_ref[0])
    tiles = jnp.broadcast_to(window_ref[...][:, None], (4, half, window))
    tiles = [
        pltpu.roll(tiles[part], window - half + 1, axis=1, stride=1, stride_axis=0)[:, :seq]
        for part in range(4)
    ]
    scores = raw + jnp.concatenate(tiles, axis=0)
    exps = jnp.exp(scores - jnp.max(scores, axis=1, keepdims=True))
    inverse = 1.0 / jnp.sum(exps, axis=1, keepdims=True)
    exps = exps.astype(BF)
    exps_ref[...] = exps.reshape(exps_ref.shape)
    total_ref[...] = jnp.broadcast_to(inverse, total_ref.shape)
    out_ref[...] = join_heads(jnp.dot(exps, kv_ref[1], preferred_element_type=F32) * inverse)


def attend(queries, key_value, windows):
    rows, width = queries.shape
    pairs, seq = key_value.shape[1:3]
    work = rows * seq * width
    return pl.pallas_call(
        attend_kernel,
        grid=(pairs,),
        in_specs=[
            pl.BlockSpec((rows, LANES), lambda h: (0, h)),
            pl.BlockSpec((2, None, seq, LANES), lambda h: (0, h, 0, 0)),
            pl.BlockSpec((None, 4, windows.shape[2]), lambda h: (h, 0, 0)),
        ],
        out_specs=[
            pl.BlockSpec((rows, LANES), lambda h: (0, h)),
            pl.BlockSpec((2, rows, seq), lambda h: (h, 0, 0)),
            pl.BlockSpec((None, 2 * rows, LANES), lambda h: (h, 0, 0)),
        ],
        out_shape=[
            jax.ShapeDtypeStruct((rows, width), BF),
            jax.ShapeDtypeStruct((2 * pairs, rows, seq), BF),
            jax.ShapeDtypeStruct((pairs, 2 * rows, LANES), F32),
        ],
        compiler_params=pltpu.CompilerParams(vmem_limit_bytes=VMEM_LIMIT),
        cost_estimate=pl.CostEstimate(
            flops=8 * work,
            bytes_accessed=4 * seq * width + 4 * pairs * rows * seq,
            transcendentals=2 * pairs * rows * seq,
        ),
        name="attend",
    )(queries, key_value, windows)


def attend_back_kernel(
    exps_ref, inverse_ref, q_ref, kv_ref, grad_ref, dq_ref, dkv_ref, diag_ref
):
    half, seq = q_ref.shape[0] // 2, kv_ref.shape[1]
    factor = (LANES // 2) ** -0.5
    rows = 4 * half
    q = split_heads(q_ref[...], factor)
    inverse = inverse_ref[:, :1]
    grad = (split_heads(grad_ref[...], 1.0).astype(F32) * inverse).astype(BF)
    exps = exps_ref[...].reshape(rows, seq)
    wide = exps.astype(F32)
    prob_grad = contract_cols(grad, kv_ref[1])
    inner = jnp.sum(wide * prob_grad, axis=1, keepdims=True)
    score_grad = wide * (prob_grad - inner * inverse)
    tiles = jnp.concatenate([score_grad, jnp.zeros((rows, 2 * half), F32)], axis=1)
    sums = shear(tiles.reshape(4, half, seq + 2 * half))
    for part in range(2):
        for head in range(2):
            diag_ref[part, head : head + 1] = sums[2 * head + part : 2 * head + part + 1]
    score_grad = score_grad.astype(BF)
    query_grad = jnp.dot(score_grad, kv_ref[0], preferred_element_type=F32) * factor
    dq_ref[...] = join_heads(query_grad)
    dkv_ref[0] = contract_rows(q, score_grad).T.astype(BF)
    dkv_ref[1] = contract_rows(grad, exps).T.astype(BF)


def attend_back(exps, inverse, queries, key_value, attended_grad):
    rows, width = queries.shape
    pairs, seq = key_value.shape[1:3]
    window = seq + rows
    row_spec = pl.BlockSpec((rows, LANES), lambda h: (0, h))
    kv_spec = pl.BlockSpec((2, None, seq, LANES), lambda h: (0, h, 0, 0))
    return pl.pallas_call(
        attend_back_kernel,
        grid=(pairs,),
        in_specs=[
            pl.BlockSpec((2, rows, seq), lambda h: (h, 0, 0)),
            pl.BlockSpec((None, 2 * rows, LANES), lambda h: (h, 0, 0)),
            row_spec,
            kv_spec,
            row_spec,
        ],
        out_specs=[
            row_spec,
            kv_spec,
            pl.BlockSpec((2, None, 2, window), lambda h: (0, h, 0, 0)),
        ],
        out_shape=[
            jax.ShapeDtypeStruct((rows, width), BF),
            jax.ShapeDtypeStruct(key_value.shape, BF),
            jax.ShapeDtypeStruct((2, pairs, 2, window), F32),
        ],
        compiler_params=pltpu.CompilerParams(vmem_limit_bytes=VMEM_LIMIT),
        cost_estimate=pl.CostEstimate(
            flops=16 * rows * seq * width,
            bytes_accessed=8 * seq * width + 4 * pairs * rows * seq,
            transcendentals=0,
        ),
        name="attend_back",
    )(exps, inverse, queries, key_value, attended_grad)


def key_value_kernel(place_ref, near_ref, far_ref, gain_ref, wk_ref, wv_ref, normed_ref, kv_ref, *, half):
    tile = normed_ref.shape[0] // half
    near_blocks = near_ref.shape[0] // half
    rows = []
    for block in range(tile):
        source = place_ref[pl.program_id(0) * tile + block]
        at = pl.ds(pl.multiple_of(lax.rem(source, near_blocks) * half, half), half)
        rows.append(jnp.where(source < near_blocks, near_ref[at].astype(F32), far_ref[at].astype(F32)))
    inputs = jnp.concatenate(rows, axis=0)
    normed = (inputs * norm_scale(inputs) * gain_ref[...]).astype(BF)
    normed_ref[...] = normed
    for part, weight_ref in enumerate((wk_ref, wv_ref)):
        out = jnp.dot(normed, weight_ref[...], preferred_element_type=F32).astype(BF)
        for pair in range(kv_ref.shape[1]):
            kv_ref[part, pair] = out[:, pair * LANES : (pair + 1) * LANES]


def keys_and_values(place, near, far, gain, w_qkv, half):
    near_rows, width = near.shape
    seq = 2 * near_rows
    tile = 8 * half
    return pl.pallas_call(
        functools.partial(key_value_kernel, half=half),
        grid_spec=pltpu.PrefetchScalarGridSpec(
            num_scalar_prefetch=1,
            grid=(seq // tile,),
            in_specs=[
                pl.BlockSpec((near_rows, width), lambda r, p: (0, 0)),
                pl.BlockSpec((near_rows, width), lambda r, p: (0, 0)),
                pl.BlockSpec((1, width), lambda r, p: (0, 0)),
                pl.BlockSpec((width, width), lambda r, p: (0, 1)),
                pl.BlockSpec((width, width), lambda r, p: (0, 2)),
            ],
            out_specs=[
                pl.BlockSpec((tile, width), lambda r, p: (r, 0)),
                pl.BlockSpec((2, width // LANES, tile, LANES), lambda r, p: (0, 0, r, 0)),
            ],
        ),
        out_shape=[
            jax.ShapeDtypeStruct((seq, width), BF),
            jax.ShapeDtypeStruct((2, width // LANES, seq, LANES), BF),
        ],
        compiler_params=pltpu.CompilerParams(vmem_limit_bytes=VMEM_LIMIT),
        cost_estimate=pl.CostEstimate(
            flops=4 * seq * width * width, bytes_accessed=8 * seq * width, transcendentals=seq
        ),
        name="keys_and_values",
    )(place, near, far, gain[None], w_qkv, w_qkv)


def normed_grad_kernel(position_ref, *refs):
    *block_refs, wk_ref, wv_ref, out_ref = refs
    out = 0.0
    for part, weight_ref in enumerate((wk_ref, wv_ref)):
        rows = []
        for block_ref in block_refs:
            pairs = [block_ref[part, pair] for pair in range(block_ref.shape[1])]
            rows.append(jnp.concatenate(pairs, axis=1))
        out += contract_cols(jnp.concatenate(rows, axis=0), weight_ref[...])
    out_ref[...] = out.astype(BF)


def normed_grads(position, key_value_grad, w_qkv, half):
    width = w_qkv.shape[0]
    pairs = key_value_grad.shape[1]
    count = position.shape[0]
    rows = count * half
    step = 8

    def block_spec(at):
        return pl.BlockSpec((2, pairs, half, LANES), lambda r, p: (0, 0, p[step * r + at], 0))

    return pl.pallas_call(
        normed_grad_kernel,
        grid_spec=pltpu.PrefetchScalarGridSpec(
            num_scalar_prefetch=1,
            grid=(count // step,),
            in_specs=[
                *[block_spec(at) for at in range(step)],
                pl.BlockSpec((width, width), lambda r, p: (0, 1)),
                pl.BlockSpec((width, width), lambda r, p: (0, 2)),
            ],
            out_specs=pl.BlockSpec((step * half, width), lambda r, p: (r, 0)),
        ),
        out_shape=jax.ShapeDtypeStruct((rows, width), BF),
        compiler_params=pltpu.CompilerParams(vmem_limit_bytes=VMEM_LIMIT),
        cost_estimate=pl.CostEstimate(
            flops=4 * rows * width * width, bytes_accessed=8 * rows * width, transcendentals=0
        ),
        name="normed_grads",
    )(position, *([key_value_grad] * step), w_qkv, w_qkv)


def weight_grad_kernel(
    core_ref,
    dq_ref,
    normed_ref,
    dkv_ref,
    all_normed_ref,
    attended_ref,
    branch_ref,
    small_ref,
    hot_ref,
    diag_ref,
    kept_ref,
    given_ref,
):
    step = pl.program_id(0)
    side = kept_ref.shape[1]

    def give(total):
        left, right = total[:, :side].astype(BF), total[:, side:].astype(BF)
        rows = total.shape[0]

        @pl.when(core_ref[0] == 0)
        def _():
            kept_ref[:rows] = left
            given_ref[:rows] = right

        @pl.when(core_ref[0] != 0)
        def _():
            kept_ref[:rows] = right
            given_ref[:rows] = left

    @pl.when(step == 0)
    def _():
        give(contract_rows(dq_ref[...], normed_ref[...]))

    @pl.when((step == 1) | (step == 2))
    def _():
        pairs = [dkv_ref[pair] for pair in range(dkv_ref.shape[0])]
        give(contract_rows(jnp.concatenate(pairs, axis=1), all_normed_ref[...]))

    @pl.when(step == 3)
    def _():
        give(contract_rows(attended_ref[...], branch_ref[...]))

    @pl.when(step == 4)
    def _():
        window = diag_ref.shape[3]
        bias_grad = 0.0
        for part in range(2):
            sums = jnp.concatenate([diag_ref[part, pair] for pair in range(diag_ref.shape[1])], axis=0)
            bias_grad += lax.dot_general(
                hot_ref[:, part * window : (part + 1) * window],
                sums,
                COLS,
                precision=HIGHEST,
                preferred_element_type=F32,
            )
        buckets, heads = bias_grad.shape
        spare = jnp.zeros((buckets, small_ref.shape[1] - heads), F32)
        bias_rows = jnp.concatenate([bias_grad, spare], axis=1)
        give(jnp.concatenate([small_ref[...], bias_rows], axis=0))


def weight_grads(
    core,
    query_grad,
    normed_one,
    key_value_grad,
    all_normed,
    attended,
    branch_grad,
    small,
    bucket_hot,
    diagonals,
    spare,
):
    rows, width = normed_one.shape
    seq = all_normed.shape[0]
    total = 4 * width + small.shape[0] + bucket_hot.shape[0] + spare
    row_spec = pl.BlockSpec((rows, width), lambda t, p: (0, 0))
    out_spec = pl.BlockSpec((width, width // 2), lambda t, p: (t, 0))
    out_shape = jax.ShapeDtypeStruct((total, width // 2), BF)
    return pl.pallas_call(
        weight_grad_kernel,
        grid_spec=pltpu.PrefetchScalarGridSpec(
            num_scalar_prefetch=1,
            grid=(5,),
            in_specs=[
                row_spec,
                row_spec,
                pl.BlockSpec(
                    (None, width // LANES, seq, LANES), lambda t, p: (jnp.clip(t - 1, 0, 1), 0, 0, 0)
                ),
                pl.BlockSpec((seq, width), lambda t, p: (0, 0)),
                row_spec,
                row_spec,
                pl.BlockSpec(small.shape, lambda t, p: (0, 0)),
                pl.BlockSpec(bucket_hot.shape, lambda t, p: (0, 0)),
                pl.BlockSpec(diagonals.shape, lambda t, p: (0, 0, 0, 0)),
            ],
            out_specs=[out_spec, out_spec],
        ),
        out_shape=[out_shape, out_shape],
        compiler_params=pltpu.CompilerParams(vmem_limit_bytes=VMEM_LIMIT),
        cost_estimate=pl.CostEstimate(
            flops=4 * seq * width * width, bytes_accessed=10 * seq * width, transcendentals=0
        ),
        name="weight_grads",
    )(
        core,
        query_grad,
        normed_one,
        key_value_grad,
        all_normed,
        attended,
        branch_grad,
        small,
        bucket_hot,
        diagonals,
    )


def whole_grad_kernel(side_ref, half_ref, weight_ref, *refs):
    grad_ref, product_ref, out_ref = refs[-3:]
    step = pl.program_id(0)
    last = pl.num_programs(0) - 1
    half = half_ref[...].astype(F32)

    @pl.when(step < last)
    def _():
        grad = half.T
        grad_ref[...] = grad
        product = jnp.sum(grad * weight_ref[...].astype(F32), axis=1, keepdims=True)
        product = jnp.broadcast_to(product, product_ref.shape)

        @pl.when(step == 0)
        def _():
            product_ref[...] = product

        @pl.when(step > 0)
        def _():
            product_ref[...] += product

    @pl.when(step == last)
    def _():
        out_ref[...] = half


def whole_grad(side, half_sums, weight, held):
    width, columns = weight.shape
    half = half_sums.shape[1]
    steps = columns // width + 1

    def tile_map(t, p):
        return (p[0], jnp.minimum(t, steps - 2))

    return pl.pallas_call(
        whole_grad_kernel,
        grid_spec=pltpu.PrefetchScalarGridSpec(
            num_scalar_prefetch=1,
            grid=(steps,),
            in_specs=[
                pl.BlockSpec((width, half), lambda t, p: (t, 0)),
                pl.BlockSpec((half, width), tile_map),
                *[pl.BlockSpec(memory_space=pl.ANY) for _ in held],
            ],
            out_specs=[
                pl.BlockSpec((half, width), tile_map),
                pl.BlockSpec((half, LANES), lambda t, p: (p[0], 0)),
                pl.BlockSpec((width, half), lambda t, p: (0, p[0])),
            ],
        ),
        out_shape=[
            jax.ShapeDtypeStruct((width, columns), F32),
            jax.ShapeDtypeStruct((width, LANES), F32),
            jax.ShapeDtypeStruct((width, width), F32),
        ],
        input_output_aliases={3 + at: at for at in range(len(held))},
        compiler_params=pltpu.CompilerParams(vmem_limit_bytes=VMEM_LIMIT),
        cost_estimate=pl.CostEstimate(
            flops=width * columns, bytes_accessed=4 * width * columns, transcendentals=0
        ),
        name="whole_grad",
    )(side, half_sums, weight, *held)


def expert_rows(x_ref, cot_ref):
    width = cot_ref.shape[-1]
    rows = x_ref.shape[0] * x_ref.shape[1]
    rows_in = x_ref[...].reshape(rows, x_ref.shape[2])
    gate = jnp.sum(rows_in[:, width:].astype(F32), axis=1, keepdims=True)
    slot_grad = (cot_ref[...].reshape(rows, width).astype(F32) * gate).astype(BF)
    return rows_in[:, :width], slot_grad


def high_and_low(column):
    high = column.astype(BF).astype(F32)
    lanes = lax.broadcasted_iota(jnp.int32, (column.shape[0], LANES), 1)
    wide = jnp.where(lanes == 0, high, jnp.where(lanes == 1, column - high, 0.0))
    return wide.astype(BF)


def write_weight_grads(x, slot_grad, activated, pre_grad, grad_ref):
    grad_in = contract_rows(x, pre_grad).astype(BF)
    grad_out = contract_rows(activated, slot_grad).astype(BF)
    slices, hidden = grad_ref.shape[0], grad_ref.shape[1] // 2
    for index in range(slices):
        columns = grad_in[:, index * hidden : (index + 1) * hidden]
        grad_ref[index, :hidden, :hidden] = columns[:hidden]
        grad_ref[index, :hidden, hidden:] = columns[hidden:]
        grad_ref[index, hidden:] = grad_out[index * hidden : (index + 1) * hidden]


def pack_kernel(in_ref, out_ref, packed_ref):
    hidden = out_ref.shape[0]
    packed_ref[:hidden, :hidden] = in_ref[:hidden]
    packed_ref[:hidden, hidden:] = in_ref[hidden:]
    packed_ref[hidden:] = out_ref[...]


def packed_weights(w_in, w_out):
    experts, width, hidden = w_in.shape
    return pl.pallas_call(
        pack_kernel,
        grid=(experts,),
        in_specs=[
            pl.BlockSpec((None, width, hidden), lambda e: (e, 0, 0)),
            pl.BlockSpec((None, hidden, width), lambda e: (e, 0, 0)),
        ],
        out_specs=pl.BlockSpec((None, 2 * hidden, width), lambda e: (e, 0, 0)),
        out_shape=jax.ShapeDtypeStruct((experts, 2 * hidden, width), BF),
        compiler_params=pltpu.CompilerParams(vmem_limit_bytes=VMEM_LIMIT),
        name="packed_weights",
    )(w_in, w_out)


def slice_weights(weight_ref):
    slices, hidden = weight_ref.shape[0], weight_ref.shape[1] // 2
    weights = [weight_ref[index] for index in range(slices)]
    tops = [weight[:hidden] for weight in weights]
    tops = [jnp.concatenate([top[:, :hidden], top[:, hidden:]], axis=0) for top in tops]
    weight_out = jnp.concatenate([weight[hidden:] for weight in weights], axis=0)
    return jnp.concatenate(tops, axis=1), weight_out


def expert_kernel(
    x_ref,
    cot_ref,
    weight_ref,
    dx_ref,
    ret_ref,
    first_grad_ref,
    act_ref,
    pre_grad_ref,
    ret_sum,
    dx_sum,
):
    part = pl.program_id(1)
    width = cot_ref.shape[-1]
    x, slot_grad = expert_rows(x_ref, cot_ref)
    weight_in, weight_out = slice_weights(weight_ref)
    pre = jnp.dot(x, weight_in, preferred_element_type=F32)
    act_grad = contract_cols(slot_grad, weight_out)
    cumulative = 0.5 * (1.0 + lax.erf(pre * 0.7071067811865476))
    activated = (pre * cumulative).astype(BF)
    slope = cumulative + pre * (jnp.exp(-0.5 * pre * pre) * 0.3989422804014327)
    pre_grad = (act_grad * slope).astype(BF)
    returned = jnp.dot(activated, weight_out, preferred_element_type=F32)
    input_grad = contract_cols(pre_grad, weight_in)

    @pl.when(pl.program_id(0) == 0)
    def _():
        write_weight_grads(x, slot_grad, activated, pre_grad, first_grad_ref)

    @pl.when(pl.program_id(0) > 0)
    def _():
        act_ref[...] = activated
        pre_grad_ref[...] = pre_grad

    @pl.when(part == 0)
    def _():
        ret_sum[...] = returned
        dx_sum[...] = input_grad

    @pl.when(part > 0)
    def _():
        ret_sum[...] += returned
        dx_sum[...] += input_grad

    @pl.when(part == pl.num_programs(1) - 1)
    def _():
        shape = cot_ref.shape
        rows = shape[0] * shape[1]
        ret = ret_sum[...]
        ret_ref[...] = ret.astype(BF).reshape(shape)
        upstream = cot_ref[...].reshape(rows, width).astype(F32)
        gate_grad = high_and_low(jnp.sum(ret * upstream, axis=1, keepdims=True))
        dx_ref[:, :, :width] = dx_sum[...].astype(BF).reshape(shape)
        dx_ref[:, :, width:] = gate_grad.reshape(shape[0], shape[1], LANES)


def expert_grad_kernel(x_ref, cot_ref, act_ref, pre_grad_ref, grad_ref):
    x, slot_grad = expert_rows(x_ref, cot_ref)
    write_weight_grads(x, slot_grad, act_ref[...], pre_grad_ref[...], grad_ref)


def run_experts(x_rows, cot_rows, weights):
    devices, experts, slots, width = cot_rows.shape
    wide = x_rows.shape[3]
    parts, _, both, _ = weights.shape
    hidden = both // 2
    rows = devices * slots
    slices = 2
    steps = parts // slices

    def row_spec(columns):
        return pl.BlockSpec((devices, None, slots, columns), lambda e, w: (0, e, 0, 0))

    later = experts - 1
    hidden_spec = pl.BlockSpec(
        (None, rows, slices * hidden),
        lambda e, w: (jnp.maximum(e - 1, 0), 0, jnp.where(e == 0, 0, w)),
    )
    hidden_shape = jax.ShapeDtypeStruct((later, rows, parts * hidden), BF)
    grad_shape = jax.ShapeDtypeStruct((parts, both, width), BF)
    work = experts * rows * width * parts * hidden
    params = pltpu.CompilerParams(vmem_limit_bytes=VMEM_LIMIT)
    input_grad, returned, first_grad, activated, pre_grad = pl.pallas_call(
        expert_kernel,
        grid=(experts, steps),
        in_specs=[
            row_spec(wide),
            row_spec(width),
            pl.BlockSpec((slices, None, both, width), lambda e, w: (w, e, 0, 0)),
        ],
        out_specs=[
            row_spec(width + LANES),
            row_spec(width),
            pl.BlockSpec(
                (slices, both, width), lambda e, w: (jnp.where(e == 0, w, steps - 1), 0, 0)
            ),
            hidden_spec,
            hidden_spec,
        ],
        out_shape=[
            jax.ShapeDtypeStruct((devices, experts, slots, width + LANES), BF),
            jax.ShapeDtypeStruct((devices, experts, slots, width), BF),
            grad_shape,
            hidden_shape,
            hidden_shape,
        ],
        scratch_shapes=[pltpu.VMEM((rows, width), F32), pltpu.VMEM((rows, width), F32)],
        compiler_params=params,
        cost_estimate=pl.CostEstimate(
            flops=10 * work,
            bytes_accessed=8 * experts * rows * width + 4 * parts * experts * width * hidden,
            transcendentals=2 * experts * rows * parts * hidden,
        ),
        name="experts",
    )(x_rows, cot_rows, weights)
    weight_grads_of = [first_grad]
    for expert in range(1, experts):

        def own_rows(columns, expert=expert):
            return pl.BlockSpec((devices, None, slots, columns), lambda w: (0, expert, 0, 0))

        own_hidden = pl.BlockSpec(
            (None, rows, slices * hidden), lambda w, expert=expert: (expert - 1, 0, w)
        )
        weight_grads_of.append(
            pl.pallas_call(
                expert_grad_kernel,
                grid=(steps,),
                in_specs=[own_rows(wide), own_rows(width), own_hidden, own_hidden],
                out_specs=pl.BlockSpec((slices, both, width), lambda w: (w, 0, 0)),
                out_shape=grad_shape,
                compiler_params=params,
                cost_estimate=pl.CostEstimate(
                    flops=4 * work // experts,
                    bytes_accessed=8 * rows * width + 4 * parts * width * hidden,
                    transcendentals=0,
                ),
                name="expert_grads",
            )(x_rows, cot_rows, activated, pre_grad)
        )
    return input_grad, returned, weight_grads_of


def into_experts_kernel(
    attended_ref,
    tokens_ref,
    w_out_ref,
    gain_ref,
    w_router_ref,
    chosen_ref,
    table_ref,
    residual_ref,
    normed_ref,
    gate_ref,
    slots_ref,
):
    inputs = tokens_ref[...].astype(F32)
    residual = inputs + jnp.dot(attended_ref[...], w_out_ref[...], preferred_element_type=F32)
    residual_ref[...] = residual
    normed = (residual * norm_scale(residual) * gain_ref[...]).astype(BF)
    normed_ref[...] = normed
    logits = jnp.dot(normed, w_router_ref[...], preferred_element_type=F32)
    hots = picked_hots(chosen_ref, logits.shape)
    first, second = [jnp.sum(hot * logits, axis=1, keepdims=True) for hot in hots]
    peak = jnp.maximum(first, second)
    first, second = jnp.exp(first - peak), jnp.exp(second - peak)
    gates = [first / (first + second), second / (first + second)]
    lanes = lax.broadcasted_iota(jnp.int32, gate_ref.shape, 1)
    gate_ref[...] = jnp.where(lanes == 0, gates[0], jnp.where(lanes == 1, gates[1], 0.0))
    picks = [jnp.concatenate([normed, high_and_low(gate)], axis=1) for gate in gates]
    slots_ref[...] = contract_rows(table_ref[...], jnp.concatenate(picks, axis=0)).astype(BF)


def picked_hots(chosen_ref, shape):
    ids = lax.broadcasted_iota(jnp.int32, shape, 1)
    return [jnp.where(chosen_ref[:, pick : pick + 1] == ids, 1.0, 0.0) for pick in range(2)]


def into_experts(attended, tokens, w_attn_out, gain, w_router, chosen, table):
    rows, width = attended.shape
    return pl.pallas_call(
        into_experts_kernel,
        out_shape=[
            jax.ShapeDtypeStruct((rows, width), F32),
            jax.ShapeDtypeStruct((rows, width), BF),
            jax.ShapeDtypeStruct((rows, LANES), F32),
            jax.ShapeDtypeStruct((table.shape[1], width + LANES), BF),
        ],
        compiler_params=pltpu.CompilerParams(vmem_limit_bytes=VMEM_LIMIT),
        name="into_experts",
    )(attended, tokens, w_attn_out, gain[None], w_router, chosen, table)


def out_of_experts_kernel(
    grads_ref,
    table_ref,
    gate_ref,
    chosen_ref,
    normed_ref,
    residual_ref,
    cot_ref,
    gain_ref,
    w_router_ref,
    w_out_ref,
    mixed_ref,
    branch_ref,
    attended_grad_ref,
    small_ref,
):
    rows, width = residual_ref.shape
    table = table_ref[...]
    grads = jnp.dot(table, grads_ref[...], preferred_element_type=F32)
    gate_grads = jnp.sum(grads[:, width:], axis=1, keepdims=True)
    gate_grads = [gate_grads[:rows], gate_grads[rows:]]
    gates = [gate_ref[:, :1], gate_ref[:, 1:2]]
    inner = gates[0] * gate_grads[0] + gates[1] * gate_grads[1]
    hots = picked_hots(chosen_ref, (rows, w_router_ref.shape[1]))
    logit_grad = sum(
        hot * (gate * (gate_grad - inner)) for hot, gate, gate_grad in zip(hots, gates, gate_grads)
    )
    normed = normed_ref[...].astype(F32)
    w_router = w_router_ref[...].astype(F32)
    w_router_grad = lax.dot_general(
        logit_grad, normed, ROWS, precision=HIGHEST, preferred_element_type=F32
    )
    router_back = lax.dot_general(
        logit_grad, w_router, COLS, precision=HIGHEST, preferred_element_type=F32
    )
    normed_grad = grads[:rows, :width] + grads[rows:, :width] + router_back
    residual = residual_ref[...]
    norm_part, gain_grad = norm_backward(
        residual, norm_scale(residual), gain_ref[...], normed_grad
    )
    mixed = cot_ref[...].astype(F32) + norm_part
    mixed_ref[...] = mixed
    branch = mixed.astype(BF)
    branch_ref[...] = branch
    attended_grad_ref[...] = contract_cols(branch, w_out_ref[...]).astype(BF)
    experts = w_router_grad.shape[0]
    small_ref[:experts] = w_router_grad
    tail = small_ref.shape[0] - experts
    first = lax.broadcasted_iota(jnp.int32, (tail, width), 0) == 0
    small_ref[experts:] = jnp.where(first, gain_grad[None], 0.0)


def out_of_experts(
    grads, table, gates, chosen, normed, residual, cotangent, gain, w_router, w_attn_out
):
    rows, width = residual.shape
    return pl.pallas_call(
        out_of_experts_kernel,
        out_shape=[
            jax.ShapeDtypeStruct((rows, width), F32),
            jax.ShapeDtypeStruct((rows, width), BF),
            jax.ShapeDtypeStruct((rows, width), BF),
            jax.ShapeDtypeStruct((w_router.shape[1] + 8, width), F32),
        ],
        compiler_params=pltpu.CompilerParams(vmem_limit_bytes=VMEM_LIMIT),
        name="out_of_experts",
    )(grads, table, gates, chosen, normed, residual, cotangent, gain[None], w_router, w_attn_out)


def on_device(
    tokens,
    gain_attn,
    w_qkv,
    rel_bias,
    w_attn_out,
    gain_ffn,
    w_router,
    w_in,
    w_out,
    routes,
    pair_order,
    bucket_table,
    cotangent,
):
    tok_rows = tokens.shape[1]
    model_width = tokens.shape[2]
    head_count = rel_bias.shape[1]
    bucket_count = rel_bias.shape[0]
    ctx_count = lax.axis_size(CTX)
    half = tok_rows // 2
    blocks = 2 * ctx_count
    seq = half * blocks
    window = seq + 2 * half
    head_pairs = head_count // 2
    local_experts = w_in.shape[0]
    experts = w_router.shape[1]
    capacity = 4 * tok_rows // experts
    device_slots = local_experts * capacity
    expert_devices = lax.axis_size(EXPERT_AXES)
    copies = expert_devices // ctx_count

    near_tokens = spread(tokens[0], SAME_CORE)
    hidden = w_in.shape[2]
    weights = lax.all_gather(packed_weights(w_in, w_out), "x", axis=0)

    chosen = routes[0].T
    expert_ids = jnp.arange(experts, dtype=jnp.int32)
    flat_expert = chosen.reshape(2 * tok_rows)
    member = flat_expert[:, None] == expert_ids[None, :]
    picks = jnp.arange(2 * tok_rows, dtype=jnp.int32)
    before = (picks[:, None] > picks[None, :]).astype(BF)
    counts = jnp.dot(before, member.astype(BF), preferred_element_type=F32)
    slot_rank = jnp.sum(jnp.where(member, counts, 0.0), axis=1).astype(jnp.int32)
    owner_index = flat_expert // local_experts
    slot_of = (flat_expert % local_experts) * capacity + slot_rank
    slot_ids = jnp.arange(expert_devices * device_slots, dtype=jnp.int32)
    slot_hot = (owner_index[:, None] == (slot_ids // (copies * device_slots))[None, :]) & (
        slot_of[:, None] == (slot_ids % device_slots)[None, :]
    )
    slot_table = slot_hot.astype(BF)
    token_table = slot_table[:tok_rows] + slot_table[tok_rows:]

    def to_slots(slots):
        arrived = exchange(slots.reshape(expert_devices, device_slots, -1), EXPERT_AXES)
        return arrived.reshape(expert_devices, local_experts, capacity, -1)

    cot_slots = contract_rows(token_table, cotangent[0]).astype(BF)

    ctx_ids = jnp.arange(ctx_count, dtype=jnp.int32)
    my_core = lax.axis_index("core")
    near = (ctx_ids % 2) == my_core
    lies = 2 * (jnp.where(near, 0, ctx_count // 2) + ctx_ids // 2)
    block_ids = jnp.arange(blocks, dtype=jnp.int32)[:, None]
    place = jnp.sum(
        jnp.where(pair_order[None, :] == block_ids, lies[None, :], 0)
        + jnp.where(blocks - 1 - pair_order[None, :] == block_ids, lies[None, :] + 1, 0),
        axis=1,
        dtype=jnp.int32,
    )
    positions = jnp.sum(
        jnp.where(
            2 * (block_ids // 2) == lies[None, :],
            jnp.where(block_ids % 2 == 0, pair_order[None, :], blocks - 1 - pair_order[None, :]),
            0,
        ),
        axis=1,
        dtype=jnp.int32,
    )
    my_pair = jnp.sum(jnp.where(ctx_ids == lax.axis_index(CTX), pair_order, 0))
    reversed_table = jnp.pad(bucket_table[::-1], (0, window - half), constant_values=-1)
    diagonal_bucket = jnp.stack(
        [
            lax.dynamic_slice(reversed_table, (seq - half - block * half,), (window,))
            for block in (my_pair, blocks - 1 - my_pair)
        ]
    ).reshape(1, 2 * window)
    bucket_ids = jnp.arange(bucket_count, dtype=jnp.int32)
    bucket_hot = (diagonal_bucket == bucket_ids[:, None]).astype(F32)
    windows = lax.dot_general(rel_bias, bucket_hot, ROWS, precision=HIGHEST)
    windows = jnp.where(diagonal_bucket >= 0, windows, MASKED)
    windows = windows.reshape(head_pairs, 4, window)

    inputs = tokens[0].astype(F32)
    scale_one = norm_scale(inputs)
    normed_one = (inputs * scale_one * gain_attn).astype(BF)
    w_q = w_qkv[:, :model_width]
    queries = jnp.dot(normed_one, w_q, preferred_element_type=F32).astype(BF)
    near_tokens, queries, windows, place, slot_table, cot_slots = lax.optimization_barrier(
        (near_tokens, queries, windows, place, slot_table, cot_slots)
    )
    cot_rows = to_slots(cot_slots)
    near_tokens = near_tokens.reshape(seq // 2, model_width)
    far_tokens = lax.ppermute(near_tokens, "core", SWAP)
    all_normed, key_value = keys_and_values(
        place, near_tokens, far_tokens, gain_attn, w_qkv, half
    )
    attended, exps, inverse = attend(queries, key_value, windows)

    residual_one, normed_two, gates, slots = into_experts(
        attended, tokens[0], w_attn_out, gain_ffn, w_router, routes[0], slot_table
    )
    x_rows = to_slots(slots)
    input_grad, returned, parts = run_experts(x_rows, cot_rows, weights)

    def from_experts(rows):
        rows = exchange(rows.reshape(expert_devices, device_slots, rows.shape[3]), EXPERT_AXES)
        return rows.reshape(expert_devices * device_slots, rows.shape[2])

    input_grad = from_experts(input_grad)
    later_parts, input_grad, returned, bucket_hot = lax.optimization_barrier(
        (parts[1:], input_grad, returned, bucket_hot)
    )
    shares = [
        lax.psum_scatter(part, "x", scatter_dimension=0) for part in (parts[0], *later_parts)
    ]
    returned = from_experts(returned)

    mixed_grad, branch_grad, attended_grad, small = out_of_experts(
        input_grad,
        slot_table,
        gates,
        routes[0],
        normed_two,
        residual_one,
        cotangent[0],
        gain_ffn,
        w_router,
        w_attn_out,
    )

    query_grad, key_value_grad, diagonals = attend_back(
        exps, inverse, queries, key_value, attended_grad
    )
    query_grad, returned = lax.optimization_barrier((query_grad, returned))

    core = jnp.reshape(my_core, (1,)).astype(jnp.int32)
    side = model_width // 2
    spare = -(4 * model_width + small.shape[0] + bucket_count) % (8 * lax.axis_size(CHIPS))
    kept, given = weight_grads(
        core,
        query_grad,
        normed_one,
        key_value_grad,
        all_normed,
        attended,
        branch_grad,
        small,
        bucket_hot,
        diagonals,
        spare,
    )
    key_value_grad, kept, given, returned = lax.optimization_barrier(
        (key_value_grad, kept, given, returned)
    )
    share = half_share(kept, given)
    picked = jnp.dot(slot_table, returned, preferred_element_type=F32)
    mixture = gates[:, :1] * picked[:tok_rows] + gates[:, 1:2] * picked[tok_rows:]
    layer_out = (residual_one + mixture).astype(BF)[None]

    far_grad = normed_grads(positions[blocks // 2 :], key_value_grad, w_qkv, half)
    near_grad = normed_grads(positions[: blocks // 2], key_value_grad, w_qkv, half)
    near_grad = near_grad.astype(F32) + lax.ppermute(far_grad, "core", SWAP).astype(F32)
    near_grad = near_grad.astype(BF).reshape(ctx_count // 2, tok_rows, model_width)
    query_part = contract_cols(query_grad, w_q)
    share, near_grad, query_part, layer_out, shares = lax.optimization_barrier(
        (share, near_grad, query_part, layer_out, shares)
    )

    mine = spread(share, CHIPS).reshape(-1, side)
    shares = jnp.stack(shares).astype(F32)
    grad_w_in = jnp.concatenate([shares[:, :hidden, :hidden], shares[:, :hidden, hidden:]], axis=1)
    grad_w_out = shares[:, hidden:]
    mine, near_grad, grad_w_in, grad_w_out = lax.optimization_barrier(
        (mine, near_grad, grad_w_in, grad_w_out)
    )
    other = lax.ppermute(mine, "core", SWAP)
    row_grads = exchange(near_grad, SAME_CORE)
    held = whole_grad(core, mine, w_qkv, ())
    whole = whole_grad(1 - core, other, w_qkv, held)
    sum_w_qkv, products, sum_w_attn_out = whole
    sum_gain_attn = products[:, 0] / gain_attn
    rows = slice(4 * model_width, 4 * model_width + small.shape[0] + bucket_count)
    left = jnp.where(my_core == 0, mine[rows], other[rows])
    right = jnp.where(my_core == 0, other[rows], mine[rows])
    sums = jnp.concatenate([left, right], axis=1).astype(F32)
    sum_w_router, sum_gain_ffn = sums[:experts].T, sums[experts]
    sum_rel_bias = sums[small.shape[0] :, :head_count]
    row_grads, sum_w_qkv, sum_gain_attn, sum_w_router, sum_gain_ffn, sum_rel_bias = (
        lax.optimization_barrier(
            (row_grads, sum_w_qkv, sum_gain_attn, sum_w_router, sum_gain_ffn, sum_rel_bias)
        )
    )
    normed_one_grad = jnp.sum(row_grads.astype(F32), axis=0) + query_part
    input_norm_grad, _ = norm_backward(inputs, scale_one, gain_attn, normed_one_grad)
    grad_tokens = (mixed_grad + input_norm_grad)[None]
    return (
        layer_out,
        grad_tokens,
        sum_gain_attn,
        sum_w_qkv,
        sum_rel_bias,
        sum_w_attn_out,
        sum_gain_ffn,
        sum_w_router,
        grad_w_in,
        grad_w_out,
    )


def solution(mesh):
    split_mesh = Mesh(mesh.devices.reshape(SPLIT), EVERY)
    in_specs = (
        P(WSH, CTX, None),
        P(),
        P(),
        P(),
        P(),
        P(),
        P(),
        P(CTX, None, WSH),
        P(CTX, WSH, None),
        P(WSH, CTX, None),
        P(),
        P(),
        P(WSH, CTX, None),
    )
    out_specs = (
        P(WSH, CTX, None),
        P(WSH, CTX, None),
        P(),
        P(),
        P(),
        P(),
        P(),
        P(),
        P(CTX, None, WSH),
        P(CTX, WSH, None),
    )
    return jax.shard_map(
        on_device, mesh=split_mesh, in_specs=in_specs, out_specs=out_specs, check_vma=False
    )
```

```python
import functools

import jax
import jax.numpy as jnp
from jax import lax
from jax.experimental import pallas as pl
from jax.experimental.pallas import tpu as pltpu
from jax.sharding import Mesh
from jax.sharding import PartitionSpec as P

BF = jnp.bfloat16
F32 = jnp.float32
EPSILON = 1e-06
HIGHEST = lax.Precision.HIGHEST
MASKED = -1e30
ROWS = (((0,), (0,)), ((), ()))
COLS = (((1,), (1,)), ((), ()))
LANES = 128
VMEM_LIMIT = 58 * 1024 * 1024
SPLIT = (2, 4, 2, 2, 4)
EVERY = ("ya", "z", "core", "yb", "x")
CTX = ("ya", "z", "core")
WSH = ("yb", "x")
SAME_CORE = ("ya", "z")
CHIPS = ("ya", "z", "yb", "x")
EXPERT_AXES = ("ya", "z", "core", "yb")
SWAP = ((0, 1), (1, 0))


def norm_scale(values):
    return lax.rsqrt(jnp.mean(values * values, axis=-1, keepdims=True) + EPSILON)


def norm_backward(values, scale_vector, gain_vector, upstream):
    weighted = upstream * gain_vector
    inner_mean = jnp.mean(weighted * values, axis=-1, keepdims=True)
    grad_input = (
        scale_vector * weighted - values * scale_vector * scale_vector * scale_vector * inner_mean
    )
    grad_gain = jnp.sum(upstream * values * scale_vector, axis=0)
    return (grad_input, grad_gain)


def contract_rows(left_matrix, right_matrix):
    return lax.dot_general(left_matrix, right_matrix, ROWS, preferred_element_type=F32)


def contract_cols(left_matrix, right_matrix):
    return lax.dot_general(left_matrix, right_matrix, COLS, preferred_element_type=F32)


def exchange(array, axes):
    return lax.all_to_all(array, axes, split_axis=0, concat_axis=0, tiled=True)


def spread(array, axes):
    return exchange(jnp.broadcast_to(array[None], (lax.axis_size(axes), *array.shape)), axes)


def chip_share(parts):
    sums = [(kept.astype(F32) + got.astype(F32)).astype(BF) for kept, got in parts]
    total = jnp.concatenate(sums, axis=0)
    for axes in (CHIPS[:-1], CHIPS[-1]):
        count = lax.axis_size(axes)
        pieces = total.reshape(count, total.shape[0] // count, total.shape[1])
        total = jnp.sum(exchange(pieces, axes).astype(F32), axis=0).astype(BF)
    return total


def shear(tiles):
    count, rows, columns = tiles.shape
    while rows > 8:
        half = rows // 2
        moved = pltpu.roll(tiles[:, :half].reshape(count * half, columns), half, axis=1)
        tiles = moved.reshape(count, half, columns) + tiles[:, half:]
        rows = half
    flat = tiles.reshape(count * rows, columns)
    row_ids = lax.broadcasted_iota(jnp.int32, flat.shape, 0)
    step = rows // 2
    while step:
        flat = jnp.where(row_ids // step % 2 == 0, pltpu.roll(flat, step, axis=1), flat)
        step //= 2
    return jnp.sum(flat.reshape(count, rows, columns), axis=1)


def split_heads(array, factor):
    lanes = lax.broadcasted_iota(jnp.int32, array.shape, 1) // (LANES // 2)
    wide = array.astype(F32) * factor
    parts = [jnp.where(lanes == head, wide, 0.0).astype(BF) for head in range(2)]
    return jnp.concatenate(parts, axis=0)


def join_heads(array):
    rows = array.shape[0] // 2
    lanes = lax.broadcasted_iota(jnp.int32, (rows, LANES), 1) // (LANES // 2)
    return jnp.where(lanes == 0, array[:rows], array[rows:]).astype(BF)


def attend_kernel(q_ref, kv_ref, window_ref, out_ref, exps_ref, total_ref):
    half, seq = q_ref.shape[0] // 2, kv_ref.shape[1]
    window = seq + 2 * half
    q = split_heads(q_ref[...], (LANES // 2) ** -0.5)
    raw = contract_cols(q, kv_ref[0])
    tiles = jnp.broadcast_to(window_ref[...][:, None], (4, half, window))
    tiles = [
        pltpu.roll(tiles[part], window - half + 1, axis=1, stride=1, stride_axis=0)[:, :seq]
        for part in range(4)
    ]
    scores = raw + jnp.concatenate(tiles, axis=0)
    exps = jnp.exp(scores - jnp.max(scores, axis=1, keepdims=True))
    inverse = 1.0 / jnp.sum(exps, axis=1, keepdims=True)
    exps = exps.astype(BF)
    exps_ref[...] = exps.reshape(exps_ref.shape)
    total_ref[...] = jnp.broadcast_to(inverse, total_ref.shape)
    out_ref[...] = join_heads(jnp.dot(exps, kv_ref[1], preferred_element_type=F32) * inverse)


def attend(queries, key_value, windows):
    rows, width = queries.shape
    pairs, seq = key_value.shape[1:3]
    work = rows * seq * width
    return pl.pallas_call(
        attend_kernel,
        grid=(pairs,),
        in_specs=[
            pl.BlockSpec((rows, LANES), lambda h: (0, h)),
            pl.BlockSpec((2, None, seq, LANES), lambda h: (0, h, 0, 0)),
            pl.BlockSpec((None, 4, windows.shape[2]), lambda h: (h, 0, 0)),
        ],
        out_specs=[
            pl.BlockSpec((rows, LANES), lambda h: (0, h)),
            pl.BlockSpec((2, rows, seq), lambda h: (h, 0, 0)),
            pl.BlockSpec((None, 2 * rows, LANES), lambda h: (h, 0, 0)),
        ],
        out_shape=[
            jax.ShapeDtypeStruct((rows, width), BF),
            jax.ShapeDtypeStruct((2 * pairs, rows, seq), BF),
            jax.ShapeDtypeStruct((pairs, 2 * rows, LANES), F32),
        ],
        compiler_params=pltpu.CompilerParams(vmem_limit_bytes=VMEM_LIMIT),
        cost_estimate=pl.CostEstimate(
            flops=8 * work,
            bytes_accessed=4 * seq * width + 4 * pairs * rows * seq,
            transcendentals=2 * pairs * rows * seq,
        ),
        name="attend",
    )(queries, key_value, windows)


def attend_back_kernel(
    exps_ref, inverse_ref, q_ref, kv_ref, grad_ref, dq_ref, dkv_ref, diag_ref
):
    half, seq = q_ref.shape[0] // 2, kv_ref.shape[1]
    factor = (LANES // 2) ** -0.5
    rows = 4 * half
    q = split_heads(q_ref[...], factor)
    inverse = inverse_ref[:, :1]
    grad = (split_heads(grad_ref[...], 1.0).astype(F32) * inverse).astype(BF)
    exps = exps_ref[...].reshape(rows, seq)
    wide = exps.astype(F32)
    prob_grad = contract_cols(grad, kv_ref[1])
    inner = jnp.sum(wide * prob_grad, axis=1, keepdims=True)
    score_grad = wide * (prob_grad - inner * inverse)
    tiles = jnp.concatenate([score_grad, jnp.zeros((rows, 2 * half), F32)], axis=1)
    sums = shear(tiles.reshape(4, half, seq + 2 * half))
    for part in range(2):
        for head in range(2):
            diag_ref[part, head : head + 1] = sums[2 * head + part : 2 * head + part + 1]
    score_grad = score_grad.astype(BF)
    query_grad = jnp.dot(score_grad, kv_ref[0], preferred_element_type=F32) * factor
    dq_ref[...] = join_heads(query_grad)
    dkv_ref[0] = contract_rows(q, score_grad).astype(BF)
    dkv_ref[1] = contract_rows(grad, exps).astype(BF)


def attend_back(exps, inverse, queries, key_value, attended_grad):
    rows, width = queries.shape
    pairs, seq = key_value.shape[1:3]
    window = seq + rows
    row_spec = pl.BlockSpec((rows, LANES), lambda h: (0, h))
    kv_spec = pl.BlockSpec((2, None, seq, LANES), lambda h: (0, h, 0, 0))
    return pl.pallas_call(
        attend_back_kernel,
        grid=(pairs,),
        in_specs=[
            pl.BlockSpec((2, rows, seq), lambda h: (h, 0, 0)),
            pl.BlockSpec((None, 2 * rows, LANES), lambda h: (h, 0, 0)),
            row_spec,
            kv_spec,
            row_spec,
        ],
        out_specs=[
            row_spec,
            pl.BlockSpec((2, None, LANES, seq), lambda h: (0, h, 0, 0)),
            pl.BlockSpec((2, None, 2, window), lambda h: (0, h, 0, 0)),
        ],
        out_shape=[
            jax.ShapeDtypeStruct((rows, width), BF),
            jax.ShapeDtypeStruct((2, pairs, LANES, seq), BF),
            jax.ShapeDtypeStruct((2, pairs, 2, window), F32),
        ],
        compiler_params=pltpu.CompilerParams(vmem_limit_bytes=VMEM_LIMIT),
        cost_estimate=pl.CostEstimate(
            flops=16 * rows * seq * width,
            bytes_accessed=8 * seq * width + 4 * pairs * rows * seq,
            transcendentals=0,
        ),
        name="attend_back",
    )(exps, inverse, queries, key_value, attended_grad)


def key_value_kernel(place_ref, near_ref, far_ref, gain_ref, wk_ref, wv_ref, normed_ref, kv_ref, *, half):
    tile = normed_ref.shape[0] // half
    near_blocks = near_ref.shape[0] // half
    rows = []
    for block in range(tile):
        source = place_ref[pl.program_id(0) * tile + block]
        at = pl.ds(pl.multiple_of(lax.rem(source, near_blocks) * half, half), half)
        rows.append(jnp.where(source < near_blocks, near_ref[at].astype(F32), far_ref[at].astype(F32)))
    inputs = jnp.concatenate(rows, axis=0)
    normed = (inputs * norm_scale(inputs) * gain_ref[...]).astype(BF)
    normed_ref[...] = normed
    for part, weight_ref in enumerate((wk_ref, wv_ref)):
        out = jnp.dot(normed, weight_ref[...], preferred_element_type=F32).astype(BF)
        for pair in range(kv_ref.shape[1]):
            kv_ref[part, pair] = out[:, pair * LANES : (pair + 1) * LANES]


def keys_and_values(place, near, far, gain, w_qkv, half):
    near_rows, width = near.shape
    seq = 2 * near_rows
    tile = 8 * half
    return pl.pallas_call(
        functools.partial(key_value_kernel, half=half),
        grid_spec=pltpu.PrefetchScalarGridSpec(
            num_scalar_prefetch=1,
            grid=(seq // tile,),
            in_specs=[
                pl.BlockSpec((near_rows, width), lambda r, p: (0, 0)),
                pl.BlockSpec((near_rows, width), lambda r, p: (0, 0)),
                pl.BlockSpec((1, width), lambda r, p: (0, 0)),
                pl.BlockSpec((width, width), lambda r, p: (0, 1)),
                pl.BlockSpec((width, width), lambda r, p: (0, 2)),
            ],
            out_specs=[
                pl.BlockSpec((tile, width), lambda r, p: (r, 0)),
                pl.BlockSpec((2, width // LANES, tile, LANES), lambda r, p: (0, 0, r, 0)),
            ],
        ),
        out_shape=[
            jax.ShapeDtypeStruct((seq, width), BF),
            jax.ShapeDtypeStruct((2, width // LANES, seq, LANES), BF),
        ],
        compiler_params=pltpu.CompilerParams(vmem_limit_bytes=VMEM_LIMIT),
        cost_estimate=pl.CostEstimate(
            flops=4 * seq * width * width, bytes_accessed=8 * seq * width, transcendentals=seq
        ),
        name="keys_and_values",
    )(place, near, far, gain[None], w_qkv, w_qkv)


def normed_grad_kernel(place_ref, dkv_ref, wk_ref, wv_ref, out_ref, *, half):
    total = 0.0
    for part, weight_ref in enumerate((wk_ref, wv_ref)):
        columns = dkv_ref[part].reshape(weight_ref.shape[1], dkv_ref.shape[3])
        total += jnp.dot(weight_ref[...], columns, preferred_element_type=F32)
    total = total.T.astype(BF)
    step = total.shape[0] // half
    for block in range(step):
        target = place_ref[pl.program_id(0) * step + block]
        at = pl.ds(pl.multiple_of(target * half, half), half)
        out_ref[at] = total[block * half : (block + 1) * half]


def normed_grads(place, key_value_grad, w_qkv, half):
    width = w_qkv.shape[0]
    pairs, seq = key_value_grad.shape[1], key_value_grad.shape[3]
    tile = 8 * half
    return pl.pallas_call(
        functools.partial(normed_grad_kernel, half=half),
        grid_spec=pltpu.PrefetchScalarGridSpec(
            num_scalar_prefetch=1,
            grid=(seq // tile,),
            in_specs=[
                pl.BlockSpec((2, pairs, LANES, tile), lambda r, p: (0, 0, 0, r)),
                pl.BlockSpec((width, width), lambda r, p: (0, 1)),
                pl.BlockSpec((width, width), lambda r, p: (0, 2)),
            ],
            out_specs=pl.BlockSpec((seq, width), lambda r, p: (0, 0)),
        ),
        out_shape=jax.ShapeDtypeStruct((seq, width), BF),
        compiler_params=pltpu.CompilerParams(vmem_limit_bytes=VMEM_LIMIT),
        cost_estimate=pl.CostEstimate(
            flops=4 * seq * width * width, bytes_accessed=8 * seq * width, transcendentals=0
        ),
        name="normed_grads",
    )(place, key_value_grad, w_qkv, w_qkv)


def give_halves(core_ref, total, kept_ref, given_ref):
    rows, side = total.shape[0], kept_ref.shape[1]
    left, right = total[:, :side].astype(BF), total[:, side:].astype(BF)

    @pl.when(core_ref[0] == 0)
    def _():
        kept_ref[:rows] = left
        given_ref[:rows] = right

    @pl.when(core_ref[0] != 0)
    def _():
        kept_ref[:rows] = right
        given_ref[:rows] = left


def key_value_weight_kernel(core_ref, dkv_ref, all_normed_ref, kept_ref, given_ref):
    columns = dkv_ref[...].reshape(dkv_ref.shape[0] * LANES, dkv_ref.shape[2])
    total = jnp.dot(columns, all_normed_ref[...], preferred_element_type=F32)
    give_halves(core_ref, total, kept_ref, given_ref)


def key_value_weight_grads(core, key_value_grad, all_normed):
    seq, width = all_normed.shape
    out_spec = pl.BlockSpec((width, width // 2), lambda t, p: (t, 0))
    out_shape = jax.ShapeDtypeStruct((2 * width, width // 2), BF)
    return pl.pallas_call(
        key_value_weight_kernel,
        grid_spec=pltpu.PrefetchScalarGridSpec(
            num_scalar_prefetch=1,
            grid=(2,),
            in_specs=[
                pl.BlockSpec((None, width // LANES, LANES, seq), lambda t, p: (t, 0, 0, 0)),
                pl.BlockSpec((seq, width), lambda t, p: (0, 0)),
            ],
            out_specs=[out_spec, out_spec],
        ),
        out_shape=[out_shape, out_shape],
        compiler_params=pltpu.CompilerParams(vmem_limit_bytes=VMEM_LIMIT),
        cost_estimate=pl.CostEstimate(
            flops=4 * seq * width * width, bytes_accessed=8 * seq * width, transcendentals=0
        ),
        name="key_value_weight_grads",
    )(core, key_value_grad, all_normed)


def weight_grad_kernel(
    core_ref,
    dq_ref,
    normed_ref,
    attended_ref,
    branch_ref,
    small_ref,
    hot_ref,
    diag_ref,
    kept_ref,
    given_ref,
):
    step = pl.program_id(0)

    @pl.when(step == 0)
    def _():
        total = contract_rows(dq_ref[...], normed_ref[...])
        give_halves(core_ref, total, kept_ref, given_ref)

    @pl.when(step == 1)
    def _():
        total = contract_rows(attended_ref[...], branch_ref[...])
        give_halves(core_ref, total, kept_ref, given_ref)

    @pl.when(step == 2)
    def _():
        window = diag_ref.shape[3]
        bias_grad = 0.0
        for part in range(2):
            sums = jnp.concatenate([diag_ref[part, pair] for pair in range(diag_ref.shape[1])], axis=0)
            bias_grad += lax.dot_general(
                hot_ref[:, part * window : (part + 1) * window],
                sums,
                COLS,
                precision=HIGHEST,
                preferred_element_type=F32,
            )
        buckets, heads = bias_grad.shape
        spare = jnp.zeros((buckets, small_ref.shape[1] - heads), F32)
        bias_rows = jnp.concatenate([bias_grad, spare], axis=1)
        total = jnp.concatenate([small_ref[...], bias_rows], axis=0)
        give_halves(core_ref, total, kept_ref, given_ref)


def weight_grads(
    core, query_grad, normed_one, attended, branch_grad, small, bucket_hot, diagonals, total
):
    rows, width = normed_one.shape
    row_spec = pl.BlockSpec((rows, width), lambda t, p: (0, 0))
    out_spec = pl.BlockSpec((width, width // 2), lambda t, p: (t, 0))
    out_shape = jax.ShapeDtypeStruct((total, width // 2), BF)
    return pl.pallas_call(
        weight_grad_kernel,
        grid_spec=pltpu.PrefetchScalarGridSpec(
            num_scalar_prefetch=1,
            grid=(3,),
            in_specs=[
                row_spec,
                row_spec,
                row_spec,
                row_spec,
                pl.BlockSpec(small.shape, lambda t, p: (0, 0)),
                pl.BlockSpec(bucket_hot.shape, lambda t, p: (0, 0)),
                pl.BlockSpec(diagonals.shape, lambda t, p: (0, 0, 0, 0)),
            ],
            out_specs=[out_spec, out_spec],
        ),
        out_shape=[out_shape, out_shape],
        compiler_params=pltpu.CompilerParams(vmem_limit_bytes=VMEM_LIMIT),
        cost_estimate=pl.CostEstimate(
            flops=4 * rows * width * width, bytes_accessed=16 * rows * width, transcendentals=0
        ),
        name="weight_grads",
    )(core, query_grad, normed_one, attended, branch_grad, small, bucket_hot, diagonals)


def whole_grad_kernel(side_ref, half_ref, weight_ref, *refs):
    grad_ref, product_ref, out_ref = refs[-3:]
    step = pl.program_id(0)
    last = pl.num_programs(0) - 1
    half = half_ref[...].astype(F32)

    @pl.when(step < last)
    def _():
        grad = half.T
        grad_ref[...] = grad
        product = jnp.sum(grad * weight_ref[...].astype(F32), axis=1, keepdims=True)
        product = jnp.broadcast_to(product, product_ref.shape)

        @pl.when(step == 0)
        def _():
            product_ref[...] = product

        @pl.when(step > 0)
        def _():
            product_ref[...] += product

    @pl.when(step == last)
    def _():
        out_ref[...] = half


def whole_grad(side, half_sums, weight, held):
    width, columns = weight.shape
    half = half_sums.shape[1]
    steps = columns // width + 1

    def tile_map(t, p):
        return (p[0], jnp.minimum(t, steps - 2))

    return pl.pallas_call(
        whole_grad_kernel,
        grid_spec=pltpu.PrefetchScalarGridSpec(
            num_scalar_prefetch=1,
            grid=(steps,),
            in_specs=[
                pl.BlockSpec(
                    (width, half), lambda t, p: (jnp.where(t < steps - 1, (t + 2) % 3, 3), 0)
                ),
                pl.BlockSpec((half, width), tile_map),
                *[pl.BlockSpec(memory_space=pl.ANY) for _ in held],
            ],
            out_specs=[
                pl.BlockSpec((half, width), tile_map),
                pl.BlockSpec((half, LANES), lambda t, p: (p[0], 0)),
                pl.BlockSpec((width, half), lambda t, p: (0, p[0])),
            ],
        ),
        out_shape=[
            jax.ShapeDtypeStruct((width, columns), F32),
            jax.ShapeDtypeStruct((width, LANES), F32),
            jax.ShapeDtypeStruct((width, width), F32),
        ],
        input_output_aliases={3 + at: at for at in range(len(held))},
        compiler_params=pltpu.CompilerParams(vmem_limit_bytes=VMEM_LIMIT),
        cost_estimate=pl.CostEstimate(
            flops=width * columns, bytes_accessed=4 * width * columns, transcendentals=0
        ),
        name="whole_grad",
    )(side, half_sums, weight, *held)


def expert_rows(x_ref, cot_ref):
    width = cot_ref.shape[-1]
    rows = x_ref.shape[0] * x_ref.shape[1]
    rows_in = x_ref[...].reshape(rows, x_ref.shape[2])
    gate = jnp.sum(rows_in[:, width:].astype(F32), axis=1, keepdims=True)
    slot_grad = (cot_ref[...].reshape(rows, width).astype(F32) * gate).astype(BF)
    return rows_in[:, :width], slot_grad


def high_and_low(column):
    high = column.astype(BF).astype(F32)
    lanes = lax.broadcasted_iota(jnp.int32, (column.shape[0], LANES), 1)
    wide = jnp.where(lanes == 0, high, jnp.where(lanes == 1, column - high, 0.0))
    return wide.astype(BF)


def write_weight_grads(x, slot_grad, activated, pre_grad, grad_ref):
    grad_in = contract_rows(x, pre_grad).astype(BF)
    grad_out = contract_rows(activated, slot_grad).astype(BF)
    slices, hidden = grad_ref.shape[0], grad_ref.shape[1] // 2
    for index in range(slices):
        columns = grad_in[:, index * hidden : (index + 1) * hidden]
        grad_ref[index, :hidden, :hidden] = columns[:hidden]
        grad_ref[index, :hidden, hidden:] = columns[hidden:]
        grad_ref[index, hidden:] = grad_out[index * hidden : (index + 1) * hidden]


def pack_kernel(in_ref, out_ref, packed_ref):
    hidden = out_ref.shape[0]
    packed_ref[:hidden, :hidden] = in_ref[:hidden]
    packed_ref[:hidden, hidden:] = in_ref[hidden:]
    packed_ref[hidden:] = out_ref[...]


def packed_weights(w_in, w_out):
    experts, width, hidden = w_in.shape
    return pl.pallas_call(
        pack_kernel,
        grid=(experts,),
        in_specs=[
            pl.BlockSpec((None, width, hidden), lambda e: (e, 0, 0)),
            pl.BlockSpec((None, hidden, width), lambda e: (e, 0, 0)),
        ],
        out_specs=pl.BlockSpec((None, 2 * hidden, width), lambda e: (e, 0, 0)),
        out_shape=jax.ShapeDtypeStruct((experts, 2 * hidden, width), BF),
        compiler_params=pltpu.CompilerParams(vmem_limit_bytes=VMEM_LIMIT),
        name="packed_weights",
    )(w_in, w_out)


def slice_weights(weight_ref):
    slices, hidden = weight_ref.shape[0], weight_ref.shape[1] // 2
    weights = [weight_ref[index] for index in range(slices)]
    tops = [weight[:hidden] for weight in weights]
    tops = [jnp.concatenate([top[:, :hidden], top[:, hidden:]], axis=0) for top in tops]
    weight_out = jnp.concatenate([weight[hidden:] for weight in weights], axis=0)
    return jnp.concatenate(tops, axis=1), weight_out


def expert_kernel(
    x_ref,
    cot_ref,
    weight_ref,
    dx_ref,
    ret_ref,
    first_grad_ref,
    act_ref,
    pre_grad_ref,
    ret_sum,
    dx_sum,
):
    part = pl.program_id(1)
    width = cot_ref.shape[-1]
    x, slot_grad = expert_rows(x_ref, cot_ref)
    weight_in, weight_out = slice_weights(weight_ref)
    pre = jnp.dot(x, weight_in, preferred_element_type=F32)
    act_grad = contract_cols(slot_grad, weight_out)
    cumulative = 0.5 * (1.0 + lax.erf(pre * 0.7071067811865476))
    activated = (pre * cumulative).astype(BF)
    slope = cumulative + pre * (jnp.exp(-0.5 * pre * pre) * 0.3989422804014327)
    pre_grad = (act_grad * slope).astype(BF)
    returned = jnp.dot(activated, weight_out, preferred_element_type=F32)
    input_grad = contract_cols(pre_grad, weight_in)

    @pl.when(pl.program_id(0) == 0)
    def _():
        write_weight_grads(x, slot_grad, activated, pre_grad, first_grad_ref)

    @pl.when(pl.program_id(0) > 0)
    def _():
        act_ref[...] = activated
        pre_grad_ref[...] = pre_grad

    @pl.when(part == 0)
    def _():
        ret_sum[...] = returned
        dx_sum[...] = input_grad

    @pl.when(part > 0)
    def _():
        ret_sum[...] += returned
        dx_sum[...] += input_grad

    @pl.when(part == pl.num_programs(1) - 1)
    def _():
        shape = cot_ref.shape
        rows = shape[0] * shape[1]
        ret = ret_sum[...]
        ret_ref[...] = ret.astype(BF).reshape(shape)
        upstream = cot_ref[...].reshape(rows, width).astype(F32)
        gate_grad = high_and_low(jnp.sum(ret * upstream, axis=1, keepdims=True))
        dx_ref[:, :, :width] = dx_sum[...].astype(BF).reshape(shape)
        dx_ref[:, :, width:] = gate_grad.reshape(shape[0], shape[1], LANES)


def expert_grad_kernel(x_ref, cot_ref, act_ref, pre_grad_ref, grad_ref):
    x, slot_grad = expert_rows(x_ref, cot_ref)
    write_weight_grads(x, slot_grad, act_ref[...], pre_grad_ref[...], grad_ref)


def run_experts(x_rows, cot_rows, weights):
    devices, experts, slots, width = cot_rows.shape
    wide = x_rows.shape[3]
    parts, _, both, _ = weights.shape
    hidden = both // 2
    rows = devices * slots
    slices = 2
    steps = parts // slices

    def row_spec(columns):
        return pl.BlockSpec((devices, None, slots, columns), lambda e, w: (0, e, 0, 0))

    later = experts - 1
    hidden_spec = pl.BlockSpec(
        (None, rows, slices * hidden),
        lambda e, w: (jnp.maximum(e - 1, 0), 0, jnp.where(e == 0, 0, w)),
    )
    hidden_shape = jax.ShapeDtypeStruct((later, rows, parts * hidden), BF)
    grad_shape = jax.ShapeDtypeStruct((parts, both, width), BF)
    work = experts * rows * width * parts * hidden
    params = pltpu.CompilerParams(vmem_limit_bytes=VMEM_LIMIT)
    input_grad, returned, first_grad, activated, pre_grad = pl.pallas_call(
        expert_kernel,
        grid=(experts, steps),
        in_specs=[
            row_spec(wide),
            row_spec(width),
            pl.BlockSpec((slices, None, both, width), lambda e, w: (w, e, 0, 0)),
        ],
        out_specs=[
            row_spec(width + LANES),
            row_spec(width),
            pl.BlockSpec(
                (slices, both, width), lambda e, w: (jnp.where(e == 0, w, steps - 1), 0, 0)
            ),
            hidden_spec,
            hidden_spec,
        ],
        out_shape=[
            jax.ShapeDtypeStruct((devices, experts, slots, width + LANES), BF),
            jax.ShapeDtypeStruct((devices, experts, slots, width), BF),
            grad_shape,
            hidden_shape,
            hidden_shape,
        ],
        scratch_shapes=[pltpu.VMEM((rows, width), F32), pltpu.VMEM((rows, width), F32)],
        compiler_params=params,
        cost_estimate=pl.CostEstimate(
            flops=10 * work,
            bytes_accessed=8 * experts * rows * width + 4 * parts * experts * width * hidden,
            transcendentals=2 * experts * rows * parts * hidden,
        ),
        name="experts",
    )(x_rows, cot_rows, weights)
    weight_grads_of = [first_grad]
    for expert in range(1, experts):

        def own_rows(columns, expert=expert):
            return pl.BlockSpec((devices, None, slots, columns), lambda w: (0, expert, 0, 0))

        own_hidden = pl.BlockSpec(
            (None, rows, slices * hidden), lambda w, expert=expert: (expert - 1, 0, w)
        )
        weight_grads_of.append(
            pl.pallas_call(
                expert_grad_kernel,
                grid=(steps,),
                in_specs=[own_rows(wide), own_rows(width), own_hidden, own_hidden],
                out_specs=pl.BlockSpec((slices, both, width), lambda w: (w, 0, 0)),
                out_shape=grad_shape,
                compiler_params=params,
                cost_estimate=pl.CostEstimate(
                    flops=4 * work // experts,
                    bytes_accessed=8 * rows * width + 4 * parts * width * hidden,
                    transcendentals=0,
                ),
                name="expert_grads",
            )(x_rows, cot_rows, activated, pre_grad)
        )
    return input_grad, returned, weight_grads_of


def into_experts_kernel(
    attended_ref,
    tokens_ref,
    w_out_ref,
    gain_ref,
    w_router_ref,
    chosen_ref,
    table_ref,
    residual_ref,
    normed_ref,
    gate_ref,
    slots_ref,
):
    inputs = tokens_ref[...].astype(F32)
    residual = inputs + jnp.dot(attended_ref[...], w_out_ref[...], preferred_element_type=F32)
    residual_ref[...] = residual
    normed = (residual * norm_scale(residual) * gain_ref[...]).astype(BF)
    normed_ref[...] = normed
    logits = jnp.dot(normed, w_router_ref[...], preferred_element_type=F32)
    hots = picked_hots(chosen_ref, logits.shape)
    first, second = [jnp.sum(hot * logits, axis=1, keepdims=True) for hot in hots]
    peak = jnp.maximum(first, second)
    first, second = jnp.exp(first - peak), jnp.exp(second - peak)
    gates = [first / (first + second), second / (first + second)]
    lanes = lax.broadcasted_iota(jnp.int32, gate_ref.shape, 1)
    gate_ref[...] = jnp.where(lanes == 0, gates[0], jnp.where(lanes == 1, gates[1], 0.0))
    picks = [jnp.concatenate([normed, high_and_low(gate)], axis=1) for gate in gates]
    slots_ref[...] = contract_rows(table_ref[...], jnp.concatenate(picks, axis=0)).astype(BF)


def picked_hots(chosen_ref, shape):
    ids = lax.broadcasted_iota(jnp.int32, shape, 1)
    return [jnp.where(chosen_ref[:, pick : pick + 1] == ids, 1.0, 0.0) for pick in range(2)]


def into_experts(attended, tokens, w_attn_out, gain, w_router, chosen, table):
    rows, width = attended.shape
    return pl.pallas_call(
        into_experts_kernel,
        out_shape=[
            jax.ShapeDtypeStruct((rows, width), F32),
            jax.ShapeDtypeStruct((rows, width), BF),
            jax.ShapeDtypeStruct((rows, LANES), F32),
            jax.ShapeDtypeStruct((table.shape[1], width + LANES), BF),
        ],
        compiler_params=pltpu.CompilerParams(vmem_limit_bytes=VMEM_LIMIT),
        name="into_experts",
    )(attended, tokens, w_attn_out, gain[None], w_router, chosen, table)


def out_of_experts_kernel(
    grads_ref,
    table_ref,
    gate_ref,
    chosen_ref,
    normed_ref,
    residual_ref,
    cot_ref,
    gain_ref,
    w_router_ref,
    w_out_ref,
    mixed_ref,
    branch_ref,
    attended_grad_ref,
    small_ref,
):
    rows, width = residual_ref.shape
    table = table_ref[...]
    grads = jnp.dot(table, grads_ref[...], preferred_element_type=F32)
    gate_grads = jnp.sum(grads[:, width:], axis=1, keepdims=True)
    gate_grads = [gate_grads[:rows], gate_grads[rows:]]
    gates = [gate_ref[:, :1], gate_ref[:, 1:2]]
    inner = gates[0] * gate_grads[0] + gates[1] * gate_grads[1]
    hots = picked_hots(chosen_ref, (rows, w_router_ref.shape[1]))
    logit_grad = sum(
        hot * (gate * (gate_grad - inner)) for hot, gate, gate_grad in zip(hots, gates, gate_grads)
    )
    normed = normed_ref[...].astype(F32)
    w_router = w_router_ref[...].astype(F32)
    w_router_grad = lax.dot_general(
        logit_grad, normed, ROWS, precision=HIGHEST, preferred_element_type=F32
    )
    router_back = lax.dot_general(
        logit_grad, w_router, COLS, precision=HIGHEST, preferred_element_type=F32
    )
    normed_grad = grads[:rows, :width] + grads[rows:, :width] + router_back
    residual = residual_ref[...]
    norm_part, gain_grad = norm_backward(
        residual, norm_scale(residual), gain_ref[...], normed_grad
    )
    mixed = cot_ref[...].astype(F32) + norm_part
    mixed_ref[...] = mixed
    branch = mixed.astype(BF)
    branch_ref[...] = branch
    attended_grad_ref[...] = contract_cols(branch, w_out_ref[...]).astype(BF)
    experts = w_router_grad.shape[0]
    small_ref[:experts] = w_router_grad
    tail = small_ref.shape[0] - experts
    first = lax.broadcasted_iota(jnp.int32, (tail, width), 0) == 0
    small_ref[experts:] = jnp.where(first, gain_grad[None], 0.0)


def out_of_experts(
    grads, table, gates, chosen, normed, residual, cotangent, gain, w_router, w_attn_out
):
    rows, width = residual.shape
    return pl.pallas_call(
        out_of_experts_kernel,
        out_shape=[
            jax.ShapeDtypeStruct((rows, width), F32),
            jax.ShapeDtypeStruct((rows, width), BF),
            jax.ShapeDtypeStruct((rows, width), BF),
            jax.ShapeDtypeStruct((w_router.shape[1] + 8, width), F32),
        ],
        compiler_params=pltpu.CompilerParams(vmem_limit_bytes=VMEM_LIMIT),
        name="out_of_experts",
    )(grads, table, gates, chosen, normed, residual, cotangent, gain[None], w_router, w_attn_out)


def on_device(
    tokens,
    gain_attn,
    w_qkv,
    rel_bias,
    w_attn_out,
    gain_ffn,
    w_router,
    w_in,
    w_out,
    routes,
    pair_order,
    bucket_table,
    cotangent,
):
    tok_rows = tokens.shape[1]
    model_width = tokens.shape[2]
    head_count = rel_bias.shape[1]
    bucket_count = rel_bias.shape[0]
    ctx_count = lax.axis_size(CTX)
    half = tok_rows // 2
    blocks = 2 * ctx_count
    seq = half * blocks
    window = seq + 2 * half
    head_pairs = head_count // 2
    local_experts = w_in.shape[0]
    experts = w_router.shape[1]
    capacity = 4 * tok_rows // experts
    device_slots = local_experts * capacity
    expert_devices = lax.axis_size(EXPERT_AXES)
    copies = expert_devices // ctx_count

    near_tokens = spread(tokens[0], SAME_CORE)
    hidden = w_in.shape[2]
    weights = lax.all_gather(packed_weights(w_in, w_out), "x", axis=0)

    chosen = routes[0].T
    expert_ids = jnp.arange(experts, dtype=jnp.int32)
    flat_expert = chosen.reshape(2 * tok_rows)
    member = flat_expert[:, None] == expert_ids[None, :]
    picks = jnp.arange(2 * tok_rows, dtype=jnp.int32)
    before = (picks[:, None] > picks[None, :]).astype(BF)
    counts = jnp.dot(before, member.astype(BF), preferred_element_type=F32)
    slot_rank = jnp.sum(jnp.where(member, counts, 0.0), axis=1).astype(jnp.int32)
    owner_index = flat_expert // local_experts
    slot_of = (flat_expert % local_experts) * capacity + slot_rank
    slot_ids = jnp.arange(expert_devices * device_slots, dtype=jnp.int32)
    slot_hot = (owner_index[:, None] == (slot_ids // (copies * device_slots))[None, :]) & (
        slot_of[:, None] == (slot_ids % device_slots)[None, :]
    )
    slot_table = slot_hot.astype(BF)
    token_table = slot_table[:tok_rows] + slot_table[tok_rows:]

    def to_slots(slots):
        arrived = exchange(slots.reshape(expert_devices, device_slots, -1), EXPERT_AXES)
        return arrived.reshape(expert_devices, local_experts, capacity, -1)

    cot_slots = contract_rows(token_table, cotangent[0]).astype(BF)

    ctx_ids = jnp.arange(ctx_count, dtype=jnp.int32)
    my_core = lax.axis_index("core")
    near = (ctx_ids % 2) == my_core
    lies = 2 * (jnp.where(near, 0, ctx_count // 2) + ctx_ids // 2)
    block_ids = jnp.arange(blocks, dtype=jnp.int32)[:, None]
    place = jnp.sum(
        jnp.where(pair_order[None, :] == block_ids, lies[None, :], 0)
        + jnp.where(blocks - 1 - pair_order[None, :] == block_ids, lies[None, :] + 1, 0),
        axis=1,
        dtype=jnp.int32,
    )
    my_pair = jnp.sum(jnp.where(ctx_ids == lax.axis_index(CTX), pair_order, 0))
    reversed_table = jnp.pad(bucket_table[::-1], (0, window - half), constant_values=-1)
    diagonal_bucket = jnp.stack(
        [
            lax.dynamic_slice(reversed_table, (seq - half - block * half,), (window,))
            for block in (my_pair, blocks - 1 - my_pair)
        ]
    ).reshape(1, 2 * window)
    bucket_ids = jnp.arange(bucket_count, dtype=jnp.int32)
    bucket_hot = (diagonal_bucket == bucket_ids[:, None]).astype(F32)
    windows = lax.dot_general(rel_bias, bucket_hot, ROWS, precision=HIGHEST)
    windows = jnp.where(diagonal_bucket >= 0, windows, MASKED)
    windows = windows.reshape(head_pairs, 4, window)

    inputs = tokens[0].astype(F32)
    scale_one = norm_scale(inputs)
    normed_one = (inputs * scale_one * gain_attn).astype(BF)
    w_q = w_qkv[:, :model_width]
    queries = jnp.dot(normed_one, w_q, preferred_element_type=F32).astype(BF)
    near_tokens, queries, windows, place, slot_table, cot_slots = lax.optimization_barrier(
        (near_tokens, queries, windows, place, slot_table, cot_slots)
    )
    cot_rows = to_slots(cot_slots)
    near_tokens = near_tokens.reshape(seq // 2, model_width)
    far_tokens = lax.ppermute(near_tokens, "core", SWAP)
    all_normed, key_value = keys_and_values(
        place, near_tokens, far_tokens, gain_attn, w_qkv, half
    )
    attended, exps, inverse = attend(queries, key_value, windows)

    residual_one, normed_two, gates, slots = into_experts(
        attended, tokens[0], w_attn_out, gain_ffn, w_router, routes[0], slot_table
    )
    x_rows = to_slots(slots)
    input_grad, returned, parts = run_experts(x_rows, cot_rows, weights)

    def from_experts(rows):
        rows = exchange(rows.reshape(expert_devices, device_slots, rows.shape[3]), EXPERT_AXES)
        return rows.reshape(expert_devices * device_slots, rows.shape[2])

    input_grad = from_experts(input_grad)
    later_parts, input_grad, returned, bucket_hot = lax.optimization_barrier(
        (parts[1:], input_grad, returned, bucket_hot)
    )
    shares = [
        lax.psum_scatter(part, "x", scatter_dimension=0) for part in (parts[0], *later_parts)
    ]
    returned = from_experts(returned)

    mixed_grad, branch_grad, attended_grad, small = out_of_experts(
        input_grad,
        slot_table,
        gates,
        routes[0],
        normed_two,
        residual_one,
        cotangent[0],
        gain_ffn,
        w_router,
        w_attn_out,
    )

    query_grad, key_value_grad, diagonals = attend_back(
        exps, inverse, queries, key_value, attended_grad
    )

    core = jnp.reshape(my_core, (1,)).astype(jnp.int32)
    side = model_width // 2
    used = 4 * model_width + small.shape[0] + bucket_count
    total = used + -used % (8 * lax.axis_size(CHIPS))
    kept, given = key_value_weight_grads(core, key_value_grad, all_normed)
    got = lax.ppermute(given, "core", SWAP)
    query_grad, returned = lax.optimization_barrier((query_grad, returned))
    kept_too, given_too = weight_grads(
        core,
        query_grad,
        normed_one,
        attended,
        branch_grad,
        small,
        bucket_hot,
        diagonals,
        total - 2 * model_width,
    )
    key_value_grad, given_too, returned = lax.optimization_barrier(
        (key_value_grad, given_too, returned)
    )
    got_too = lax.ppermute(given_too, "core", SWAP)
    share = chip_share(((kept, got), (kept_too, got_too)))
    picked = jnp.dot(slot_table, returned, preferred_element_type=F32)
    mixture = gates[:, :1] * picked[:tok_rows] + gates[:, 1:2] * picked[tok_rows:]
    layer_out = (residual_one + mixture).astype(BF)[None]

    all_grads = normed_grads(place, key_value_grad, w_qkv, half)
    far_grad = lax.ppermute(all_grads[seq // 2 :], "core", SWAP)
    near_grad = all_grads[: seq // 2].astype(F32) + far_grad.astype(F32)
    near_grad = near_grad.astype(BF).reshape(ctx_count // 2, tok_rows, model_width)
    query_part = contract_cols(query_grad, w_q)
    share, near_grad, query_part, layer_out, shares = lax.optimization_barrier(
        (share, near_grad, query_part, layer_out, shares)
    )

    mine = spread(share, CHIPS).reshape(-1, side)
    shares = jnp.stack(shares).astype(F32)
    grad_w_in = jnp.concatenate([shares[:, :hidden, :hidden], shares[:, :hidden, hidden:]], axis=1)
    grad_w_out = shares[:, hidden:]
    mine, near_grad, grad_w_in, grad_w_out = lax.optimization_barrier(
        (mine, near_grad, grad_w_in, grad_w_out)
    )
    other = lax.ppermute(mine, "core", SWAP)
    row_grads = exchange(near_grad, SAME_CORE)
    held = whole_grad(core, mine, w_qkv, ())
    whole = whole_grad(1 - core, other, w_qkv, held)
    sum_w_qkv, products, sum_w_attn_out = whole
    sum_gain_attn = products[:, 0] / gain_attn
    rows = slice(4 * model_width, 4 * model_width + small.shape[0] + bucket_count)
    left = jnp.where(my_core == 0, mine[rows], other[rows])
    right = jnp.where(my_core == 0, other[rows], mine[rows])
    sums = jnp.concatenate([left, right], axis=1).astype(F32)
    sum_w_router, sum_gain_ffn = sums[:experts].T, sums[experts]
    sum_rel_bias = sums[small.shape[0] :, :head_count]
    row_grads, sum_w_qkv, sum_gain_attn, sum_w_router, sum_gain_ffn, sum_rel_bias = (
        lax.optimization_barrier(
            (row_grads, sum_w_qkv, sum_gain_attn, sum_w_router, sum_gain_ffn, sum_rel_bias)
        )
    )
    normed_one_grad = jnp.sum(row_grads.astype(F32), axis=0) + query_part
    input_norm_grad, _ = norm_backward(inputs, scale_one, gain_attn, normed_one_grad)
    grad_tokens = (mixed_grad + input_norm_grad)[None]
    return (
        layer_out,
        grad_tokens,
        sum_gain_attn,
        sum_w_qkv,
        sum_rel_bias,
        sum_w_attn_out,
        sum_gain_ffn,
        sum_w_router,
        grad_w_in,
        grad_w_out,
    )


def solution(mesh):
    split_mesh = Mesh(mesh.devices.reshape(SPLIT), EVERY)
    in_specs = (
        P(WSH, CTX, None),
        P(),
        P(),
        P(),
        P(),
        P(),
        P(),
        P(CTX, None, WSH),
        P(CTX, WSH, None),
        P(WSH, CTX, None),
        P(),
        P(),
        P(WSH, CTX, None),
    )
    out_specs = (
        P(WSH, CTX, None),
        P(WSH, CTX, None),
        P(),
        P(),
        P(),
        P(),
        P(),
        P(),
        P(CTX, None, WSH),
        P(CTX, WSH, None),
    )
    return jax.shard_map(
        on_device, mesh=split_mesh, in_specs=in_specs, out_specs=out_specs, check_vma=False
    )
```

```python
import functools

import jax
import jax.numpy as jnp
from jax import lax
from jax.experimental import pallas as pl
from jax.experimental.pallas import tpu as pltpu
from jax.sharding import Mesh
from jax.sharding import PartitionSpec as P

BF = jnp.bfloat16
F32 = jnp.float32
EPSILON = 1e-06
HIGHEST = lax.Precision.HIGHEST
MASKED = -1e30
ROWS = (((0,), (0,)), ((), ()))
COLS = (((1,), (1,)), ((), ()))
LANES = 128
VMEM_LIMIT = 58 * 1024 * 1024
SPLIT = (2, 4, 2, 2, 4)
EVERY = ("ya", "z", "core", "yb", "x")
CTX = ("ya", "z", "core")
WSH = ("yb", "x")
SAME_CORE = ("ya", "z")
CHIPS = ("ya", "z", "yb", "x")
EXPERT_AXES = ("ya", "z", "core", "yb")
SWAP = ((0, 1), (1, 0))


def norm_scale(values):
    return lax.rsqrt(jnp.mean(values * values, axis=-1, keepdims=True) + EPSILON)


def norm_backward(values, scale_vector, gain_vector, upstream):
    weighted = upstream * gain_vector
    inner_mean = jnp.mean(weighted * values, axis=-1, keepdims=True)
    grad_input = (
        scale_vector * weighted - values * scale_vector * scale_vector * scale_vector * inner_mean
    )
    grad_gain = jnp.sum(upstream * values * scale_vector, axis=0)
    return (grad_input, grad_gain)


def contract_rows(left_matrix, right_matrix):
    return lax.dot_general(left_matrix, right_matrix, ROWS, preferred_element_type=F32)


def contract_cols(left_matrix, right_matrix):
    return lax.dot_general(left_matrix, right_matrix, COLS, preferred_element_type=F32)


def exchange(array, axes):
    return lax.all_to_all(array, axes, split_axis=0, concat_axis=0, tiled=True)


def spread(array, axes):
    return exchange(jnp.broadcast_to(array[None], (lax.axis_size(axes), *array.shape)), axes)


def chip_share(parts):
    sums = [(kept.astype(F32) + got.astype(F32)).astype(BF) for kept, got in parts]
    total = jnp.concatenate(sums, axis=0)
    for axes in (CHIPS[:-1], CHIPS[-1]):
        count = lax.axis_size(axes)
        pieces = total.reshape(count, total.shape[0] // count, total.shape[1])
        total = jnp.sum(exchange(pieces, axes).astype(F32), axis=0).astype(BF)
    return total


def shear(tiles):
    count, rows, columns = tiles.shape
    while rows > 8:
        half = rows // 2
        moved = pltpu.roll(tiles[:, :half].reshape(count * half, columns), half, axis=1)
        tiles = moved.reshape(count, half, columns) + tiles[:, half:]
        rows = half
    flat = tiles.reshape(count * rows, columns)
    row_ids = lax.broadcasted_iota(jnp.int32, flat.shape, 0)
    step = rows // 2
    while step:
        flat = jnp.where(row_ids // step % 2 == 0, pltpu.roll(flat, step, axis=1), flat)
        step //= 2
    return jnp.sum(flat.reshape(count, rows, columns), axis=1)


def split_heads(array, factor):
    lanes = lax.broadcasted_iota(jnp.int32, array.shape, 1) // (LANES // 2)
    wide = array.astype(F32) * factor
    parts = [jnp.where(lanes == head, wide, 0.0).astype(BF) for head in range(2)]
    return jnp.concatenate(parts, axis=0)


def join_heads(array):
    rows = array.shape[0] // 2
    lanes = lax.broadcasted_iota(jnp.int32, (rows, LANES), 1) // (LANES // 2)
    return jnp.where(lanes == 0, array[:rows], array[rows:]).astype(BF)


def attend_kernel(q_ref, kv_ref, window_ref, out_ref, exps_ref, total_ref):
    half, seq = q_ref.shape[0] // 2, kv_ref.shape[1]
    window = seq + 2 * half
    q = split_heads(q_ref[...], (LANES // 2) ** -0.5)
    raw = contract_cols(q, kv_ref[0])
    tiles = jnp.broadcast_to(window_ref[...][:, None], (4, half, window))
    tiles = [
        pltpu.roll(tiles[part], window - half + 1, axis=1, stride=1, stride_axis=0)[:, :seq]
        for part in range(4)
    ]
    scores = raw + jnp.concatenate(tiles, axis=0)
    exps = jnp.exp(scores - jnp.max(scores, axis=1, keepdims=True))
    inverse = 1.0 / jnp.sum(exps, axis=1, keepdims=True)
    exps = exps.astype(BF)
    exps_ref[...] = exps.reshape(exps_ref.shape)
    total_ref[...] = jnp.broadcast_to(inverse, total_ref.shape)
    out_ref[...] = join_heads(jnp.dot(exps, kv_ref[1], preferred_element_type=F32) * inverse)


def attend(queries, key_value, windows):
    rows, width = queries.shape
    pairs, seq = key_value.shape[1:3]
    work = rows * seq * width
    return pl.pallas_call(
        attend_kernel,
        grid=(pairs,),
        in_specs=[
            pl.BlockSpec((rows, LANES), lambda h: (0, h)),
            pl.BlockSpec((2, None, seq, LANES), lambda h: (0, h, 0, 0)),
            pl.BlockSpec((None, 4, windows.shape[2]), lambda h: (h, 0, 0)),
        ],
        out_specs=[
            pl.BlockSpec((rows, LANES), lambda h: (0, h)),
            pl.BlockSpec((2, rows, seq), lambda h: (h, 0, 0)),
            pl.BlockSpec((None, 2 * rows, LANES), lambda h: (h, 0, 0)),
        ],
        out_shape=[
            jax.ShapeDtypeStruct((rows, width), BF),
            jax.ShapeDtypeStruct((2 * pairs, rows, seq), BF),
            jax.ShapeDtypeStruct((pairs, 2 * rows, LANES), F32),
        ],
        compiler_params=pltpu.CompilerParams(vmem_limit_bytes=VMEM_LIMIT),
        cost_estimate=pl.CostEstimate(
            flops=8 * work,
            bytes_accessed=4 * seq * width + 4 * pairs * rows * seq,
            transcendentals=2 * pairs * rows * seq,
        ),
        name="attend",
    )(queries, key_value, windows)


def attend_back_kernel(
    exps_ref, inverse_ref, q_ref, kv_ref, grad_ref, dq_ref, dkv_ref, diag_ref
):
    half, seq = q_ref.shape[0] // 2, kv_ref.shape[1]
    factor = (LANES // 2) ** -0.5
    rows = 4 * half
    q = split_heads(q_ref[...], factor)
    inverse = inverse_ref[:, :1]
    grad = (split_heads(grad_ref[...], 1.0).astype(F32) * inverse).astype(BF)
    exps = exps_ref[...].reshape(rows, seq)
    wide = exps.astype(F32)
    prob_grad = contract_cols(grad, kv_ref[1])
    inner = jnp.sum(wide * prob_grad, axis=1, keepdims=True)
    score_grad = wide * (prob_grad - inner * inverse)
    tiles = jnp.concatenate([score_grad, jnp.zeros((rows, 2 * half), F32)], axis=1)
    sums = shear(tiles.reshape(4, half, seq + 2 * half))
    for part in range(2):
        for head in range(2):
            diag_ref[part, head : head + 1] = sums[2 * head + part : 2 * head + part + 1]
    score_grad = score_grad.astype(BF)
    query_grad = jnp.dot(score_grad, kv_ref[0], preferred_element_type=F32) * factor
    dq_ref[...] = join_heads(query_grad)
    dkv_ref[0] = contract_rows(q, score_grad).astype(BF)
    dkv_ref[1] = contract_rows(grad, exps).astype(BF)


def attend_back(exps, inverse, queries, key_value, attended_grad):
    rows, width = queries.shape
    pairs, seq = key_value.shape[1:3]
    window = seq + rows
    row_spec = pl.BlockSpec((rows, LANES), lambda h: (0, h))
    kv_spec = pl.BlockSpec((2, None, seq, LANES), lambda h: (0, h, 0, 0))
    return pl.pallas_call(
        attend_back_kernel,
        grid=(pairs,),
        in_specs=[
            pl.BlockSpec((2, rows, seq), lambda h: (h, 0, 0)),
            pl.BlockSpec((None, 2 * rows, LANES), lambda h: (h, 0, 0)),
            row_spec,
            kv_spec,
            row_spec,
        ],
        out_specs=[
            row_spec,
            pl.BlockSpec((2, None, LANES, seq), lambda h: (0, h, 0, 0)),
            pl.BlockSpec((2, None, 2, window), lambda h: (0, h, 0, 0)),
        ],
        out_shape=[
            jax.ShapeDtypeStruct((rows, width), BF),
            jax.ShapeDtypeStruct((2, pairs, LANES, seq), BF),
            jax.ShapeDtypeStruct((2, pairs, 2, window), F32),
        ],
        compiler_params=pltpu.CompilerParams(vmem_limit_bytes=VMEM_LIMIT),
        cost_estimate=pl.CostEstimate(
            flops=16 * rows * seq * width,
            bytes_accessed=8 * seq * width + 4 * pairs * rows * seq,
            transcendentals=0,
        ),
        name="attend_back",
    )(exps, inverse, queries, key_value, attended_grad)


def key_value_kernel(place_ref, near_ref, far_ref, gain_ref, wk_ref, wv_ref, normed_ref, kv_ref, *, half):
    tile = normed_ref.shape[0] // half
    near_blocks = near_ref.shape[0] // half
    rows = []
    for block in range(tile):
        source = place_ref[pl.program_id(0) * tile + block]
        at = pl.ds(pl.multiple_of(lax.rem(source, near_blocks) * half, half), half)
        rows.append(jnp.where(source < near_blocks, near_ref[at].astype(F32), far_ref[at].astype(F32)))
    inputs = jnp.concatenate(rows, axis=0)
    normed = (inputs * norm_scale(inputs) * gain_ref[...]).astype(BF)
    normed_ref[...] = normed
    for part, weight_ref in enumerate((wk_ref, wv_ref)):
        out = jnp.dot(normed, weight_ref[...], preferred_element_type=F32).astype(BF)
        for pair in range(kv_ref.shape[1]):
            kv_ref[part, pair] = out[:, pair * LANES : (pair + 1) * LANES]


def keys_and_values(place, near, far, gain, w_qkv, half):
    near_rows, width = near.shape
    seq = 2 * near_rows
    tile = 8 * half
    return pl.pallas_call(
        functools.partial(key_value_kernel, half=half),
        grid_spec=pltpu.PrefetchScalarGridSpec(
            num_scalar_prefetch=1,
            grid=(seq // tile,),
            in_specs=[
                pl.BlockSpec((near_rows, width), lambda r, p: (0, 0)),
                pl.BlockSpec((near_rows, width), lambda r, p: (0, 0)),
                pl.BlockSpec((1, width), lambda r, p: (0, 0)),
                pl.BlockSpec((width, width), lambda r, p: (0, 1)),
                pl.BlockSpec((width, width), lambda r, p: (0, 2)),
            ],
            out_specs=[
                pl.BlockSpec((tile, width), lambda r, p: (r, 0)),
                pl.BlockSpec((2, width // LANES, tile, LANES), lambda r, p: (0, 0, r, 0)),
            ],
        ),
        out_shape=[
            jax.ShapeDtypeStruct((seq, width), BF),
            jax.ShapeDtypeStruct((2, width // LANES, seq, LANES), BF),
        ],
        compiler_params=pltpu.CompilerParams(vmem_limit_bytes=VMEM_LIMIT),
        cost_estimate=pl.CostEstimate(
            flops=4 * seq * width * width, bytes_accessed=8 * seq * width, transcendentals=seq
        ),
        name="keys_and_values",
    )(place, near, far, gain[None], w_qkv, w_qkv)


def normed_grad_kernel(place_ref, dkv_ref, wk_ref, wv_ref, out_ref, *, half):
    total = 0.0
    for part, weight_ref in enumerate((wk_ref, wv_ref)):
        columns = dkv_ref[part].reshape(weight_ref.shape[1], dkv_ref.shape[3])
        total += jnp.dot(weight_ref[...], columns, preferred_element_type=F32)
    total = total.T.astype(BF)
    step = total.shape[0] // half
    for block in range(step):
        target = place_ref[pl.program_id(0) * step + block]
        at = pl.ds(pl.multiple_of(target * half, half), half)
        out_ref[at] = total[block * half : (block + 1) * half]


def normed_grads(place, key_value_grad, w_qkv, half):
    width = w_qkv.shape[0]
    pairs, seq = key_value_grad.shape[1], key_value_grad.shape[3]
    tile = 8 * half
    return pl.pallas_call(
        functools.partial(normed_grad_kernel, half=half),
        grid_spec=pltpu.PrefetchScalarGridSpec(
            num_scalar_prefetch=1,
            grid=(seq // tile,),
            in_specs=[
                pl.BlockSpec((2, pairs, LANES, tile), lambda r, p: (0, 0, 0, r)),
                pl.BlockSpec((width, width), lambda r, p: (0, 1)),
                pl.BlockSpec((width, width), lambda r, p: (0, 2)),
            ],
            out_specs=pl.BlockSpec((seq, width), lambda r, p: (0, 0)),
        ),
        out_shape=jax.ShapeDtypeStruct((seq, width), BF),
        compiler_params=pltpu.CompilerParams(vmem_limit_bytes=VMEM_LIMIT),
        cost_estimate=pl.CostEstimate(
            flops=4 * seq * width * width, bytes_accessed=8 * seq * width, transcendentals=0
        ),
        name="normed_grads",
    )(place, key_value_grad, w_qkv, w_qkv)


def give_halves(core_ref, total, kept_ref, given_ref):
    rows, side = total.shape[0], kept_ref.shape[1]
    left, right = total[:, :side].astype(BF), total[:, side:].astype(BF)

    @pl.when(core_ref[0] == 0)
    def _():
        kept_ref[:rows] = left
        given_ref[:rows] = right

    @pl.when(core_ref[0] != 0)
    def _():
        kept_ref[:rows] = right
        given_ref[:rows] = left


def key_value_weight_kernel(core_ref, dkv_ref, all_normed_ref, kept_ref, given_ref):
    columns = dkv_ref[...].reshape(dkv_ref.shape[0] * LANES, dkv_ref.shape[2])
    total = jnp.dot(columns, all_normed_ref[...], preferred_element_type=F32)
    give_halves(core_ref, total, kept_ref, given_ref)


def key_value_weight_grads(core, key_value_grad, all_normed):
    seq, width = all_normed.shape
    out_spec = pl.BlockSpec((width, width // 2), lambda t, p: (t, 0))
    out_shape = jax.ShapeDtypeStruct((2 * width, width // 2), BF)
    return pl.pallas_call(
        key_value_weight_kernel,
        grid_spec=pltpu.PrefetchScalarGridSpec(
            num_scalar_prefetch=1,
            grid=(2,),
            in_specs=[
                pl.BlockSpec((None, width // LANES, LANES, seq), lambda t, p: (t, 0, 0, 0)),
                pl.BlockSpec((seq, width), lambda t, p: (0, 0)),
            ],
            out_specs=[out_spec, out_spec],
        ),
        out_shape=[out_shape, out_shape],
        compiler_params=pltpu.CompilerParams(vmem_limit_bytes=VMEM_LIMIT),
        cost_estimate=pl.CostEstimate(
            flops=4 * seq * width * width, bytes_accessed=8 * seq * width, transcendentals=0
        ),
        name="key_value_weight_grads",
    )(core, key_value_grad, all_normed)


def weight_grad_kernel(
    core_ref,
    dq_ref,
    normed_ref,
    attended_ref,
    branch_ref,
    small_ref,
    hot_ref,
    diag_ref,
    kept_ref,
    given_ref,
):
    step = pl.program_id(0)

    @pl.when(step == 0)
    def _():
        total = contract_rows(dq_ref[...], normed_ref[...])
        give_halves(core_ref, total, kept_ref, given_ref)

    @pl.when(step == 1)
    def _():
        total = contract_rows(attended_ref[...], branch_ref[...])
        give_halves(core_ref, total, kept_ref, given_ref)

    @pl.when(step == 2)
    def _():
        window = diag_ref.shape[3]
        bias_grad = 0.0
        for part in range(2):
            sums = jnp.concatenate([diag_ref[part, pair] for pair in range(diag_ref.shape[1])], axis=0)
            bias_grad += lax.dot_general(
                hot_ref[:, part * window : (part + 1) * window],
                sums,
                COLS,
                precision=HIGHEST,
                preferred_element_type=F32,
            )
        buckets, heads = bias_grad.shape
        spare = jnp.zeros((buckets, small_ref.shape[1] - heads), F32)
        bias_rows = jnp.concatenate([bias_grad, spare], axis=1)
        total = jnp.concatenate([small_ref[...], bias_rows], axis=0)
        give_halves(core_ref, total, kept_ref, given_ref)


def weight_grads(
    core, query_grad, normed_one, attended, branch_grad, small, bucket_hot, diagonals, total
):
    rows, width = normed_one.shape
    row_spec = pl.BlockSpec((rows, width), lambda t, p: (0, 0))
    out_spec = pl.BlockSpec((width, width // 2), lambda t, p: (t, 0))
    out_shape = jax.ShapeDtypeStruct((total, width // 2), BF)
    return pl.pallas_call(
        weight_grad_kernel,
        grid_spec=pltpu.PrefetchScalarGridSpec(
            num_scalar_prefetch=1,
            grid=(3,),
            in_specs=[
                row_spec,
                row_spec,
                row_spec,
                row_spec,
                pl.BlockSpec(small.shape, lambda t, p: (0, 0)),
                pl.BlockSpec(bucket_hot.shape, lambda t, p: (0, 0)),
                pl.BlockSpec(diagonals.shape, lambda t, p: (0, 0, 0, 0)),
            ],
            out_specs=[out_spec, out_spec],
        ),
        out_shape=[out_shape, out_shape],
        compiler_params=pltpu.CompilerParams(vmem_limit_bytes=VMEM_LIMIT),
        cost_estimate=pl.CostEstimate(
            flops=4 * rows * width * width, bytes_accessed=16 * rows * width, transcendentals=0
        ),
        name="weight_grads",
    )(core, query_grad, normed_one, attended, branch_grad, small, bucket_hot, diagonals)


def whole_grad_kernel(side_ref, half_ref, weight_ref, *refs):
    grad_ref, product_ref, out_ref = refs[-3:]
    step = pl.program_id(0)
    last = pl.num_programs(0) - 1
    half = half_ref[...].astype(F32)

    @pl.when(step < last)
    def _():
        grad = half.T
        grad_ref[...] = grad
        product = jnp.sum(grad * weight_ref[...].astype(F32), axis=1, keepdims=True)
        product = jnp.broadcast_to(product, product_ref.shape)

        @pl.when(step == 0)
        def _():
            product_ref[...] = product

        @pl.when(step > 0)
        def _():
            product_ref[...] += product

    @pl.when(step == last)
    def _():
        out_ref[...] = half


def whole_grad(side, half_sums, weight, held):
    width, columns = weight.shape
    half = half_sums.shape[1]
    steps = columns // width + 1

    def tile_map(t, p):
        return (p[0], jnp.minimum(t, steps - 2))

    return pl.pallas_call(
        whole_grad_kernel,
        grid_spec=pltpu.PrefetchScalarGridSpec(
            num_scalar_prefetch=1,
            grid=(steps,),
            in_specs=[
                pl.BlockSpec(
                    (width, half), lambda t, p: (jnp.where(t < steps - 1, (t + 2) % 3, 3), 0)
                ),
                pl.BlockSpec((half, width), tile_map),
                *[pl.BlockSpec(memory_space=pl.ANY) for _ in held],
            ],
            out_specs=[
                pl.BlockSpec((half, width), tile_map),
                pl.BlockSpec((half, LANES), lambda t, p: (p[0], 0)),
                pl.BlockSpec((width, half), lambda t, p: (0, p[0])),
            ],
        ),
        out_shape=[
            jax.ShapeDtypeStruct((width, columns), F32),
            jax.ShapeDtypeStruct((width, LANES), F32),
            jax.ShapeDtypeStruct((width, width), F32),
        ],
        input_output_aliases={3 + at: at for at in range(len(held))},
        compiler_params=pltpu.CompilerParams(vmem_limit_bytes=VMEM_LIMIT),
        cost_estimate=pl.CostEstimate(
            flops=width * columns, bytes_accessed=4 * width * columns, transcendentals=0
        ),
        name="whole_grad",
    )(side, half_sums, weight, *held)


def expert_rows(x_ref, cot_ref):
    width = cot_ref.shape[-1]
    rows = x_ref.shape[0] * x_ref.shape[1]
    rows_in = x_ref[...].reshape(rows, x_ref.shape[2])
    gate = jnp.sum(rows_in[:, width:].astype(F32), axis=1, keepdims=True)
    slot_grad = (cot_ref[...].reshape(rows, width).astype(F32) * gate).astype(BF)
    return rows_in[:, :width], slot_grad


def high_and_low(column):
    high = column.astype(BF).astype(F32)
    lanes = lax.broadcasted_iota(jnp.int32, (column.shape[0], LANES), 1)
    wide = jnp.where(lanes == 0, high, jnp.where(lanes == 1, column - high, 0.0))
    return wide.astype(BF)


def write_weight_grads(x, slot_grad, activated, pre_grad, grad_ref):
    grad_in = contract_rows(x, pre_grad).astype(BF)
    grad_out = contract_rows(activated, slot_grad).astype(BF)
    slices, hidden = grad_ref.shape[0], grad_ref.shape[1] // 2
    for index in range(slices):
        columns = grad_in[:, index * hidden : (index + 1) * hidden]
        grad_ref[index, :hidden, :hidden] = columns[:hidden]
        grad_ref[index, :hidden, hidden:] = columns[hidden:]
        grad_ref[index, hidden:] = grad_out[index * hidden : (index + 1) * hidden]


def pack_kernel(in_ref, out_ref, packed_ref):
    hidden = out_ref.shape[0]
    packed_ref[:hidden, :hidden] = in_ref[:hidden]
    packed_ref[:hidden, hidden:] = in_ref[hidden:]
    packed_ref[hidden:] = out_ref[...]


def packed_weights(w_in, w_out):
    experts, width, hidden = w_in.shape
    return pl.pallas_call(
        pack_kernel,
        grid=(experts,),
        in_specs=[
            pl.BlockSpec((None, width, hidden), lambda e: (e, 0, 0)),
            pl.BlockSpec((None, hidden, width), lambda e: (e, 0, 0)),
        ],
        out_specs=pl.BlockSpec((None, 2 * hidden, width), lambda e: (e, 0, 0)),
        out_shape=jax.ShapeDtypeStruct((experts, 2 * hidden, width), BF),
        compiler_params=pltpu.CompilerParams(vmem_limit_bytes=VMEM_LIMIT),
        name="packed_weights",
    )(w_in, w_out)


def slice_weights(weight_ref):
    slices, hidden = weight_ref.shape[0], weight_ref.shape[1] // 2
    weights = [weight_ref[index] for index in range(slices)]
    tops = [weight[:hidden] for weight in weights]
    tops = [jnp.concatenate([top[:, :hidden], top[:, hidden:]], axis=0) for top in tops]
    weight_out = jnp.concatenate([weight[hidden:] for weight in weights], axis=0)
    return jnp.concatenate(tops, axis=1), weight_out


def expert_kernel(
    x_ref,
    cot_ref,
    weight_ref,
    dx_ref,
    ret_ref,
    act_ref,
    pre_grad_ref,
    ret_sum,
    dx_sum,
):
    part = pl.program_id(1)
    width = cot_ref.shape[-1]
    x, slot_grad = expert_rows(x_ref, cot_ref)
    weight_in, weight_out = slice_weights(weight_ref)
    pre = jnp.dot(x, weight_in, preferred_element_type=F32)
    act_grad = contract_cols(slot_grad, weight_out)
    cumulative = 0.5 * (1.0 + lax.erf(pre * 0.7071067811865476))
    activated = (pre * cumulative).astype(BF)
    slope = cumulative + pre * (jnp.exp(-0.5 * pre * pre) * 0.3989422804014327)
    pre_grad = (act_grad * slope).astype(BF)
    returned = jnp.dot(activated, weight_out, preferred_element_type=F32)
    input_grad = contract_cols(pre_grad, weight_in)

    act_ref[...] = activated
    pre_grad_ref[...] = pre_grad

    @pl.when(part == 0)
    def _():
        ret_sum[...] = returned
        dx_sum[...] = input_grad

    @pl.when(part > 0)
    def _():
        ret_sum[...] += returned
        dx_sum[...] += input_grad

    @pl.when(part == pl.num_programs(1) - 1)
    def _():
        shape = cot_ref.shape
        rows = shape[0] * shape[1]
        ret = ret_sum[...]
        ret_ref[...] = ret.astype(BF).reshape(shape)
        upstream = cot_ref[...].reshape(rows, width).astype(F32)
        gate_grad = high_and_low(jnp.sum(ret * upstream, axis=1, keepdims=True))
        dx_ref[:, :, :width] = dx_sum[...].astype(BF).reshape(shape)
        dx_ref[:, :, width:] = gate_grad.reshape(shape[0], shape[1], LANES)


def expert_grad_kernel(x_ref, cot_ref, act_ref, pre_grad_ref, grad_ref):
    x, slot_grad = expert_rows(x_ref, cot_ref)
    write_weight_grads(x, slot_grad, act_ref[...], pre_grad_ref[...], grad_ref)


def run_experts(x_rows, cot_rows, weights):
    devices, experts, slots, width = cot_rows.shape
    wide = x_rows.shape[3]
    parts, _, both, _ = weights.shape
    hidden = both // 2
    rows = devices * slots
    slices = 2
    steps = parts // slices

    def row_spec(columns):
        return pl.BlockSpec((devices, None, slots, columns), lambda e, w: (0, e, 0, 0))

    hidden_spec = pl.BlockSpec((None, rows, slices * hidden), lambda e, w: (e, 0, w))
    hidden_shape = jax.ShapeDtypeStruct((experts, rows, parts * hidden), BF)
    grad_shape = jax.ShapeDtypeStruct((parts, both, width), BF)
    work = experts * rows * width * parts * hidden
    params = pltpu.CompilerParams(vmem_limit_bytes=VMEM_LIMIT)
    input_grad, returned, activated, pre_grad = pl.pallas_call(
        expert_kernel,
        grid=(experts, steps),
        in_specs=[
            row_spec(wide),
            row_spec(width),
            pl.BlockSpec((slices, None, both, width), lambda e, w: (w, e, 0, 0)),
        ],
        out_specs=[
            row_spec(width + LANES),
            row_spec(width),
            hidden_spec,
            hidden_spec,
        ],
        out_shape=[
            jax.ShapeDtypeStruct((devices, experts, slots, width + LANES), BF),
            jax.ShapeDtypeStruct((devices, experts, slots, width), BF),
            hidden_shape,
            hidden_shape,
        ],
        scratch_shapes=[pltpu.VMEM((rows, width), F32), pltpu.VMEM((rows, width), F32)],
        compiler_params=params,
        cost_estimate=pl.CostEstimate(
            flops=8 * work,
            bytes_accessed=8 * experts * rows * width + 4 * parts * experts * width * hidden,
            transcendentals=2 * experts * rows * parts * hidden,
        ),
        name="experts",
    )(x_rows, cot_rows, weights)
    weight_grads_of = []
    for expert in range(experts):

        def own_rows(columns, expert=expert):
            return pl.BlockSpec((devices, None, slots, columns), lambda w: (0, expert, 0, 0))

        own_hidden = pl.BlockSpec(
            (None, rows, slices * hidden), lambda w, expert=expert: (expert, 0, w)
        )
        weight_grads_of.append(
            pl.pallas_call(
                expert_grad_kernel,
                grid=(steps,),
                in_specs=[own_rows(wide), own_rows(width), own_hidden, own_hidden],
                out_specs=pl.BlockSpec((slices, both, width), lambda w: (w, 0, 0)),
                out_shape=grad_shape,
                compiler_params=params,
                cost_estimate=pl.CostEstimate(
                    flops=4 * work // experts,
                    bytes_accessed=8 * rows * width + 4 * parts * width * hidden,
                    transcendentals=0,
                ),
                name="expert_grads",
            )(x_rows, cot_rows, activated, pre_grad)
        )
    return input_grad, returned, weight_grads_of


def into_experts_kernel(
    attended_ref,
    tokens_ref,
    w_out_ref,
    gain_ref,
    w_router_ref,
    chosen_ref,
    table_ref,
    residual_ref,
    normed_ref,
    gate_ref,
    slots_ref,
):
    inputs = tokens_ref[...].astype(F32)
    residual = inputs + jnp.dot(attended_ref[...], w_out_ref[...], preferred_element_type=F32)
    residual_ref[...] = residual
    normed = (residual * norm_scale(residual) * gain_ref[...]).astype(BF)
    normed_ref[...] = normed
    logits = jnp.dot(normed, w_router_ref[...], preferred_element_type=F32)
    hots = picked_hots(chosen_ref, logits.shape)
    first, second = [jnp.sum(hot * logits, axis=1, keepdims=True) for hot in hots]
    peak = jnp.maximum(first, second)
    first, second = jnp.exp(first - peak), jnp.exp(second - peak)
    gates = [first / (first + second), second / (first + second)]
    lanes = lax.broadcasted_iota(jnp.int32, gate_ref.shape, 1)
    gate_ref[...] = jnp.where(lanes == 0, gates[0], jnp.where(lanes == 1, gates[1], 0.0))
    picks = [jnp.concatenate([normed, high_and_low(gate)], axis=1) for gate in gates]
    slots_ref[...] = contract_rows(table_ref[...], jnp.concatenate(picks, axis=0)).astype(BF)


def picked_hots(chosen_ref, shape):
    ids = lax.broadcasted_iota(jnp.int32, shape, 1)
    return [jnp.where(chosen_ref[:, pick : pick + 1] == ids, 1.0, 0.0) for pick in range(2)]


def into_experts(attended, tokens, w_attn_out, gain, w_router, chosen, table):
    rows, width = attended.shape
    return pl.pallas_call(
        into_experts_kernel,
        out_shape=[
            jax.ShapeDtypeStruct((rows, width), F32),
            jax.ShapeDtypeStruct((rows, width), BF),
            jax.ShapeDtypeStruct((rows, LANES), F32),
            jax.ShapeDtypeStruct((table.shape[1], width + LANES), BF),
        ],
        compiler_params=pltpu.CompilerParams(vmem_limit_bytes=VMEM_LIMIT),
        name="into_experts",
    )(attended, tokens, w_attn_out, gain[None], w_router, chosen, table)


def out_of_experts_kernel(
    grads_ref,
    table_ref,
    gate_ref,
    chosen_ref,
    normed_ref,
    residual_ref,
    cot_ref,
    gain_ref,
    w_router_ref,
    w_out_ref,
    mixed_ref,
    branch_ref,
    attended_grad_ref,
    small_ref,
):
    rows, width = residual_ref.shape
    table = table_ref[...]
    grads = jnp.dot(table, grads_ref[...], preferred_element_type=F32)
    gate_grads = jnp.sum(grads[:, width:], axis=1, keepdims=True)
    gate_grads = [gate_grads[:rows], gate_grads[rows:]]
    gates = [gate_ref[:, :1], gate_ref[:, 1:2]]
    inner = gates[0] * gate_grads[0] + gates[1] * gate_grads[1]
    hots = picked_hots(chosen_ref, (rows, w_router_ref.shape[1]))
    logit_grad = sum(
        hot * (gate * (gate_grad - inner)) for hot, gate, gate_grad in zip(hots, gates, gate_grads)
    )
    normed = normed_ref[...].astype(F32)
    w_router = w_router_ref[...].astype(F32)
    w_router_grad = lax.dot_general(
        logit_grad, normed, ROWS, precision=HIGHEST, preferred_element_type=F32
    )
    router_back = lax.dot_general(
        logit_grad, w_router, COLS, precision=HIGHEST, preferred_element_type=F32
    )
    normed_grad = grads[:rows, :width] + grads[rows:, :width] + router_back
    residual = residual_ref[...]
    norm_part, gain_grad = norm_backward(
        residual, norm_scale(residual), gain_ref[...], normed_grad
    )
    mixed = cot_ref[...].astype(F32) + norm_part
    mixed_ref[...] = mixed
    branch = mixed.astype(BF)
    branch_ref[...] = branch
    attended_grad_ref[...] = contract_cols(branch, w_out_ref[...]).astype(BF)
    experts = w_router_grad.shape[0]
    small_ref[:experts] = w_router_grad
    tail = small_ref.shape[0] - experts
    first = lax.broadcasted_iota(jnp.int32, (tail, width), 0) == 0
    small_ref[experts:] = jnp.where(first, gain_grad[None], 0.0)


def out_of_experts(
    grads, table, gates, chosen, normed, residual, cotangent, gain, w_router, w_attn_out
):
    rows, width = residual.shape
    return pl.pallas_call(
        out_of_experts_kernel,
        out_shape=[
            jax.ShapeDtypeStruct((rows, width), F32),
            jax.ShapeDtypeStruct((rows, width), BF),
            jax.ShapeDtypeStruct((rows, width), BF),
            jax.ShapeDtypeStruct((w_router.shape[1] + 8, width), F32),
        ],
        compiler_params=pltpu.CompilerParams(vmem_limit_bytes=VMEM_LIMIT),
        name="out_of_experts",
    )(grads, table, gates, chosen, normed, residual, cotangent, gain[None], w_router, w_attn_out)


def on_device(
    tokens,
    gain_attn,
    w_qkv,
    rel_bias,
    w_attn_out,
    gain_ffn,
    w_router,
    w_in,
    w_out,
    routes,
    pair_order,
    bucket_table,
    cotangent,
):
    tok_rows = tokens.shape[1]
    model_width = tokens.shape[2]
    head_count = rel_bias.shape[1]
    bucket_count = rel_bias.shape[0]
    ctx_count = lax.axis_size(CTX)
    half = tok_rows // 2
    blocks = 2 * ctx_count
    seq = half * blocks
    window = seq + 2 * half
    head_pairs = head_count // 2
    local_experts = w_in.shape[0]
    experts = w_router.shape[1]
    capacity = 4 * tok_rows // experts
    device_slots = local_experts * capacity
    expert_devices = lax.axis_size(EXPERT_AXES)
    copies = expert_devices // ctx_count

    near_tokens = spread(tokens[0], SAME_CORE)
    hidden = w_in.shape[2]
    weights = lax.all_gather(packed_weights(w_in, w_out), "x", axis=0)

    chosen = routes[0].T
    expert_ids = jnp.arange(experts, dtype=jnp.int32)
    flat_expert = chosen.reshape(2 * tok_rows)
    member = flat_expert[:, None] == expert_ids[None, :]
    picks = jnp.arange(2 * tok_rows, dtype=jnp.int32)
    before = (picks[:, None] > picks[None, :]).astype(BF)
    counts = jnp.dot(before, member.astype(BF), preferred_element_type=F32)
    slot_rank = jnp.sum(jnp.where(member, counts, 0.0), axis=1).astype(jnp.int32)
    owner_index = flat_expert // local_experts
    slot_of = (flat_expert % local_experts) * capacity + slot_rank
    slot_ids = jnp.arange(expert_devices * device_slots, dtype=jnp.int32)
    slot_hot = (owner_index[:, None] == (slot_ids // (copies * device_slots))[None, :]) & (
        slot_of[:, None] == (slot_ids % device_slots)[None, :]
    )
    slot_table = slot_hot.astype(BF)
    token_table = slot_table[:tok_rows] + slot_table[tok_rows:]

    def to_slots(slots):
        arrived = exchange(slots.reshape(expert_devices, device_slots, -1), EXPERT_AXES)
        return arrived.reshape(expert_devices, local_experts, capacity, -1)

    cot_slots = contract_rows(token_table, cotangent[0]).astype(BF)

    ctx_ids = jnp.arange(ctx_count, dtype=jnp.int32)
    my_core = lax.axis_index("core")
    near = (ctx_ids % 2) == my_core
    lies = 2 * (jnp.where(near, 0, ctx_count // 2) + ctx_ids // 2)
    block_ids = jnp.arange(blocks, dtype=jnp.int32)[:, None]
    place = jnp.sum(
        jnp.where(pair_order[None, :] == block_ids, lies[None, :], 0)
        + jnp.where(blocks - 1 - pair_order[None, :] == block_ids, lies[None, :] + 1, 0),
        axis=1,
        dtype=jnp.int32,
    )
    my_pair = jnp.sum(jnp.where(ctx_ids == lax.axis_index(CTX), pair_order, 0))
    reversed_table = jnp.pad(bucket_table[::-1], (0, window - half), constant_values=-1)
    diagonal_bucket = jnp.stack(
        [
            lax.dynamic_slice(reversed_table, (seq - half - block * half,), (window,))
            for block in (my_pair, blocks - 1 - my_pair)
        ]
    ).reshape(1, 2 * window)
    bucket_ids = jnp.arange(bucket_count, dtype=jnp.int32)
    bucket_hot = (diagonal_bucket == bucket_ids[:, None]).astype(F32)
    windows = lax.dot_general(rel_bias, bucket_hot, ROWS, precision=HIGHEST)
    windows = jnp.where(diagonal_bucket >= 0, windows, MASKED)
    windows = windows.reshape(head_pairs, 4, window)

    inputs = tokens[0].astype(F32)
    scale_one = norm_scale(inputs)
    normed_one = (inputs * scale_one * gain_attn).astype(BF)
    w_q = w_qkv[:, :model_width]
    queries = jnp.dot(normed_one, w_q, preferred_element_type=F32).astype(BF)
    near_tokens, queries, windows, place, slot_table, cot_slots = lax.optimization_barrier(
        (near_tokens, queries, windows, place, slot_table, cot_slots)
    )
    cot_rows = to_slots(cot_slots)
    near_tokens = near_tokens.reshape(seq // 2, model_width)
    far_tokens = lax.ppermute(near_tokens, "core", SWAP)
    all_normed, key_value = keys_and_values(
        place, near_tokens, far_tokens, gain_attn, w_qkv, half
    )
    attended, exps, inverse = attend(queries, key_value, windows)

    residual_one, normed_two, gates, slots = into_experts(
        attended, tokens[0], w_attn_out, gain_ffn, w_router, routes[0], slot_table
    )
    x_rows = to_slots(slots)
    input_grad, returned, parts = run_experts(x_rows, cot_rows, weights)

    def from_experts(rows):
        rows = exchange(rows.reshape(expert_devices, device_slots, rows.shape[3]), EXPERT_AXES)
        return rows.reshape(expert_devices * device_slots, rows.shape[2])

    input_grad = from_experts(input_grad)
    parts, input_grad, returned, bucket_hot = lax.optimization_barrier(
        (parts, input_grad, returned, bucket_hot)
    )
    shares = [
        lax.psum_scatter(part, "x", scatter_dimension=0) for part in parts
    ]
    returned = from_experts(returned)

    mixed_grad, branch_grad, attended_grad, small = out_of_experts(
        input_grad,
        slot_table,
        gates,
        routes[0],
        normed_two,
        residual_one,
        cotangent[0],
        gain_ffn,
        w_router,
        w_attn_out,
    )

    query_grad, key_value_grad, diagonals = attend_back(
        exps, inverse, queries, key_value, attended_grad
    )

    core = jnp.reshape(my_core, (1,)).astype(jnp.int32)
    side = model_width // 2
    used = 4 * model_width + small.shape[0] + bucket_count
    total = used + -used % (8 * lax.axis_size(CHIPS))
    kept, given = key_value_weight_grads(core, key_value_grad, all_normed)
    got = lax.ppermute(given, "core", SWAP)
    query_grad, returned = lax.optimization_barrier((query_grad, returned))
    kept_too, given_too = weight_grads(
        core,
        query_grad,
        normed_one,
        attended,
        branch_grad,
        small,
        bucket_hot,
        diagonals,
        total - 2 * model_width,
    )
    key_value_grad, given_too, returned = lax.optimization_barrier(
        (key_value_grad, given_too, returned)
    )
    got_too = lax.ppermute(given_too, "core", SWAP)
    share = chip_share(((kept, got), (kept_too, got_too)))
    picked = jnp.dot(slot_table, returned, preferred_element_type=F32)
    mixture = gates[:, :1] * picked[:tok_rows] + gates[:, 1:2] * picked[tok_rows:]
    layer_out = (residual_one + mixture).astype(BF)[None]

    all_grads = normed_grads(place, key_value_grad, w_qkv, half)
    far_grad = lax.ppermute(all_grads[seq // 2 :], "core", SWAP)
    near_grad = all_grads[: seq // 2].astype(F32) + far_grad.astype(F32)
    near_grad = near_grad.astype(BF).reshape(ctx_count // 2, tok_rows, model_width)
    query_part = contract_cols(query_grad, w_q)
    share, near_grad, query_part, layer_out, shares = lax.optimization_barrier(
        (share, near_grad, query_part, layer_out, shares)
    )

    mine = spread(share, CHIPS).reshape(-1, side)
    shares = jnp.stack(shares).astype(F32)
    grad_w_in = jnp.concatenate([shares[:, :hidden, :hidden], shares[:, :hidden, hidden:]], axis=1)
    grad_w_out = shares[:, hidden:]
    mine, near_grad, grad_w_in, grad_w_out = lax.optimization_barrier(
        (mine, near_grad, grad_w_in, grad_w_out)
    )
    other = lax.ppermute(mine, "core", SWAP)
    row_grads = exchange(near_grad, SAME_CORE)
    held = whole_grad(core, mine, w_qkv, ())
    whole = whole_grad(1 - core, other, w_qkv, held)
    sum_w_qkv, products, sum_w_attn_out = whole
    sum_gain_attn = products[:, 0] / gain_attn
    rows = slice(4 * model_width, 4 * model_width + small.shape[0] + bucket_count)
    left = jnp.where(my_core == 0, mine[rows], other[rows])
    right = jnp.where(my_core == 0, other[rows], mine[rows])
    sums = jnp.concatenate([left, right], axis=1).astype(F32)
    sum_w_router, sum_gain_ffn = sums[:experts].T, sums[experts]
    sum_rel_bias = sums[small.shape[0] :, :head_count]
    row_grads, sum_w_qkv, sum_gain_attn, sum_w_router, sum_gain_ffn, sum_rel_bias = (
        lax.optimization_barrier(
            (row_grads, sum_w_qkv, sum_gain_attn, sum_w_router, sum_gain_ffn, sum_rel_bias)
        )
    )
    normed_one_grad = jnp.sum(row_grads.astype(F32), axis=0) + query_part
    input_norm_grad, _ = norm_backward(inputs, scale_one, gain_attn, normed_one_grad)
    grad_tokens = (mixed_grad + input_norm_grad)[None]
    return (
        layer_out,
        grad_tokens,
        sum_gain_attn,
        sum_w_qkv,
        sum_rel_bias,
        sum_w_attn_out,
        sum_gain_ffn,
        sum_w_router,
        grad_w_in,
        grad_w_out,
    )


def solution(mesh):
    split_mesh = Mesh(mesh.devices.reshape(SPLIT), EVERY)
    in_specs = (
        P(WSH, CTX, None),
        P(),
        P(),
        P(),
        P(),
        P(),
        P(),
        P(CTX, None, WSH),
        P(CTX, WSH, None),
        P(WSH, CTX, None),
        P(),
        P(),
        P(WSH, CTX, None),
    )
    out_specs = (
        P(WSH, CTX, None),
        P(WSH, CTX, None),
        P(),
        P(),
        P(),
        P(),
        P(),
        P(),
        P(CTX, None, WSH),
        P(CTX, WSH, None),
    )
    return jax.shard_map(
        on_device, mesh=split_mesh, in_specs=in_specs, out_specs=out_specs, check_vma=False
    )
```
